32 devices in a mesh: slab: 16 (over z, y, core), sub: 2 (over x).
Axes of the slice: x: 2, y: 2, z: 4, core: 2. Of those that a mesh axis runs over, the one named last changes fastest.
Arguments:
- positions: float32 [3, 4096], P(None, ('slab', 'sub')), may hold values from 0 to 1
- velocities: float32 [3, 4096], P(None, ('slab', 'sub'))
- species: int32 [4096], P(('slab', 'sub')), may hold values from 0 to 7
- ghost_species: int32 [6144], P(('slab', 'sub')), may hold values from 0 to 7, as said below
- neighbours: int32 [20, 4096], P(None, ('slab', 'sub')), may hold values from 0 to 319, as said below
- slot_mask: int32 [20, 4096], P(None, ('slab', 'sub')), may hold values from 0 to 1, as said below
- edge_vectors: float32 [3, 20, 4096], P(None, None, ('slab', 'sub')), may hold values from -4.8 to 4.8, as said below
- send_slab: int32 [2, 1536], P(None, ('slab', 'sub')), may hold values from 0 to 127, as said below
- send_sub: int32 [2, 1536], P(None, ('slab', 'sub')), may hold values from 0 to 127, as said below
- migrants: int32 [4, 128], P(None, ('slab', 'sub')), may hold values from 0 to 127, as said below
- embedding: float32 [8, 128], replicated, may hold values from -6 to 6
- energy_shift: float32 [8], replicated, may hold values from -4 to 4
- masses: float32 [8], replicated, may hold values from 0.5 to 4
- radial_one_in: float32 [64, 8], replicated, may hold values from -2 to 2
- radial_one_mid: float32 [2, 64, 64], replicated, may hold values from -0.75 to 0.75
- radial_one_out: float32 [256, 64], replicated, may hold values from -0.75 to 0.75
- node_one: float32 [6, 128, 128], replicated, may hold values from -0.5 to 0.5
- radial_two_in: float32 [64, 8], replicated, may hold values from -2 to 2
- radial_two_mid: float32 [2, 64, 64], replicated, may hold values from -0.75 to 0.75
- radial_two_out: float32 [512, 64], replicated, may hold values from -0.75 to 0.75
- node_two: float32 [5, 128, 128], replicated, may hold values from -0.5 to 0.5
- readout_linear: float32 [128], replicated, may hold values from -0.5 to 0.5
- readout_hidden: float32 [16, 128], replicated, may hold values from -0.5 to 0.5
- readout_out: float32 [16], replicated, may hold values from -1.5 to 1.5
- box_matrix: float32 [3, 3], replicated, as said below
- box_velocity: float32 [3, 3], replicated, may hold values from -3 to 3
Outputs:
- atom_energy: float32 [4096], P(('slab', 'sub'))
- forces: float32 [3, 4096], P(None, ('slab', 'sub'))
- new_velocities: float32 [3, 4096], P(None, ('slab', 'sub'))
- new_positions: float32 [3, 4096], P(None, ('slab', 'sub'))
- arrivals: float32 [6, 512], P(None, ('slab', 'sub'))
- new_box: float32 [3, 3], replicated
- new_box_velocity: float32 [3, 3], replicated
The draws below stay inside these ranges and needn't reach their ends.
Inputs may be any that keep to these rules, and one draw needn't show every extreme that they name: `neighbours`: the 20 entries of an atom are distinct extended rows of its device. `slot_mask`: live slots of an atom come first; every atom has 10 to 20 live slots and the first atom of each device has all 20. `edge_vectors`: every edge vector has a length between 1.8 and 4.8. `send_slab`: each row holds, for each device, 48 distinct own atoms; row 0 goes to slab index - 1, row 1 to slab index + 1. `send_sub`: each row holds, for each device, 48 distinct own atoms; row 0 goes to sub index - 1, row 1 to sub index + 1. `migrants`: for each device the four rows hold 16 distinct own atoms, moving to slab index - 1, slab index + 1, sub index - 1 and sub index + 1. `ghost_species`: each ghost row holds the species of the atom that the send lists deliver to it. `box_matrix`: the diagonal dominates each row, so the determinant is positive.
All inputs are finite; a program needn't handle non-finite values.
Results may differ from the reference program's by a relative error of at most 0.000061.
Values sent between devices are 32-bit elements; how exact they have to be, the bound alone decides.
No kernel may reach another device: no remote copies, remote signals or barrier semaphores. Data moves between devices by JAX's collectives and lax.ppermute only.
A program may use at most 128 MiB of HBM per device.

```python
import math
import jax
import jax.numpy as jnp
from jax import lax

C = 128
RH = 64
NB = 8
RO = 16
NSPEC = 8
SLOTS = 20
ATOMS = 128
MIG = 4
GHOST_SLAB = 48
GHOST_SUB = 48
EXT_ROWS = 320
SLAB_COUNT = 16
SUB_COUNT = 2
ATOMS_ALL = 4096


def layout_lists(key):
    devices = SLAB_COUNT * SUB_COUNT
    key_species, key_slab, key_sub = jax.random.split(key, 3)
    species = jax.random.randint(key_species, (devices, ATOMS), 0, NSPEC, dtype=jnp.int32)
    slab_keys = jax.random.split(key_slab, 2 * devices)
    slab_lists = jax.vmap(lambda single: jax.random.permutation(single, ATOMS)[:GHOST_SLAB])(slab_keys).reshape(2, devices, GHOST_SLAB)
    sub_keys = jax.random.split(key_sub, 2 * devices)
    sub_lists = jax.vmap(lambda single: jax.random.permutation(single, ATOMS)[:GHOST_SUB])(sub_keys).reshape(2, devices, GHOST_SUB)
    return (species, slab_lists.astype(jnp.int32), sub_lists.astype(jnp.int32))


def draw_species(key, part):
    species, slab_lists, sub_lists = layout_lists(key)
    return species.reshape(-1)


def draw_send_slab(key, part):
    species, slab_lists, sub_lists = layout_lists(key)
    return slab_lists.reshape(2, -1)


def draw_send_sub(key, part):
    species, slab_lists, sub_lists = layout_lists(key)
    return sub_lists.reshape(2, -1)


def draw_ghost_species(key, part):
    species, slab_lists, sub_lists = layout_lists(key)
    devices = SLAB_COUNT * SUB_COUNT
    index = jnp.arange(devices).astype(jnp.int32)
    slab_at = index // SUB_COUNT
    sub_at = index % SUB_COUNT
    slab_prev = (slab_at - 1) % SLAB_COUNT * SUB_COUNT + sub_at
    slab_next = (slab_at + 1) % SLAB_COUNT * SUB_COUNT + sub_at
    sub_prev = slab_at * SUB_COUNT + (sub_at - 1) % SUB_COUNT
    sub_next = slab_at * SUB_COUNT + (sub_at + 1) % SUB_COUNT
    blocks = [jnp.take_along_axis(species[source], lists[source], axis=1) for source, lists in ((slab_prev, slab_lists[1]), (slab_next, slab_lists[0]), (sub_prev, sub_lists[1]), (sub_next, sub_lists[0]))]
    return jnp.concatenate(blocks, axis=1).reshape(-1)


def draw_neighbours(key, part):
    key = jax.random.fold_in(key, 11)
    row_keys = jax.random.split(key, ATOMS_ALL)
    picks = jax.vmap(lambda single: jax.random.permutation(single, EXT_ROWS)[:SLOTS])(row_keys)
    return jnp.transpose(picks).astype(jnp.int32)


def draw_slot_mask(key, part):
    key = jax.random.fold_in(key, 12)
    counts = jax.random.randint(key, (ATOMS_ALL,), SLOTS // 2, SLOTS + 1, dtype=jnp.int32)
    counts = counts.at[::ATOMS].set(SLOTS)
    slots_index = jnp.arange(SLOTS).astype(jnp.int32)[:, None]
    return (slots_index < counts[None, :]).astype(jnp.int32)


def draw_edge_vectors(key, part):
    key = jax.random.fold_in(key, 13)
    key_direction, key_length = jax.random.split(key)
    direction = jax.random.normal(key_direction, (3, SLOTS, ATOMS_ALL), jnp.float32)
    length = jax.random.uniform(key_length, (SLOTS, ATOMS_ALL), jnp.float32, 1.8, 4.8)
    magnitude = jnp.maximum(jnp.sqrt(jnp.sum(direction * direction, axis=0)), 1e-06)
    return direction / magnitude[None] * length[None]


def draw_migrants(key, part):
    key = jax.random.fold_in(key, 14)
    devices = SLAB_COUNT * SUB_COUNT
    device_keys = jax.random.split(key, devices)
    picks = jax.vmap(lambda single: jax.random.permutation(single, ATOMS)[:4 * MIG])(device_keys)
    return picks.reshape(devices, 4, MIG).transpose(1, 0, 2).reshape(4, -1).astype(jnp.int32)


def draw_velocities(key, part):
    key = jax.random.fold_in(key, 15)
    atom_index = jnp.arange(ATOMS_ALL).astype(jnp.int32)
    slab_at = (atom_index // (ATOMS * SUB_COUNT)).astype(jnp.float32)
    ramp = slab_at / max(SLAB_COUNT - 1, 1)
    heat = 1.0 + 2.0 * ramp
    noise = jax.random.normal(key, (3, ATOMS_ALL), jnp.float32)
    return noise * jnp.sqrt(heat)[None, :]


def draw_box_matrix(key, part):
    key = jax.random.fold_in(key, 16)
    key_length, key_slant = jax.random.split(key)
    side_length = (ATOMS_ALL / 1.024) ** (1.0 / 3.0)
    slant_range = 0.1
    lengths = jnp.array([side_length, side_length, 4.0 * side_length], jnp.float32) * jax.random.uniform(key_length, (3,), jnp.float32, 0.9, 1.1)
    slanted = jax.random.uniform(key_slant, (3, 3), jnp.float32, -slant_range, slant_range) * side_length
    return slanted * (1.0 - jnp.eye(3, dtype=jnp.float32)) + jnp.diag(lengths)


def shard_levels(own_key, extent, cuts, low, top_value):
    def one(position, blocks):
        draws = jax.random.uniform(jax.random.fold_in(jax.random.fold_in(own_key, 6), position), (blocks,), jnp.float32, low / len(cuts), top_value / len(cuts))
        return jnp.repeat(jnp.exp(draws), extent[position] // blocks).reshape((-1,) + (1,) * (len(extent) - position - 1))

    factor_of = one(*cuts[0])
    for cut in cuts[1:]:
        factor_of = factor_of * one(*cut)
    return factor_of


def scatter_about(rng, shape, spread, most, held_as=jnp.bfloat16):
    values = jax.random.normal(rng, shape, jnp.float32) * spread
    return jnp.minimum(jnp.maximum(values, -most), most).astype(held_as)


def setup_inputs(seed: int = 0) -> dict:
    seeds = jax.random.split(jax.random.key(seed), 27)
    positions = jnp.clip(1.0 * jax.random.uniform(seeds[0], (3, ATOMS_ALL), jnp.float32) ** shard_levels(seeds[0], (3, ATOMS_ALL), ((1, 32),), -0.2, 0.2), 0.0, 1.0)
    velocities = draw_velocities(jax.random.fold_in(seeds[26], 71), 0)
    species = draw_species(jax.random.fold_in(seeds[26], 71), 0)
    ghost_species = draw_ghost_species(jax.random.fold_in(seeds[26], 71), 0)
    neighbours = draw_neighbours(jax.random.fold_in(seeds[26], 71), 0)
    slot_mask = draw_slot_mask(jax.random.fold_in(seeds[26], 71), 0)
    edge_vectors = draw_edge_vectors(jax.random.fold_in(seeds[26], 71), 0)
    send_slab = draw_send_slab(jax.random.fold_in(seeds[26], 71), 0)
    send_sub = draw_send_sub(jax.random.fold_in(seeds[26], 71), 0)
    migrants = draw_migrants(jax.random.fold_in(seeds[26], 71), 0)
    embedding = scatter_about(seeds[10], (NSPEC, C), 1.0, 6.0, jnp.float32)
    energy_shift = scatter_about(seeds[11], (NSPEC,), 1.0, 4.0, jnp.float32)
    masses = jnp.clip(jnp.exp(jax.random.uniform(seeds[12], (NSPEC,), jnp.float32, math.log(0.5), math.log(4.0))), 0.5, 4.0)
    radial_one_in = scatter_about(seeds[13], (RH, NB), NB ** -0.5, 2.0, jnp.float32)
    radial_one_mid = scatter_about(seeds[14], (2, RH, RH), RH ** -0.5, 0.75, jnp.float32)
    radial_one_out = scatter_about(seeds[15], (2 * C, RH), RH ** -0.5, 0.75, jnp.float32)
    node_one = scatter_about(seeds[16], (6, C, C), C ** -0.5, 0.5, jnp.float32)
    radial_two_in = scatter_about(seeds[17], (RH, NB), NB ** -0.5, 2.0, jnp.float32)
    radial_two_mid = scatter_about(seeds[18], (2, RH, RH), RH ** -0.5, 0.75, jnp.float32)
    radial_two_out = scatter_about(seeds[19], (4 * C, RH), RH ** -0.5, 0.75, jnp.float32)
    node_two = scatter_about(seeds[20], (5, C, C), C ** -0.5, 0.5, jnp.float32)
    readout_linear = scatter_about(seeds[21], (C,), C ** -0.5, 0.5, jnp.float32)
    readout_hidden = scatter_about(seeds[22], (RO, C), C ** -0.5, 0.5, jnp.float32)
    readout_out = scatter_about(seeds[23], (RO,), RO ** -0.5, 1.5, jnp.float32)
    box_matrix = draw_box_matrix(jax.random.fold_in(seeds[26], 71), 0)
    box_velocity = scatter_about(seeds[25], (3, 3), 0.3, 3.0, jnp.float32)
    return {"positions": positions, "velocities": velocities, "species": species, "ghost_species": ghost_species, "neighbours": neighbours, "slot_mask": slot_mask, "edge_vectors": edge_vectors, "send_slab": send_slab, "send_sub": send_sub, "migrants": migrants, "embedding": embedding, "energy_shift": energy_shift, "masses": masses, "radial_one_in": radial_one_in, "radial_one_mid": radial_one_mid, "radial_one_out": radial_one_out, "node_one": node_one, "radial_two_in": radial_two_in, "radial_two_mid": radial_two_mid, "radial_two_out": radial_two_out, "node_two": node_two, "readout_linear": readout_linear, "readout_hidden": readout_hidden, "readout_out": readout_out, "box_matrix": box_matrix, "box_velocity": box_velocity}


cutoff = 5.0
neighbor_norm = 0.125
time_step = 0.5
outside_pressure = 0.5
box_mass = 0.125
highest = lax.Precision.HIGHEST

def radial(distance, radial_in, radial_mid, radial_out):
    scaled = distance / cutoff
    orders = jnp.arange(1, radial_in.shape[1] + 1).astype(jnp.float32)[:, None]
    envelope = 1.0 - 28.0 * scaled ** 6 + 48.0 * scaled ** 7 - 21.0 * scaled ** 8
    basis = jnp.sqrt(2.0 / cutoff) * jnp.sin(orders * jnp.pi * scaled) / distance * envelope
    hidden = jax.nn.silu(jnp.dot(radial_in, basis, precision=highest))
    hidden = jax.nn.silu(jnp.dot(radial_mid[0], hidden, precision=highest))
    hidden = jax.nn.silu(jnp.dot(radial_mid[1], hidden, precision=highest))
    return jnp.dot(radial_out, hidden, precision=highest)

def geometry(edges):
    flat = edges.reshape(3, -1)
    distance = jnp.sqrt(lax.optimization_barrier(jnp.sum(flat * flat, axis=0)))
    return (distance, flat / distance)

def slot_sum(values, atoms):
    return values.reshape(values.shape[:-1] + (-1, atoms)).sum(axis=-2)

def layer_one(edges, weights_edge, neighbour_rows, first_table, radial_in, radial_mid, radial_out, node):
    atoms = edges.shape[2]
    width = node.shape[1]
    distance, unit = geometry(edges)
    radial_weights = radial(distance, radial_in, radial_mid, radial_out)
    lifted = jnp.dot(node[0], first_table, precision=highest)
    picked = lifted[:, neighbour_rows] * weights_edge
    scalar_sum = slot_sum(radial_weights[:width] * picked, atoms)
    vector_sum = slot_sum(unit[:, None, :] * (radial_weights[width:] * picked)[None], atoms)
    own = first_table[:, :atoms]
    squares = lax.optimization_barrier(jnp.sum(vector_sum * vector_sum, axis=0))
    scalars = own + jnp.dot(node[1], scalar_sum, precision=highest) + jnp.dot(node[2], scalar_sum * scalar_sum, precision=highest) + jnp.dot(node[3], squares, precision=highest)
    vectors = jnp.einsum('cd,xda->xca', node[4], vector_sum, precision=highest) + jnp.dot(node[5], scalar_sum, precision=highest)[None] * vector_sum
    return jnp.concatenate([scalars, vectors.reshape(3 * width, atoms)], axis=0)

def layer_two(edges, weights_edge, neighbour_rows, table, radial_in, radial_mid, radial_out, node, shift_own, readout_linear, readout_hidden, readout_out):
    atoms = edges.shape[2]
    width = node.shape[1]
    distance, unit = geometry(edges)
    radial_weights = radial(distance, radial_in, radial_mid, radial_out)
    scalars = table[:width]
    vectors = table[width:].reshape(3, width, -1)
    lifted = jnp.dot(node[0], scalars, precision=highest)
    turned = jnp.einsum('cd,xde->xce', node[1], vectors, precision=highest)
    picked = lifted[:, neighbour_rows] * weights_edge
    picked_vector = turned[:, :, neighbour_rows] * weights_edge
    along = lax.optimization_barrier(jnp.sum(picked_vector * unit[:, None, :], axis=0))
    scalar_sum = slot_sum(radial_weights[:width] * picked + radial_weights[3 * width:] * along, atoms)
    vector_sum = slot_sum((radial_weights[width:2 * width] * picked)[None] * unit[:, None, :] + radial_weights[2 * width:3 * width][None] * picked_vector, atoms)
    own = scalars[:, :atoms]
    squares = lax.optimization_barrier(jnp.sum(vector_sum * vector_sum, axis=0))
    second = own + jnp.dot(node[2], scalar_sum, precision=highest) + jnp.dot(node[3], scalar_sum * scalar_sum, precision=highest) + jnp.dot(node[4], squares, precision=highest)
    hidden = jax.nn.silu(jnp.dot(readout_hidden, second, precision=highest))
    return shift_own + jnp.dot(readout_linear, own, precision=highest) + jnp.dot(readout_out, hidden, precision=highest)

def determinant(matrix):
    return matrix[0, 0] * (matrix[1, 1] * matrix[2, 2] - matrix[1, 2] * matrix[2, 1]) - matrix[0, 1] * (matrix[1, 0] * matrix[2, 2] - matrix[1, 2] * matrix[2, 0]) + matrix[0, 2] * (matrix[1, 0] * matrix[2, 1] - matrix[1, 1] * matrix[2, 0])

def inverse(matrix):
    cofactors = []
    for row_index in range(3):
        entries = []
        for column_index in range(3):
            entries.append(matrix[(row_index + 1) % 3, (column_index + 1) % 3] * matrix[(row_index + 2) % 3, (column_index + 2) % 3] - matrix[(row_index + 1) % 3, (column_index + 2) % 3] * matrix[(row_index + 2) % 3, (column_index + 1) % 3])
        cofactors.append(jnp.stack(entries))
    return jnp.transpose(jnp.stack(cofactors)) / determinant(matrix)

def drift(inverse_box, moving):
    return lax.optimization_barrier(jnp.sum(inverse_box[:, :, None] * moving[None, :, :], axis=1))

def neighbour_devices():
    index = jnp.arange(SLAB_COUNT * SUB_COUNT).astype(jnp.int32)
    slab_at = index // SUB_COUNT
    sub_at = index % SUB_COUNT
    slab_prev = (slab_at - 1) % SLAB_COUNT * SUB_COUNT + sub_at
    slab_next = (slab_at + 1) % SLAB_COUNT * SUB_COUNT + sub_at
    sub_prev = slab_at * SUB_COUNT + (sub_at - 1) % SUB_COUNT
    sub_next = slab_at * SUB_COUNT + (sub_at + 1) % SUB_COUNT
    return (slab_prev, slab_next, sub_prev, sub_next)

def reference(positions, velocities, species, ghost_species, neighbours, slot_mask, edge_vectors, send_slab, send_sub, migrants, embedding, energy_shift, masses, radial_one_in, radial_one_mid, radial_one_out, node_one, radial_two_in, radial_two_mid, radial_two_out, node_two, readout_linear, readout_hidden, readout_out, box_matrix, box_velocity):
    devices = SLAB_COUNT * SUB_COUNT
    atoms = ATOMS
    width = node_one.shape[1]
    slab_prev, slab_next, sub_prev, sub_next = neighbour_devices()
    own_ids = jnp.arange(devices * atoms).astype(jnp.int32).reshape(devices, atoms)
    slab_lists = send_slab.reshape(2, devices, -1)
    sub_lists = send_sub.reshape(2, devices, -1)
    extended_ids = jnp.concatenate([own_ids, slab_prev[:, None] * atoms + slab_lists[1][slab_prev], slab_next[:, None] * atoms + slab_lists[0][slab_next], sub_prev[:, None] * atoms + sub_lists[1][sub_prev], sub_next[:, None] * atoms + sub_lists[0][sub_next]], axis=1)
    edges_dev = edge_vectors.reshape(3, SLOTS, devices, atoms).transpose(2, 0, 1, 3)
    rows_dev = neighbours.reshape(SLOTS, devices, atoms).transpose(1, 0, 2).reshape(devices, -1)
    weights_dev = slot_mask.reshape(SLOTS, devices, atoms).transpose(1, 0, 2).reshape(devices, -1).astype(jnp.float32) * neighbor_norm
    species_ext = jnp.concatenate([species.reshape(devices, atoms), ghost_species.reshape(devices, -1)], axis=1)
    first_dev = jnp.transpose(embedding)[:, species_ext].transpose(1, 0, 2)
    shift_dev = energy_shift[species].reshape(devices, atoms)

    def group(values):
        return values.reshape((devices // 8, 8) + values.shape[1:])

    def energies_of(edges):

        def first_one(block):
            return layer_one(block[0], block[1], block[2], block[3], radial_one_in, radial_one_mid, radial_one_out, node_one)
        features = lax.map(jax.checkpoint(jax.vmap(first_one)), (group(edges), group(weights_dev), group(rows_dev), group(first_dev)))
        features = features.reshape(devices, 4 * width, atoms)
        table = features.transpose(1, 0, 2).reshape(4 * width, devices * atoms)

        def second_one(block):
            return layer_two(block[0], block[1], block[2], table[:, block[3]], radial_two_in, radial_two_mid, radial_two_out, node_two, block[4], readout_linear, readout_hidden, readout_out)
        energies = lax.map(jax.checkpoint(jax.vmap(second_one)), (group(edges), group(weights_dev), group(rows_dev), group(extended_ids), group(shift_dev)))
        return energies.reshape(devices * atoms)
    atom_energy, pullback = jax.vjp(energies_of, edges_dev)
    gradient, = pullback(jnp.ones_like(atom_energy))
    gradient_t = gradient.transpose(1, 2, 0, 3)
    gradient_flat = gradient_t.reshape(3, -1)
    forces = lax.optimization_barrier(jnp.sum(gradient_t, axis=1)).reshape(3, -1)
    global_rows = jax.vmap(lambda identity, picks: identity[picks])(extended_ids, rows_dev)
    global_rows = global_rows.reshape(devices, SLOTS, atoms).transpose(1, 0, 2).reshape(-1)
    forces = forces.at[:, global_rows].add(-gradient_flat)
    mass = masses[species]
    new_velocities = velocities + time_step * forces / mass[None]
    kinetic = jnp.einsum('ai,bi->ab', new_velocities * mass[None], new_velocities, precision=highest)
    virial = jnp.einsum('ae,be->ab', edge_vectors.reshape(3, -1), gradient_flat, precision=highest)
    stress = kinetic - virial
    volume = determinant(box_matrix)
    identity_three = jnp.eye(3, dtype=jnp.float32)
    push = jnp.dot(stress - outside_pressure * volume * identity_three, jnp.transpose(inverse(box_matrix)), precision=highest)
    new_box_velocity = box_velocity + time_step * push / (box_mass * devices * atoms)
    new_box = box_matrix + time_step * new_box_velocity
    new_positions = positions + time_step * drift(inverse(new_box), new_velocities)
    moving = migrants.reshape(4, devices, -1)
    come_ids = jnp.concatenate([slab_prev[:, None] * atoms + moving[1][slab_prev], slab_next[:, None] * atoms + moving[0][slab_next], sub_prev[:, None] * atoms + moving[3][sub_prev], sub_next[:, None] * atoms + moving[2][sub_next]], axis=1).reshape(-1)
    arrivals = jnp.concatenate([new_positions, new_velocities], axis=0)[:, come_ids]
    return (atom_energy, forces, new_velocities, new_positions, arrivals, new_box, new_box_velocity)
```

```python
import math

import jax
import jax.numpy as jnp
from jax import lax
from jax.experimental import pallas as pl
from jax.experimental.pallas import tpu as pltpu
from jax.sharding import PartitionSpec as P

cutoff = 5.0
neighbor_norm = 0.125
time_step = 0.5
outside_pressure = 0.5
box_mass = 0.125
highest = lax.Precision.HIGHEST
f32 = jnp.float32
bf16 = jnp.bfloat16
GROUP = 4


def shifted(block, axis, distance):
    count = lax.axis_size(axis)
    return lax.ppermute(block, axis, [((i - distance) % count, i) for i in range(count)])


def trade(to_minus, to_plus, to_prev, to_next):
    from_minus, from_plus = shifted(to_plus, "slab", 1), shifted(to_minus, "slab", -1)
    return from_minus, from_plus, shifted(to_next, "sub", 1), shifted(to_prev, "sub", -1)


def parts(x):
    high = x.astype(bf16)
    return high, (x - high.astype(f32)).astype(bf16)


def dot(a, b):
    return jnp.dot(a, b, preferred_element_type=f32)


def dot_nt(a, b):
    return lax.dot_general(a, b, (((1,), (1,)), ((), ())), preferred_element_type=f32)


def exact(a, b, dims=((1,), (0,))):
    return lax.dot_general(a, b, (dims, ((), ())), precision=highest, preferred_element_type=f32)


def product(weight, x):
    high, low = parts(x)
    return dot(weight[0], high) + dot(weight[0], low) + dot(weight[1], high)


def weight_stack(w):
    high = w.astype(bf16).astype(f32)
    return jnp.concatenate([high, high, w - high], axis=1).astype(bf16)


def weight_stack_t(w):
    high = w.astype(bf16).astype(f32)
    return jnp.transpose(jnp.concatenate([high, high, w - high], axis=0)).astype(bf16)


def value_stack(x):
    high, low = parts(x)
    return jnp.concatenate([high, low, high], axis=0)


def value_stack_small(x):
    high = x.astype(bf16).astype(f32)
    return jnp.concatenate([high, x - high, high], axis=0).astype(bf16)


def over_groups(count, step, carry):
    for i in range(count):
        carry = step(i, carry)
    return carry


def span_of(first, count):
    if isinstance(first, int):
        return pl.ds(first, count)
    return pl.ds(pl.multiple_of(first, count), count)


def iota(shape, axis):
    return lax.broadcasted_iota(jnp.int32, shape, axis)


def column(row):
    n = row.shape[1]
    return jnp.sum(jnp.where(iota((n, n), 0) == iota((n, n), 1), row, 0.0), axis=1, keepdims=True)


def sigmoid(x):
    return 0.5 + 0.5 * jnp.tanh(0.5 * x)


def basis(distance, inverse_distance, count, with_slope):
    orders = (iota((count, distance.shape[1]), 0) + 1).astype(f32)
    scaled = distance * (1.0 / cutoff)
    angle = orders * (math.pi * scaled)
    second = scaled * scaled
    fourth = second * second
    fifth = fourth * scaled
    sixth = fourth * second
    scale = math.sqrt(2.0 / cutoff)
    envelope = 1.0 + sixth * (-28.0 + scaled * (48.0 - 21.0 * scaled))
    sine = jnp.sin(angle)
    front = scale * envelope * inverse_distance
    value = sine * front
    if not with_slope:
        return value, None
    slope_envelope = fifth * (-168.0 + scaled * (336.0 - 168.0 * scaled)) * (1.0 / cutoff)
    slope_front = scale * inverse_distance * (slope_envelope - envelope * inverse_distance)
    slope = sine * slope_front + jnp.cos(angle) * (orders * (math.pi / cutoff)) * front
    return value, slope


def basis_group(geo, first, count, with_slope):
    found = [
        basis(geo[4, pl.ds(first + j, 1), :], geo[5, pl.ds(first + j, 1), :], count, with_slope)
        for j in range(GROUP)
    ]
    value = jnp.concatenate([pair[0] for pair in found], axis=1)
    slope = jnp.concatenate([pair[1] for pair in found], axis=1) if with_slope else None
    return value, slope


def hidden_values(value, inner, mid_a, mid_b):
    x = dot(inner, value_stack_small(value))
    h = x * sigmoid(x)
    x = dot(mid_a, value_stack(h))
    h = x * sigmoid(x)
    x = dot(mid_b, value_stack(h))
    return x * sigmoid(x)


def hidden_pairs(value, slope, inner, mid_a, mid_b):
    x, dx = dot(inner, value_stack_small(value)), dot(inner, value_stack_small(slope))
    for mid in (mid_a, mid_b, None):
        gate = sigmoid(x)
        h = x * gate
        dh = (gate + h * (1.0 - gate)) * dx
        if mid is not None:
            x, dx = dot(mid, value_stack(h)), dot(mid, value_stack(dh))
    return h, dh


def species_matrix(first_mixing, embedding):
    lifted = exact(first_mixing, embedding, ((1,), (1,)))
    high = lifted.astype(bf16).astype(f32)
    rest = lifted - high
    mid = rest.astype(bf16).astype(f32)
    return jnp.concatenate([high, mid, rest - mid], axis=1).astype(bf16)


def picked_group(lifted, geo, kinds, first, species_count):
    blocks = []
    for j in range(GROUP):
        kind = kinds[pl.ds(first + j, 1), :]
        weight = geo[3, pl.ds(first + j, 1), :]
        blocks.append(jnp.where(iota((species_count, kind.shape[1]), 0) == kind, weight, 0.0))
    block = jnp.concatenate(blocks, axis=1)
    return dot(lifted, jnp.concatenate([block, block, block], axis=0).astype(bf16))


def send_onehot(facts, first, slab_rows, sub_rows):
    atoms = facts.shape[1]
    lengths = (slab_rows, slab_rows, sub_rows, sub_rows)
    rows = [facts[first + 9 + i : first + 10 + i, :n] for i, n in enumerate(lengths)]
    rows = jnp.concatenate(rows, axis=1)
    return (iota((atoms, rows.shape[1]), 0).astype(f32) == rows).astype(f32)


FIRST_INPUTS = 24
FACTS = 16


def packed_step(slots):
    return -(-slots // 8) * 8


def first_kernel(
    *refs,
):
    count = FIRST_INPUTS
    buffers, ready, gone = refs[-count - 2 : -2], refs[-2], refs[-1]
    copies = [pltpu.make_async_copy(refs[i], buffers[i], ready.at[i]) for i in range(count)]
    for copy in copies:
        copy.start()
    (
        edges, mask, neighbours, species, ghosts, embedding, radial_in, radial_mid, radial_out, node_one,
        send_slab, send_sub, velocities, positions, migrants, masses, shifts,
        hidden_head, linear_head, out_head, next_in, next_mid, next_out, node_two,
    ) = buffers
    kinds, far_sums, far_packed, to_minus, to_plus, to_prev, to_next, geo, packed, sums = refs[count : -count - 2]
    for copy in copies[:2]:
        copy.wait()
    slots, atoms = mask.shape
    width = node_one.shape[1]
    species_count, basis_count = embedding.shape[0], radial_in.shape[0]
    ex, ey, ez = edges[0], edges[1], edges[2]
    square = ex * ex + ey * ey + ez * ez
    distance = jnp.sqrt(square)
    inverse_distance = 1.0 / distance
    for a, e in enumerate((ex, ey, ez)):
        geo[a] = e * inverse_distance
    geo[3] = mask[...].astype(f32) * neighbor_norm
    geo[4] = distance
    geo[5] = inverse_distance
    base = 5 * width
    step = packed_step(slots)
    for a in range(6):
        packed[base + a * step : base + a * step + slots] = geo[a]
    for copy in copies[2:5]:
        copy.wait()
    ghost_row = ghosts[...]
    extra = -ghost_row.shape[1] % atoms
    if extra:
        ghost_row = jnp.concatenate([ghost_row, jnp.zeros((1, extra), jnp.int32)], axis=1)
    tables = [species[...]] + [ghost_row[:, i : i + atoms] for i in range(0, ghost_row.shape[1], atoms)]
    pad = -slots % 8
    rows = neighbours[...]
    if pad:
        rows = jnp.concatenate([rows, jnp.zeros((pad, atoms), jnp.int32)], axis=0)
    inner_index = lax.rem(rows, atoms)
    block_index = lax.div(rows, atoms)
    found = jnp.zeros_like(rows)
    for i, table in enumerate(tables):
        spread = jnp.broadcast_to(table, rows.shape)
        got = jnp.take_along_axis(spread, inner_index, axis=1)
        found = jnp.where(block_index == i, got, found)
    kinds[...] = found[:slots]

    for copy in copies[5:10]:
        copy.wait()
    inner = weight_stack_t(radial_in[...])
    mid_a, mid_b = weight_stack(radial_mid[0]), weight_stack(radial_mid[1])
    outer = weight_stack_t(radial_out[...])
    lifted = species_matrix(node_one[0], embedding[...])
    sums[...] = jnp.zeros_like(sums)

    def group(step, carry):
        first = step * GROUP
        value, _ = basis_group(geo, first, basis_count, False)
        h = hidden_values(value, inner, mid_a, mid_b)
        weights = dot(outer, value_stack(h))
        picked = picked_group(lifted, geo, kinds, first, species_count)
        totals = [0.0] * 4
        for j in range(GROUP):
            at = slice(j * atoms, (j + 1) * atoms)
            p = picked[:, at]
            totals[0] = totals[0] + weights[:width, at] * p
            q = weights[width:, at] * p
            for a in range(3):
                totals[a + 1] = totals[a + 1] + q * geo[a, pl.ds(first + j, 1), :]
        for a in range(4):
            sums[a] += totals[a]
        return carry

    over_groups(slots // GROUP, group, 0)

    early_sums = pltpu.make_async_copy(sums.at[:4], far_sums.at[:4], gone.at[2])
    early_sums.start()
    for copy in copies[10:]:
        copy.wait()
    mass = shift = jnp.zeros((1, atoms), f32)
    for i in range(masses.shape[1]):
        mass = jnp.where(species[...] == i, masses[:, i : i + 1], mass)
        shift = jnp.where(species[...] == i, shifts[:, i : i + 1], shift)
    facts = base + 6 * step
    packed[facts : facts + 1] = iota((1, atoms), 1).astype(f32)
    packed[facts + 1 : facts + 4] = velocities[...]
    packed[facts + 4 : facts + 7] = positions[...]
    packed[facts + 7 : facts + 8] = 1.0 / jnp.sqrt(mass)
    packed[facts + 8 : facts + 9] = mass
    packed[facts + 9 : facts + FACTS] = jnp.zeros((FACTS - 9, atoms), f32)
    for i, (lists, at) in enumerate(((send_slab, 1), (send_slab, 0), (send_sub, 1), (send_sub, 0))):
        packed[facts + 9 + i : facts + 10 + i, : lists.shape[1]] = lists[at : at + 1, :].astype(f32)
    count = migrants.shape[1]
    for i, at in enumerate((1, 0, 3, 2)):
        packed[facts + 13 : facts + 14, i * count : (i + 1) * count] = migrants[at : at + 1, :].astype(f32)
    inner_rows = next_mid.shape[1]
    start = facts + FACTS
    for i in range(3):
        packed[start : start + width] = node_two[i + 2]
        start += width
    for i in range(next_out.shape[1] // atoms):
        packed[start : start + inner_rows] = next_out[:, i * atoms : (i + 1) * atoms]
        start += inner_rows
    for i in range(2):
        packed[start : start + inner_rows, :inner_rows] = next_mid[i]
        start += inner_rows
    packed[start : start + next_in.shape[0], :inner_rows] = next_in[...]
    start += next_in.shape[0]
    packed[start : start + slots] = neighbours[...].astype(f32)
    start += step
    count = hidden_head.shape[0]
    packed[start : start + count] = hidden_head[...]
    packed[start + count : start + count + 1] = linear_head[...]
    packed[start + count + 1 : start + count + 2, : out_head.shape[1]] = out_head[...]
    packed[start + count + 2 : start + count + 3] = shift
    early = pltpu.make_async_copy(packed.at[base:], far_packed.at[base:], gone.at[0])
    early.start()

    own_onehot = (iota((species_count, atoms), 0) == species[...]).astype(f32)
    own = exact(embedding[...], own_onehot, ((0,), (0,)))
    scalar_sum = sums[0]
    vectors = [sums[1], sums[2], sums[3]]
    squares = vectors[0] * vectors[0] + vectors[1] * vectors[1] + vectors[2] * vectors[2]
    scalars = (
        own
        + product(parts(node_one[1]), scalar_sum)
        + product(parts(node_one[2]), scalar_sum * scalar_sum)
        + product(parts(node_one[3]), squares)
    )
    gate = product(parts(node_one[5]), scalar_sum)
    sums[4] = gate
    late_sums = pltpu.make_async_copy(sums.at[4:], far_sums.at[4:], gone.at[3])
    late_sums.start()
    turned = product(parts(node_one[4]), jnp.concatenate(vectors, axis=1))
    moved = turned + jnp.concatenate([gate * v for v in vectors], axis=1)
    packed[:width] = scalars
    x = product(parts(node_two[0]), scalars)
    y = product(parts(node_two[1]), moved)
    table = jnp.concatenate([x] + [y[:, a * atoms : (a + 1) * atoms] for a in range(3)], axis=0)
    packed[width : 5 * width] = table
    late = pltpu.make_async_copy(packed.at[:base], far_packed.at[:base], gone.at[1])
    late.start()
    pick = send_onehot(packed, facts, send_slab.shape[1], send_sub.shape[1]).astype(bf16)
    high, low = parts(table)
    sent = jnp.transpose(dot(high, pick) + dot(low, pick))
    slab_rows = send_slab.shape[1]
    to_plus[...] = sent[:slab_rows]
    to_minus[...] = sent[slab_rows : 2 * slab_rows]
    sub_rows = send_sub.shape[1]
    to_next[...] = sent[2 * slab_rows : 2 * slab_rows + sub_rows]
    to_prev[...] = sent[2 * slab_rows + sub_rows :]
    for copy in (early, late, early_sums, late_sums):
        copy.wait()


def radial_kernel(
    packed,
    weights_all, slopes, onehot, outer, forward_high, forward_low, backward_high, backward_low,
    geo, table, scalars, extras, facts, heads, *, slab_rows, sub_rows, moves, basis_count,
):
    slots, atoms = geo.shape[1:]
    width = scalars.shape[0]
    depth = 4 * width
    inner_rows = slopes.shape[0] // 3
    scalars[...] = packed[:width]
    first_fact = 5 * width + 6 * packed_step(slots)
    start = first_fact + FACTS
    mixings = [packed[start + i * width : start + (i + 1) * width] for i in range(3)]
    start += 3 * width
    pieces = depth // atoms
    radial_out = [packed[start + i * inner_rows : start + (i + 1) * inner_rows] for i in range(pieces)]
    radial_out = jnp.concatenate(radial_out, axis=1)
    start += pieces * inner_rows
    radial_mid = [packed[start + i * inner_rows : start + (i + 1) * inner_rows, :inner_rows] for i in range(2)]
    start += 2 * inner_rows
    radial_in = packed[start : start + basis_count, :inner_rows]
    first_row = start + basis_count
    heads[...] = packed[first_row + packed_step(slots) :]
    table[:, :atoms], table[:, atoms:] = parts(packed[width : 5 * width])
    for a in range(6):
        start = 5 * width + a * packed_step(slots)
        geo[a] = packed[start : start + slots]
    facts[...] = packed[first_fact : first_fact + FACTS]
    listed = exact(facts[:8], send_onehot(facts, 0, slab_rows, sub_rows))
    moving = exact(facts[:8], (iota((atoms, 4 * moves), 0).astype(f32) == facts[13:14, : 4 * moves]).astype(f32))
    start = 0
    extras[...] = jnp.zeros_like(extras)
    for i, length in enumerate((slab_rows, slab_rows, sub_rows, sub_rows)):
        extras[i, :, :length] = listed[:, start : start + length]
        extras[i, :, atoms : atoms + moves] = moving[:, i * moves : (i + 1) * moves]
        start += length
    rows = onehot.shape[0] // 2
    outer[...] = weight_stack_t(radial_out)
    mixing = jnp.concatenate(mixings, axis=1)
    forward_high[...], forward_low[...] = parts(mixing)
    turned = jnp.concatenate([jnp.transpose(m) for m in mixings], axis=0)
    backward_high[...], backward_low[...] = parts(turned)
    inner = weight_stack_t(radial_in)
    mid_a, mid_b = weight_stack(radial_mid[0]), weight_stack(radial_mid[1])

    def group(step, carry):
        first = step * GROUP
        at = span_of(step * GROUP * atoms, GROUP * atoms)
        value, slope = basis_group(geo, first, basis_count, True)
        h, dh = hidden_pairs(value, slope, inner, mid_a, mid_b)
        slopes[:, at] = value_stack(dh)
        blocks = []
        for j in range(GROUP):
            row = packed[first_row + first + j : first_row + first + j + 1]
            weight = geo[3, pl.ds(first + j, 1), :]
            row = row.astype(jnp.int32)
            blocks.append(jnp.where(iota((rows, atoms), 0) == row, weight, 0.0).astype(bf16))
        block = jnp.concatenate(blocks, axis=1)
        own, ghosts = block[:atoms], block[atoms:]
        onehot[:, at] = jnp.concatenate([own, own, ghosts, ghosts], axis=0)
        weights_all[:, at] = dot(outer[...], value_stack(h))
        return carry

    over_groups(slots // GROUP, group, 0)


def second_kernel(
    geo, own_table, from_minus, from_plus, from_prev, from_next, scalars, extras,
    weights_all, onehot, forward_high, forward_low, backward_high, backward_low, heads,
    energy, scalar_pull, picked_all, sums, own_pull, back_minus, back_plus, back_prev, back_next,
    table, pulled,
):
    slots, atoms = geo.shape[1], geo.shape[2]
    width = scalars.shape[0]
    depth = 4 * width
    ghosts = jnp.concatenate([from_minus[...], from_plus[...], from_prev[...], from_next[...]], axis=0)
    high = ghosts.astype(bf16).astype(f32)
    table[:, : 2 * atoms] = own_table[...]
    table[:, 2 * atoms :] = jnp.transpose(jnp.concatenate([high, ghosts - high], axis=0)).astype(bf16)
    ghost_rows = ghosts.shape[0]
    sums[...] = jnp.zeros_like(sums)

    def units(first, j):
        return [geo[a, pl.ds(first + j, 1), :] for a in range(3)]

    def forward(step, carry):
        first = step * GROUP
        at = span_of(step * GROUP * atoms, GROUP * atoms)
        picked = dot(table[...], onehot[:, at])
        picked_all[:, at] = picked
        totals = [0.0] * 4
        for j in range(GROUP):
            span = slice(j * atoms, (j + 1) * atoms)
            here = span_of((step * GROUP + j) * atoms, atoms)
            p = [picked[a * width : (a + 1) * width, span] for a in range(4)]
            r = [weights_all[a * width : (a + 1) * width, here] for a in range(4)]
            u = units(first, j)
            along = p[1] * u[0] + p[2] * u[1] + p[3] * u[2]
            totals[0] = totals[0] + (r[0] * p[0] + r[3] * along)
            q = r[1] * p[0]
            for a in range(3):
                totals[a + 1] = totals[a + 1] + (q * u[a] + r[2] * p[a + 1])
        for a in range(4):
            sums[a] += totals[a]
        return carry

    over_groups(slots // GROUP, forward, 0)

    scalar_sum = sums[0]
    vectors = [sums[1], sums[2], sums[3]]
    squares = vectors[0] * vectors[0] + vectors[1] * vectors[1] + vectors[2] * vectors[2]
    mixed = jnp.concatenate([scalar_sum, scalar_sum * scalar_sum, squares], axis=0)
    second = scalars[...] + product((forward_high[...], forward_low[...]), mixed)
    units_out = heads.shape[0] - 8
    readout_hidden = heads[:units_out]
    readout_linear, readout_out = heads[units_out : units_out + 1], heads[units_out + 1 : units_out + 2, :units_out]
    hidden_in = product(parts(readout_hidden), second)
    hidden_gate = sigmoid(hidden_in)
    hidden = hidden_in * hidden_gate
    shift = heads[units_out + 2 : units_out + 3]
    energy[...] = shift + exact(readout_linear, scalars[...]) + exact(readout_out, hidden)
    hidden_pull = column(readout_out) * (hidden_gate + hidden * (1.0 - hidden_gate))
    second_pull = exact(readout_hidden, hidden_pull, ((0,), (0,)))
    scalar_pull[...] = second_pull
    spread = product((backward_high[...], backward_low[...]), second_pull)
    double = 2.0 * spread[2 * width :]
    sums[0] = spread[:width] + 2.0 * scalar_sum * spread[width : 2 * width]
    for a in range(3):
        sums[a + 1] = vectors[a] * double
    pulled[...] = jnp.zeros_like(pulled)

    def backward(step, carry):
        first = step * GROUP
        at = span_of(step * GROUP * atoms, GROUP * atoms)
        highs, lows = [], []
        for j in range(GROUP):
            here = span_of((step * GROUP + j) * atoms, atoms)
            r = [weights_all[a * width : (a + 1) * width, here] for a in range(4)]
            u = units(first, j)
            ga = [sums[a] for a in range(4)]
            flow = ga[1] * u[0] + ga[2] * u[1] + ga[3] * u[2]
            pull = r[3] * ga[0]
            given = [r[0] * ga[0] + r[1] * flow] + [pull * u[a] + r[2] * ga[a + 1] for a in range(3)]
            high, low = parts(jnp.concatenate(given, axis=0))
            highs.append(high)
            lows.append(low)
        split = jnp.concatenate(highs + lows, axis=1)
        chosen = jnp.concatenate([onehot[:atoms, at], onehot[2 * atoms : 2 * atoms + ghost_rows, at]], axis=0)
        pulled[...] += dot_nt(jnp.concatenate([chosen, chosen], axis=1), split)
        return carry

    over_groups(slots // GROUP, backward, 0)
    own_pull[...] = pulled[:atoms]
    start = atoms
    fill = jnp.zeros((8, depth - extras.shape[2]), f32)
    for out, which in ((back_minus, 1), (back_plus, 0), (back_prev, 3), (back_next, 2)):
        count = out.shape[0] - 8
        out[:count] = pulled[start : start + count]
        out[count:] = jnp.concatenate([extras[which], fill], axis=1)
        start += count


def edge_kernel(geo, slopes, outer, picked_all, weights_all, sums, geo_pull):
    slots, atoms = geo.shape[1], geo.shape[2]
    width = sums.shape[1]

    def group(step, carry):
        first = step * GROUP
        slope = dot(outer[...], slopes[:, span_of(step * GROUP * atoms, GROUP * atoms)])
        for j in range(GROUP):
            span = slice(j * atoms, (j + 1) * atoms)
            here = span_of((step * GROUP + j) * atoms, atoms)
            p = [picked_all[a * width : (a + 1) * width, here] for a in range(4)]
            r = [weights_all[a * width : (a + 1) * width, here] for a in (1, 3)]
            s = [slope[a * width : (a + 1) * width, span] for a in range(4)]
            u = [geo[a, pl.ds(first + j, 1), :] for a in range(3)]
            ga = [sums[a] for a in range(4)]
            along = p[1] * u[0] + p[2] * u[1] + p[3] * u[2]
            flow = ga[1] * u[0] + ga[2] * u[1] + ga[3] * u[2]
            cross = p[1] * ga[1] + p[2] * ga[2] + p[3] * ga[3]
            stretch = p[0] * (s[0] * ga[0] + s[1] * flow) + s[2] * cross + s[3] * (along * ga[0])
            geo_pull[0, pl.ds(first + j, 1), :] = jnp.sum(stretch, axis=0, keepdims=True)
            lean = r[0] * p[0]
            pull = r[1] * ga[0]
            for a in range(3):
                turn = lean * ga[a + 1] + pull * p[a + 1]
                geo_pull[a + 1, pl.ds(first + j, 1), :] = jnp.sum(turn, axis=0, keepdims=True)
        return carry

    over_groups(slots // GROUP, group, 0)


def slope_kernel(
    geo, kinds, after, embedding, radial_in, radial_mid, radial_out, node_one, node_two, readout_linear,
    scalar_slope, vector_slope, vector_value, turned_high, turned_low, linear,
):
    slots, atoms = kinds.shape
    width = node_one.shape[1]
    species_count, basis_count = embedding.shape[0], radial_in.shape[0]
    inner = weight_stack_t(radial_in[...])
    mid_a, mid_b = weight_stack(radial_mid[0]), weight_stack(radial_mid[1])
    outer = weight_stack_t(radial_out[...])
    lifted = species_matrix(node_one[0], embedding[...])
    linear[...] = jnp.broadcast_to(column(readout_linear[...]), linear.shape)
    mixings = [node_one[i] for i in (1, 2, 3, 4, 5)] + [node_two[0], node_two[1]]
    turned = jnp.concatenate([jnp.transpose(m) for m in mixings], axis=0)
    turned_high[...], turned_low[...] = parts(turned)

    def group(step, carry):
        first = step * GROUP
        at = span_of(step * GROUP * atoms, GROUP * atoms)
        value, slope = basis_group(geo, first, basis_count, True)
        h, dh = hidden_pairs(value, slope, inner, mid_a, mid_b)
        picked = picked_group(lifted, geo, kinds, first, species_count)
        weights_slope = dot(outer, value_stack(dh))
        scalar_slope[:, at] = weights_slope[:width] * picked
        vector_slope[:, at] = weights_slope[width:] * picked
        vector_value[:, at] = dot(outer[width:], value_stack(h)) * picked
        return carry

    over_groups(slots // GROUP, group, 0)


def third_kernel(
    facts, geo, sums, geo_pull, scalar_pull, own_pull, ret_minus, ret_plus, ret_prev, ret_next,
    onehot, scalar_slope, vector_slope, vector_value, turned_high, turned_low, linear,
    everyone, came,
    pieces, pulls, flat, *, moves, slab_rows, sub_rows,
):
    slots, atoms = geo.shape[1], geo.shape[2]
    width = scalar_pull.shape[0]
    pick = send_onehot(facts, 0, slab_rows, sub_rows).astype(bf16)
    returned = jnp.concatenate(
        [ret_plus[:slab_rows], ret_minus[:slab_rows], ret_next[:sub_rows], ret_prev[:sub_rows]], axis=0
    )
    high, low = parts(returned)
    total = jnp.transpose(own_pull[...] + dot(pick, high) + dot(pick, low))
    x_pull = total[:width]
    y_pull = jnp.concatenate([total[a * width : (a + 1) * width] for a in (1, 2, 3)], axis=1)

    def turned(i, count=1):
        at = slice(i * width, (i + count) * width)
        return turned_high[at, :], turned_low[at, :]

    scalars = product(turned(5), x_pull) + linear[...] + scalar_pull[...]
    moved = product(turned(6), y_pull)
    gv = [moved[:, a * atoms : (a + 1) * atoms] for a in range(3)]
    scalar_sum, gate = sums[0], sums[4]
    vectors = [sums[1], sums[2], sums[3]]
    spread = product(turned(0, 3), scalars)
    mixed = product(turned(3), moved)
    gated = product(turned(4), gv[0] * vectors[0] + gv[1] * vectors[1] + gv[2] * vectors[2])
    pulls[0] = spread[:width] + 2.0 * scalar_sum * spread[width : 2 * width] + gated
    double = 2.0 * spread[2 * width :]
    for a in range(3):
        pulls[a + 1] = vectors[a] * double + mixed[:, a * atoms : (a + 1) * atoms] + gate * gv[a]

    def contract(step, carry):
        first = step * GROUP
        for j in range(GROUP):
            here = span_of((step * GROUP + j) * atoms, atoms)
            row = pl.ds(first + j, 1)
            ga = [pulls[a] for a in range(4)]
            u = [geo[a, row, :] for a in range(3)]
            flow = ga[1] * u[0] + ga[2] * u[1] + ga[3] * u[2]
            stretch = scalar_slope[:, here] * ga[0] + vector_slope[:, here] * flow
            value = vector_value[:, here]
            flat[0, row, :] = jnp.sum(stretch, axis=0, keepdims=True)
            for a in range(3):
                flat[a + 1, row, :] = jnp.sum(value * ga[a + 1], axis=0, keepdims=True)
        return carry

    over_groups(slots // GROUP, contract, 0)
    stretch = flat[0] + geo_pull[0]
    turn = [flat[a + 1] + geo_pull[a + 1] for a in range(3)]
    u = [geo[a] for a in range(3)]
    inner = turn[0] * u[0] + turn[1] * u[1] + turn[2] * u[2]
    gradient = [stretch * u[a] + (turn[a] - inner * u[a]) * geo[5] for a in range(3)]
    at_row = iota((8, atoms), 0)
    own = jnp.zeros((8, atoms), f32)
    for a in range(3):
        flat[a] = gradient[a]
        own = jnp.where(at_row == a, jnp.sum(gradient[a], axis=0, keepdims=True), own)

    def push(step, carry):
        blocks = []
        for j in range(GROUP):
            row = pl.ds(step * GROUP + j, 1)
            block = jnp.where(at_row == 0, flat[0, row, :], jnp.where(at_row == 1, flat[1, row, :], flat[2, row, :]))
            blocks.append(block)
        block = jnp.concatenate(blocks, axis=1)
        top = block.astype(bf16).astype(f32)
        rest = block - top
        mid = rest.astype(bf16).astype(f32)
        split = jnp.concatenate([top, mid, rest - mid], axis=0).astype(bf16)
        at = span_of(step * GROUP * atoms, GROUP * atoms)
        chosen = jnp.concatenate([onehot[:atoms, at], onehot[2 * atoms : 2 * atoms + ghost_rows, at]], axis=0)
        return carry + dot_nt(chosen, split)

    ghost_rows = onehot.shape[0] // 2 - atoms
    zero = jnp.zeros((onehot.shape[0] // 2, 24), f32)
    pushed = over_groups(slots // GROUP, push, zero)
    pushed = jnp.transpose(pushed)
    pushed = (pushed[:8] + pushed[8:16] + pushed[16:]) * (1.0 / neighbor_norm)
    own = own - pushed[:, :atoms]
    velocities, mass = facts[1:4], facts[8:9]
    pieces[0:3] = (own * facts[7:8])[:3]
    blocks = ((ret_minus, slab_rows), (ret_plus, slab_rows), (ret_prev, sub_rows), (ret_next, sub_rows))
    start = atoms
    ghost_lines = [[0.0] * 3 for _ in range(3)]
    for i, (ref, count) in enumerate(blocks):
        told = ref[count : count + 8, :count]
        force = -pushed[:, start : start + count]
        start += count
        for a in range(3):
            for b in range(3):
                ghost_lines[a][b] = ghost_lines[a][b] + told[a + 1 : a + 2] * force[b : b + 1]
        scaled = force * told[7:8]
        top = scaled.astype(bf16).astype(f32)
        rest = scaled - top
        mid = rest.astype(bf16).astype(f32)
        split = jnp.concatenate([top, mid, rest - mid], axis=0).astype(bf16)
        place = (iota((atoms, count), 0) == told[0:1].astype(jnp.int32)).astype(bf16)
        spread = dot_nt(split, place)
        pieces[3 * i + 3 : 3 * i + 6] = (spread[:8] + spread[8:16] + spread[16:])[:3]
    came[...] = jnp.zeros_like(came)
    for i, (ref, count) in enumerate(blocks):
        came[:, i * moves : (i + 1) * moves] = ref[count : count + 8, atoms : atoms + moves]

    def line(a, b):
        start = velocities[a : a + 1] * velocities[b : b + 1] * mass
        mixed = velocities[a : a + 1] * own[b : b + 1] + velocities[b : b + 1] * own[a : a + 1]
        return start + time_step * mixed - jnp.sum(u[a] * geo[4] * gradient[b], axis=0, keepdims=True)

    lines = jnp.concatenate([line(a, b) for a in range(3) for b in range(3)] + [jnp.zeros((7, atoms), f32)], axis=0)
    ghosts = [time_step * (ghost_lines[a][b] + ghost_lines[b][a]) for a in range(3) for b in range(3)]
    ghosts = jnp.concatenate(ghosts + [jnp.zeros((7, slab_rows), f32)], axis=0)
    summed = jnp.sum(lines, axis=1, keepdims=True) + jnp.sum(ghosts, axis=1, keepdims=True)
    row = jnp.zeros((1, atoms), f32)
    for i in range(9):
        row = jnp.where(iota((1, atoms), 1) == i, summed[i : i + 1], row)
    pieces[15:16] = row
    for i in range(everyone.shape[0]):
        everyone[i] = pieces[...]


def determinant(m):
    return (
        m[0][0] * (m[1][1] * m[2][2] - m[1][2] * m[2][1])
        - m[0][1] * (m[1][0] * m[2][2] - m[1][2] * m[2][0])
        + m[0][2] * (m[1][0] * m[2][1] - m[1][1] * m[2][0])
    )


def inverse(m):
    whole = determinant(m)
    return [
        [
            (
                m[(j + 1) % 3][(i + 1) % 3] * m[(j + 2) % 3][(i + 2) % 3]
                - m[(j + 1) % 3][(i + 2) % 3] * m[(j + 2) % 3][(i + 1) % 3]
            )
            / whole
            for j in range(3)
        ]
        for i in range(3)
    ]


def fifth_kernel(
    pieces, own_facts, came, box, box_speed,
    forces_out, velocities_out, positions_out, arrivals, new_box, new_box_speed,
    whole, *, atoms_all, slab_count, sub_count,
):
    atoms = own_facts.shape[1]
    velocities, positions = own_facts[1:4], own_facts[4:7]
    devices = slab_count * sub_count
    sub = lax.rem(iota((devices, atoms), 0), sub_count)

    def row_of_all(r):
        return pieces[:, r, :]

    def piece(i, a):
        return row_of_all(3 * i + a)

    def moved(x, step):
        return pltpu.roll(x, (-step) % devices, 0)

    for a in range(3):
        total = piece(0, a) + moved(piece(1, a), sub_count) + moved(piece(2, a), -sub_count)
        x = piece(3, a)
        total = total + jnp.where(sub == sub_count - 1, moved(x, 1 - sub_count), moved(x, 1))
        x = piece(4, a)
        whole[a] = total + jnp.where(sub == 0, moved(x, sub_count - 1), moved(x, -1))
    squares = {}
    for a in range(3):
        for b in range(a, 3):
            squares[a, b] = jnp.sum(whole[a] * whole[b], axis=0, keepdims=True)
    order = list(squares)
    squares = jnp.concatenate([squares[k] for k in order] + [jnp.zeros((2, atoms), f32)], axis=0)
    squares = jnp.sum(squares, axis=1, keepdims=True)
    rest = jnp.sum(row_of_all(15), axis=0, keepdims=True)
    stress = [[None] * 3 for _ in range(3)]
    for i in range(3):
        for j in range(3):
            at = order.index((min(i, j), max(i, j)))
            stress[i][j] = rest[:, 3 * i + j : 3 * i + j + 1] + (time_step * time_step) * squares[at : at + 1]
    slab_at, sub_at = lax.axis_index("slab"), lax.axis_index("sub")
    mine = slab_at * sub_count + sub_at
    root, mass = own_facts[7:8], own_facts[8:9]
    for a in range(3):
        force = whole[a, pl.ds(mine, 1), :] * (mass * root)
        forces_out[a : a + 1, :] = force
        velocities_out[a : a + 1, :] = velocities[a : a + 1, :] + time_step * force / mass
    lane, row = iota((8, atoms), 1), iota((8, atoms), 0)
    facts = came[...]
    index = jnp.broadcast_to(facts[0:1].astype(jnp.int32), (8, atoms))
    count = arrivals.shape[1] // 4
    picked = jnp.zeros((8, atoms), f32)
    for i, (slab_step, sub_step) in enumerate(((-1, 0), (1, 0), (0, -1), (0, 1))):
        slab = lax.rem(slab_at + (slab_step + slab_count), slab_count)
        source = slab * sub_count + lax.rem(sub_at + (sub_step + sub_count), sub_count)
        force = [whole[a, pl.ds(source, 1), :] for a in range(3)]
        force = jnp.where(row == 0, force[0], jnp.where(row == 1, force[1], force[2]))
        found = jnp.take_along_axis(force, index, axis=1)
        picked = jnp.where((lane >= i * count) & (lane < (i + 1) * count), found, picked)
    speeds = [facts[1 + a : 2 + a] + time_step * picked[a : a + 1] * facts[7:8] for a in range(3)]

    def spread(value):
        return jnp.full((1, atoms), value, f32)

    old = [[spread(box[i, j]) for j in range(3)] for i in range(3)]
    volume = determinant(old)
    old_inverse = inverse(old)
    for i in range(3):
        stress[i][i] = stress[i][i] - outside_pressure * volume
    fresh = [[None] * 3 for _ in range(3)]
    for i in range(3):
        for j in range(3):
            push = stress[i][0] * old_inverse[j][0] + stress[i][1] * old_inverse[j][1] + stress[i][2] * old_inverse[j][2]
            speed = spread(box_speed[i, j]) + time_step * push / (box_mass * atoms_all)
            fresh[i][j] = old[i][j] + time_step * speed
            new_box_speed[i : i + 1, j : j + 1] = speed[:, :1]
            new_box[i : i + 1, j : j + 1] = fresh[i][j][:, :1]
    new_inverse = inverse(fresh)
    for i in range(3):
        move = sum(new_inverse[i][j] * velocities_out[j : j + 1, :] for j in range(3))
        positions_out[i : i + 1, :] = positions[i : i + 1, :] + time_step * move
    for i in range(3):
        move = sum(new_inverse[i][j] * speeds[j] for j in range(3))
        arrivals[i : i + 1, :] = (facts[4 + i : 5 + i] + time_step * move)[:, : 4 * count]
        arrivals[3 + i : 4 + i, :] = speeds[i][:, : 4 * count]


VM = pl.BlockSpec(memory_space=pltpu.VMEM)
HB = pl.BlockSpec(memory_space=pltpu.HBM)
SM = pl.BlockSpec(memory_space=pltpu.SMEM)


def shape(*dims, dtype=f32):
    return jax.ShapeDtypeStruct(dims, dtype)


def call(kernel, outs, scalar_inputs=(), far_inputs=False, far_outputs=(), scratch=(), flops=0, vmem=16, name=None):
    def run(*args):
        moved = sum(math.prod(x.shape) * x.dtype.itemsize for x in list(args) + list(outs))
        return pl.pallas_call(
            kernel,
            out_shape=tuple(outs),
            in_specs=[HB if far_inputs else SM if i in scalar_inputs else VM for i in range(len(args))],
            out_specs=tuple(HB if i in far_outputs else VM for i in range(len(outs))),
            scratch_shapes=list(scratch),
            compiler_params=pltpu.CompilerParams(vmem_limit_bytes=vmem * 1024 * 1024),
            cost_estimate=pl.CostEstimate(flops=flops, bytes_accessed=moved, transcendentals=0),
            name=name,
        )(*args)

    return run


def body(
    positions, velocities, species, ghost_species, neighbours, slot_mask, edge_vectors, send_slab, send_sub, migrants,
    embedding, energy_shift, masses, radial_one_in, radial_one_mid, radial_one_out, node_one,
    radial_two_in, radial_two_mid, radial_two_out, node_two, readout_linear, readout_hidden, readout_out,
    box_matrix, box_velocity,
):
    slots, atoms = neighbours.shape
    width = node_one.shape[1]
    hidden = radial_one_mid.shape[1]
    depth = 4 * width
    ghost_slab, ghost_sub = send_slab.shape[1], send_sub.shape[1]
    extended = atoms + 2 * ghost_slab + 2 * ghost_sub
    edges = slots * atoms
    devices = lax.axis_size("slab") * lax.axis_size("sub")
    species_row = species.reshape(1, atoms)
    ghost_row = ghost_species.reshape(1, -1)
    linear_row = readout_linear.reshape(1, -1)
    out_row = readout_out.reshape(1, -1)
    radial_one_in, radial_one_out = jnp.transpose(radial_one_in), jnp.transpose(radial_one_out)
    radial_two_in, radial_two_out = jnp.transpose(radial_two_in), jnp.transpose(radial_two_out)

    first_inputs = (
        edge_vectors, slot_mask, neighbours, species_row, ghost_row, embedding,
        radial_one_in, radial_one_mid, radial_one_out, node_one, send_slab, send_sub,
        velocities, positions, migrants, masses.reshape(1, -1), energy_shift.reshape(1, -1),
        readout_hidden, linear_row, out_row, radial_two_in, radial_two_mid, radial_two_out, node_two,
    )
    packed_rows = (
        8 * width + 6 * packed_step(slots) + FACTS + 6 * hidden + radial_two_in.shape[0] + packed_step(slots)
        + readout_hidden.shape[0] + 8
    )
    kinds, sums, packed, to_minus, to_plus, to_prev, to_next = call(
        first_kernel,
        (
            shape(slots, atoms, dtype=jnp.int32),
            shape(5, width, atoms),
            shape(packed_rows, atoms),
            shape(ghost_slab, depth),
            shape(ghost_slab, depth),
            shape(ghost_sub, depth),
            shape(ghost_sub, depth),
        ),
        far_inputs=True,
        far_outputs=(1, 2),
        scratch=(
            pltpu.VMEM((6, slots, atoms), f32),
            pltpu.VMEM((packed_rows, atoms), f32),
            pltpu.VMEM((5, width, atoms), f32),
        )
        + tuple(pltpu.VMEM(x.shape, x.dtype) for x in first_inputs)
        + (pltpu.SemaphoreType.DMA((FIRST_INPUTS,)), pltpu.SemaphoreType.DMA((4,))),
        flops=6 * edges * 26000,
        vmem=56,
        name="layer_one",
    )(
        *first_inputs
    )
    from_minus, from_plus, from_prev, from_next = trade(to_minus, to_plus, to_prev, to_next)

    def radial(*refs):
        radial_kernel(
            *refs,
            slab_rows=ghost_slab,
            sub_rows=ghost_sub,
            moves=migrants.shape[1],
            basis_count=radial_two_in.shape[0],
        )

    (
        weights_all, slopes, onehot, outer, forward_high, forward_low, backward_high, backward_low,
        geo, own_table, scalars, extras, facts, heads,
    ) = call(
        radial,
        (
            shape(depth, edges),
            shape(3 * hidden, edges, dtype=bf16),
            shape(2 * extended, edges, dtype=bf16),
            shape(depth, 3 * hidden, dtype=bf16),
            shape(width, 3 * width, dtype=bf16),
            shape(width, 3 * width, dtype=bf16),
            shape(3 * width, width, dtype=bf16),
            shape(3 * width, width, dtype=bf16),
            shape(6, slots, atoms),
            shape(depth, 2 * atoms, dtype=bf16),
            shape(width, atoms),
            shape(4, 8, 2 * atoms),
            shape(FACTS, atoms),
            shape(readout_hidden.shape[0] + 8, atoms),
        ),
        flops=12 * edges * 10000,
        vmem=12,
        name="radial_two",
    )(
        packed,
    )

    energy, scalar_pull, picked_all, pulls, own_pull, back_minus, back_plus, back_prev, back_next = call(
        second_kernel,
        (
            shape(1, atoms),
            shape(width, atoms),
            shape(depth, edges),
            shape(4, width, atoms),
            shape(atoms, depth),
            shape(ghost_slab + 8, depth),
            shape(ghost_slab + 8, depth),
            shape(ghost_sub + 8, depth),
            shape(ghost_sub + 8, depth),
        ),
        scratch=(pltpu.VMEM((depth, 2 * extended), bf16), pltpu.VMEM((extended, depth), f32)),
        flops=4 * edges * depth * extended * 2,
        vmem=28,
        name="layer_two",
    )(
        geo, own_table, from_minus, from_plus, from_prev, from_next, scalars, extras,
        weights_all, onehot, forward_high, forward_low, backward_high, backward_low, heads,
    )
    ret_minus, ret_plus, ret_prev, ret_next = trade(back_minus, back_plus, back_prev, back_next)
    (geo_pull,) = call(
        edge_kernel,
        (shape(4, slots, atoms),),
        flops=edges * depth * 400,
        vmem=16,
        name="edge_two",
    )(geo, slopes, outer, picked_all, weights_all, pulls)
    scalar_slope, vector_slope, vector_value, turned_high, turned_low, linear = call(
        slope_kernel,
        (
            shape(width, edges),
            shape(width, edges),
            shape(width, edges),
            shape(7 * width, width, dtype=bf16),
            shape(7 * width, width, dtype=bf16),
            shape(width, atoms),
        ),
        flops=12 * edges * 20000,
        vmem=12,
        name="radial_one",
    )(
        geo, kinds, scalar_pull, embedding, radial_one_in, radial_one_mid, radial_one_out, node_one, node_two, linear_row,
    )


    def back(*refs):
        third_kernel(*refs, moves=migrants.shape[1], slab_rows=ghost_slab, sub_rows=ghost_sub)

    everyone, came = call(
        back,
        (shape(devices, 16, atoms), shape(8, atoms)),
        scratch=(
            pltpu.VMEM((16, atoms), f32),
            pltpu.VMEM((4, width, atoms), f32),
            pltpu.VMEM((4, slots, atoms), f32),
        ),
        flops=6 * edges * 1000,
        vmem=12,
        name="layer_one_back",
    )(
        facts, geo, sums, geo_pull, scalar_pull, own_pull, ret_minus, ret_plus, ret_prev, ret_next,
        onehot, scalar_slope, vector_slope, vector_value, turned_high, turned_low, linear,
    )
    everyone = lax.all_to_all(everyone, ("slab", "sub"), 0, 0, tiled=True)

    def last(*refs):
        fifth_kernel(
            *refs, atoms_all=atoms * devices, slab_count=lax.axis_size("slab"), sub_count=lax.axis_size("sub")
        )

    forces, new_velocities, new_positions, arrivals, new_box, new_box_velocity = call(
        last,
        (
            shape(3, atoms), shape(3, atoms), shape(3, atoms), shape(6, 4 * migrants.shape[1]),
            shape(3, 3), shape(3, 3),
        ),
        scalar_inputs=(3, 4),
        scratch=(pltpu.VMEM((3, devices, atoms), f32),),
        flops=1000000,
        vmem=8,
        name="box",
    )(everyone, facts, came, box_matrix, box_velocity)
    return energy.reshape(atoms), forces, new_velocities, new_positions, arrivals, new_box, new_box_velocity


def solution(mesh):
    split = ("slab", "sub")
    one, two, three, copied = P(split), P(None, split), P(None, None, split), P()
    placed = (two, two, one, one, two, two, three, two, two, two) + (copied,) * 16
    return jax.shard_map(
        body,
        mesh=mesh,
        in_specs=placed,
        out_specs=(one, two, two, two, two, copied, copied),
        check_vma=False,
    )
```

```python
import math

import jax
import jax.numpy as jnp
from jax import lax
from jax.experimental import pallas as pl
from jax.experimental.pallas import tpu as pltpu
from jax.sharding import PartitionSpec as P

cutoff = 5.0
neighbor_norm = 0.125
time_step = 0.5
outside_pressure = 0.5
box_mass = 0.125
highest = lax.Precision.HIGHEST
f32 = jnp.float32
bf16 = jnp.bfloat16
GROUP = 4


def shifted(block, axis, distance):
    count = lax.axis_size(axis)
    return lax.ppermute(block, axis, [((i - distance) % count, i) for i in range(count)])


def trade(to_minus, to_plus, to_prev, to_next):
    from_minus, from_plus = shifted(to_plus, "slab", 1), shifted(to_minus, "slab", -1)
    return from_minus, from_plus, shifted(to_next, "sub", 1), shifted(to_prev, "sub", -1)


def parts(x):
    high = x.astype(bf16)
    return high, (x - high.astype(f32)).astype(bf16)


def dot(a, b):
    return jnp.dot(a, b, preferred_element_type=f32)


def dot_nt(a, b):
    return lax.dot_general(a, b, (((1,), (1,)), ((), ())), preferred_element_type=f32)


def exact(a, b, dims=((1,), (0,))):
    return lax.dot_general(a, b, (dims, ((), ())), precision=highest, preferred_element_type=f32)


def product(weight, x):
    high, low = parts(x)
    return dot(weight[0], high) + dot(weight[0], low) + dot(weight[1], high)


def weight_stack(w):
    high = w.astype(bf16).astype(f32)
    return jnp.concatenate([high, high, w - high], axis=1).astype(bf16)


def weight_stack_t(w):
    high = w.astype(bf16).astype(f32)
    return jnp.transpose(jnp.concatenate([high, high, w - high], axis=0)).astype(bf16)


def value_stack(x):
    high, low = parts(x)
    return jnp.concatenate([high, low, high], axis=0)


def value_stack_small(x):
    high = x.astype(bf16).astype(f32)
    return jnp.concatenate([high, x - high, high], axis=0).astype(bf16)


def over_groups(count, step, carry):
    for i in range(count):
        carry = step(i, carry)
    return carry


def span_of(first, count):
    if isinstance(first, int):
        return pl.ds(first, count)
    return pl.ds(pl.multiple_of(first, count), count)


def iota(shape, axis):
    return lax.broadcasted_iota(jnp.int32, shape, axis)


def column(row):
    n = row.shape[1]
    return jnp.sum(jnp.where(iota((n, n), 0) == iota((n, n), 1), row, 0.0), axis=1, keepdims=True)


def sigmoid(x):
    return 0.5 + 0.5 * jnp.tanh(0.5 * x)


def basis(distance, inverse_distance, count):
    scaled = distance * (1.0 / cutoff)
    second = scaled * scaled
    fourth = second * second
    fifth = fourth * scaled
    sixth = fourth * second
    scale = math.sqrt(2.0 / cutoff)
    envelope = 1.0 + sixth * (-28.0 + scaled * (48.0 - 21.0 * scaled))
    front = scale * envelope * inverse_distance
    slope_envelope = fifth * (-168.0 + scaled * (336.0 - 168.0 * scaled)) * (1.0 / cutoff)
    slope_front = scale * inverse_distance * (slope_envelope - envelope * inverse_distance)
    angle = math.pi * scaled
    first_sine, first_cosine = jnp.sin(angle), jnp.cos(angle)
    sine, cosine = first_sine, first_cosine
    values, slopes = [], []
    for order in range(1, count + 1):
        if order > 1:
            sine, cosine = (
                sine * first_cosine + cosine * first_sine,
                cosine * first_cosine - sine * first_sine,
            )
        values.append(sine * front)
        slopes.append(sine * slope_front + cosine * (front * (order * math.pi / cutoff)))
    return values, slopes


def basis_group(waves, first, start, count):
    return jnp.concatenate([waves[start : start + count, first + j, :] for j in range(GROUP)], axis=1)


def hidden_values(value, inner, mid_a, mid_b):
    x = dot(inner, value_stack_small(value))
    h = x * sigmoid(x)
    x = dot(mid_a, value_stack(h))
    h = x * sigmoid(x)
    x = dot(mid_b, value_stack(h))
    return x * sigmoid(x)


def hidden_pairs(value, slope, inner, mid_a, mid_b):
    x, dx = dot(inner, value_stack_small(value)), dot(inner, value_stack_small(slope))
    for mid in (mid_a, mid_b, None):
        gate = sigmoid(x)
        h = x * gate
        dh = (gate + h * (1.0 - gate)) * dx
        if mid is not None:
            x, dx = dot(mid, value_stack(h)), dot(mid, value_stack(dh))
    return h, dh


def species_matrix(first_mixing, embedding):
    lifted = exact(first_mixing, embedding, ((1,), (1,)))
    high = lifted.astype(bf16).astype(f32)
    rest = lifted - high
    mid = rest.astype(bf16).astype(f32)
    return jnp.concatenate([high, mid, rest - mid], axis=1).astype(bf16)


def picked_group(lifted, geo, kinds, first, species_count):
    blocks = []
    for j in range(GROUP):
        kind = kinds[pl.ds(first + j, 1), :]
        weight = geo[3, pl.ds(first + j, 1), :]
        blocks.append(jnp.where(iota((species_count, kind.shape[1]), 0) == kind, weight, 0.0))
    block = jnp.concatenate(blocks, axis=1)
    return dot(lifted, jnp.concatenate([block, block, block], axis=0).astype(bf16))


def send_onehot(facts, first, slab_rows, sub_rows):
    atoms = facts.shape[1]
    lengths = (slab_rows, slab_rows, sub_rows, sub_rows)
    rows = [facts[first + 9 + i : first + 10 + i, :n] for i, n in enumerate(lengths)]
    rows = jnp.concatenate(rows, axis=1)
    return (iota((atoms, rows.shape[1]), 0).astype(f32) == rows).astype(f32)


FIRST_INPUTS = 24
FACTS = 16


def packed_step(slots):
    return -(-slots // 8) * 8


def first_kernel(
    *refs,
):
    count = FIRST_INPUTS
    buffers, ready, gone = refs[-count - 2 : -2], refs[-2], refs[-1]
    copies = [pltpu.make_async_copy(refs[i], buffers[i], ready.at[i]) for i in range(count)]
    for copy in copies:
        copy.start()
    (
        edges, mask, neighbours, species, ghosts, embedding, radial_in, radial_mid, radial_out, node_one,
        send_slab, send_sub, velocities, positions, migrants, masses, shifts,
        hidden_head, linear_head, out_head, next_in, next_mid, next_out, node_two,
    ) = buffers
    kinds, far_sums, far_packed, to_minus, to_plus, to_prev, to_next, geo, waves, packed, sums = refs[count : -count - 2]
    for copy in copies[:2]:
        copy.wait()
    slots, atoms = mask.shape
    width = node_one.shape[1]
    species_count, basis_count = embedding.shape[0], radial_in.shape[0]
    ex, ey, ez = edges[0], edges[1], edges[2]
    square = ex * ex + ey * ey + ez * ez
    distance = jnp.sqrt(square)
    inverse_distance = 1.0 / distance
    for a, e in enumerate((ex, ey, ez)):
        geo[a] = e * inverse_distance
    geo[3] = mask[...].astype(f32) * neighbor_norm
    geo[4] = distance
    geo[5] = inverse_distance
    base = 5 * width
    step = packed_step(slots)
    values, slopes = basis(distance, inverse_distance, radial_in.shape[0])
    for i, wave in enumerate(values + slopes):
        waves[i] = wave
    for a in range(6):
        packed[base + a * step : base + a * step + slots] = geo[a]
    for copy in copies[2:5]:
        copy.wait()
    ghost_row = ghosts[...]
    extra = -ghost_row.shape[1] % atoms
    if extra:
        ghost_row = jnp.concatenate([ghost_row, jnp.zeros((1, extra), jnp.int32)], axis=1)
    tables = [species[...]] + [ghost_row[:, i : i + atoms] for i in range(0, ghost_row.shape[1], atoms)]
    pad = -slots % 8
    rows = neighbours[...]
    if pad:
        rows = jnp.concatenate([rows, jnp.zeros((pad, atoms), jnp.int32)], axis=0)
    inner_index = lax.rem(rows, atoms)
    block_index = lax.div(rows, atoms)
    found = jnp.zeros_like(rows)
    for i, table in enumerate(tables):
        spread = jnp.broadcast_to(table, rows.shape)
        got = jnp.take_along_axis(spread, inner_index, axis=1)
        found = jnp.where(block_index == i, got, found)
    kinds[...] = found[:slots]

    for copy in copies[5:10]:
        copy.wait()
    inner = weight_stack_t(radial_in[...])
    mid_a, mid_b = weight_stack(radial_mid[0]), weight_stack(radial_mid[1])
    outer = weight_stack_t(radial_out[...])
    lifted = species_matrix(node_one[0], embedding[...])
    sums[...] = jnp.zeros_like(sums)

    def group(step, carry):
        first = step * GROUP
        value = basis_group(waves, first, 0, basis_count)
        h = hidden_values(value, inner, mid_a, mid_b)
        weights = dot(outer, value_stack(h))
        picked = picked_group(lifted, geo, kinds, first, species_count)
        totals = [0.0] * 4
        for j in range(GROUP):
            at = slice(j * atoms, (j + 1) * atoms)
            p = picked[:, at]
            totals[0] = totals[0] + weights[:width, at] * p
            q = weights[width:, at] * p
            for a in range(3):
                totals[a + 1] = totals[a + 1] + q * geo[a, pl.ds(first + j, 1), :]
        for a in range(4):
            sums[a] += totals[a]
        return carry

    over_groups(slots // GROUP, group, 0)

    early_sums = pltpu.make_async_copy(sums.at[:4], far_sums.at[:4], gone.at[2])
    early_sums.start()
    for copy in copies[10:]:
        copy.wait()
    mass = shift = jnp.zeros((1, atoms), f32)
    for i in range(masses.shape[1]):
        mass = jnp.where(species[...] == i, masses[:, i : i + 1], mass)
        shift = jnp.where(species[...] == i, shifts[:, i : i + 1], shift)
    facts = base + 6 * step
    packed[facts : facts + 1] = iota((1, atoms), 1).astype(f32)
    packed[facts + 1 : facts + 4] = velocities[...]
    packed[facts + 4 : facts + 7] = positions[...]
    packed[facts + 7 : facts + 8] = 1.0 / jnp.sqrt(mass)
    packed[facts + 8 : facts + 9] = mass
    packed[facts + 9 : facts + FACTS] = jnp.zeros((FACTS - 9, atoms), f32)
    for i, (lists, at) in enumerate(((send_slab, 1), (send_slab, 0), (send_sub, 1), (send_sub, 0))):
        packed[facts + 9 + i : facts + 10 + i, : lists.shape[1]] = lists[at : at + 1, :].astype(f32)
    count = migrants.shape[1]
    for i, at in enumerate((1, 0, 3, 2)):
        packed[facts + 13 : facts + 14, i * count : (i + 1) * count] = migrants[at : at + 1, :].astype(f32)
    inner_rows = next_mid.shape[1]
    start = facts + FACTS
    for i in range(3):
        packed[start : start + width] = node_two[i + 2]
        start += width
    for i in range(next_out.shape[1] // atoms):
        packed[start : start + inner_rows] = next_out[:, i * atoms : (i + 1) * atoms]
        start += inner_rows
    for i in range(2):
        packed[start : start + inner_rows, :inner_rows] = next_mid[i]
        start += inner_rows
    packed[start : start + next_in.shape[0], :inner_rows] = next_in[...]
    start += next_in.shape[0]
    packed[start : start + slots] = neighbours[...].astype(f32)
    start += step
    count = hidden_head.shape[0]
    packed[start : start + count] = hidden_head[...]
    packed[start + count : start + count + 1] = linear_head[...]
    packed[start + count + 1 : start + count + 2, : out_head.shape[1]] = out_head[...]
    packed[start + count + 2 : start + count + 3] = shift
    start += count + 8
    for i in range(waves.shape[0]):
        packed[start + i * step : start + i * step + slots] = waves[i]
    early = pltpu.make_async_copy(packed.at[base:], far_packed.at[base:], gone.at[0])
    early.start()

    own_onehot = (iota((species_count, atoms), 0) == species[...]).astype(f32)
    own = exact(embedding[...], own_onehot, ((0,), (0,)))
    scalar_sum = sums[0]
    vectors = [sums[1], sums[2], sums[3]]
    squares = vectors[0] * vectors[0] + vectors[1] * vectors[1] + vectors[2] * vectors[2]
    scalars = (
        own
        + product(parts(node_one[1]), scalar_sum)
        + product(parts(node_one[2]), scalar_sum * scalar_sum)
        + product(parts(node_one[3]), squares)
    )
    gate = product(parts(node_one[5]), scalar_sum)
    sums[4] = gate
    late_sums = pltpu.make_async_copy(sums.at[4:], far_sums.at[4:], gone.at[3])
    late_sums.start()
    turned = product(parts(node_one[4]), jnp.concatenate(vectors, axis=1))
    moved = turned + jnp.concatenate([gate * v for v in vectors], axis=1)
    packed[:width] = scalars
    x = product(parts(node_two[0]), scalars)
    y = product(parts(node_two[1]), moved)
    table = jnp.concatenate([x] + [y[:, a * atoms : (a + 1) * atoms] for a in range(3)], axis=0)
    packed[width : 5 * width] = table
    late = pltpu.make_async_copy(packed.at[:base], far_packed.at[:base], gone.at[1])
    late.start()
    pick = send_onehot(packed, facts, send_slab.shape[1], send_sub.shape[1]).astype(bf16)
    high, low = parts(table)
    sent = jnp.transpose(dot(high, pick) + dot(low, pick))
    slab_rows = send_slab.shape[1]
    to_plus[...] = sent[:slab_rows]
    to_minus[...] = sent[slab_rows : 2 * slab_rows]
    sub_rows = send_sub.shape[1]
    to_next[...] = sent[2 * slab_rows : 2 * slab_rows + sub_rows]
    to_prev[...] = sent[2 * slab_rows + sub_rows :]
    for copy in (early, late, early_sums, late_sums):
        copy.wait()


def radial_kernel(
    packed,
    weights_all, slopes, onehot, outer, forward_high, forward_low, backward_high, backward_low,
    geo, table, scalars, extras, facts, heads, waves, *, slab_rows, sub_rows, moves, basis_count,
):
    slots, atoms = geo.shape[1:]
    width = scalars.shape[0]
    depth = 4 * width
    inner_rows = slopes.shape[0] // 3
    scalars[...] = packed[:width]
    first_fact = 5 * width + 6 * packed_step(slots)
    start = first_fact + FACTS
    mixings = [packed[start + i * width : start + (i + 1) * width] for i in range(3)]
    start += 3 * width
    pieces = depth // atoms
    radial_out = [packed[start + i * inner_rows : start + (i + 1) * inner_rows] for i in range(pieces)]
    radial_out = jnp.concatenate(radial_out, axis=1)
    start += pieces * inner_rows
    radial_mid = [packed[start + i * inner_rows : start + (i + 1) * inner_rows, :inner_rows] for i in range(2)]
    start += 2 * inner_rows
    radial_in = packed[start : start + basis_count, :inner_rows]
    first_row = start + basis_count
    start = first_row + packed_step(slots)
    heads[...] = packed[start : start + heads.shape[0]]
    start += heads.shape[0]
    for i in range(2 * basis_count):
        waves[i] = packed[start + i * packed_step(slots) : start + i * packed_step(slots) + slots]
    table[:, :atoms], table[:, atoms:] = parts(packed[width : 5 * width])
    for a in range(6):
        start = 5 * width + a * packed_step(slots)
        geo[a] = packed[start : start + slots]
    facts[...] = packed[first_fact : first_fact + FACTS]
    listed = exact(facts[:8], send_onehot(facts, 0, slab_rows, sub_rows))
    moving = exact(facts[:8], (iota((atoms, 4 * moves), 0).astype(f32) == facts[13:14, : 4 * moves]).astype(f32))
    start = 0
    extras[...] = jnp.zeros_like(extras)
    for i, length in enumerate((slab_rows, slab_rows, sub_rows, sub_rows)):
        extras[i, :, :length] = listed[:, start : start + length]
        extras[i, :, atoms : atoms + moves] = moving[:, i * moves : (i + 1) * moves]
        start += length
    rows = onehot.shape[0] // 2
    outer[...] = weight_stack_t(radial_out)
    mixing = jnp.concatenate(mixings, axis=1)
    forward_high[...], forward_low[...] = parts(mixing)
    turned = jnp.concatenate([jnp.transpose(m) for m in mixings], axis=0)
    backward_high[...], backward_low[...] = parts(turned)
    inner = weight_stack_t(radial_in)
    mid_a, mid_b = weight_stack(radial_mid[0]), weight_stack(radial_mid[1])

    def group(step, carry):
        first = step * GROUP
        at = span_of(step * GROUP * atoms, GROUP * atoms)
        value, slope = (basis_group(waves, first, i * basis_count, basis_count) for i in range(2))
        h, dh = hidden_pairs(value, slope, inner, mid_a, mid_b)
        slopes[:, at] = value_stack(dh)
        blocks = []
        for j in range(GROUP):
            row = packed[first_row + first + j : first_row + first + j + 1]
            weight = geo[3, pl.ds(first + j, 1), :]
            row = row.astype(jnp.int32)
            blocks.append(jnp.where(iota((rows, atoms), 0) == row, weight, 0.0).astype(bf16))
        block = jnp.concatenate(blocks, axis=1)
        own, ghosts = block[:atoms], block[atoms:]
        onehot[:, at] = jnp.concatenate([own, own, ghosts, ghosts], axis=0)
        weights_all[:, at] = dot(outer[...], value_stack(h))
        return carry

    over_groups(slots // GROUP, group, 0)


def second_kernel(
    geo, own_table, from_minus, from_plus, from_prev, from_next, scalars, extras,
    weights_all, onehot, forward_high, forward_low, backward_high, backward_low, heads,
    energy, scalar_pull, picked_all, sums, own_pull, back_minus, back_plus, back_prev, back_next,
    table, pulled,
):
    slots, atoms = geo.shape[1], geo.shape[2]
    width = scalars.shape[0]
    depth = 4 * width
    ghosts = jnp.concatenate([from_minus[...], from_plus[...], from_prev[...], from_next[...]], axis=0)
    high = ghosts.astype(bf16).astype(f32)
    table[:, : 2 * atoms] = own_table[...]
    table[:, 2 * atoms :] = jnp.transpose(jnp.concatenate([high, ghosts - high], axis=0)).astype(bf16)
    ghost_rows = ghosts.shape[0]
    sums[...] = jnp.zeros_like(sums)

    def units(first, j):
        return [geo[a, pl.ds(first + j, 1), :] for a in range(3)]

    def forward(step, carry):
        first = step * GROUP
        at = span_of(step * GROUP * atoms, GROUP * atoms)
        picked = dot(table[...], onehot[:, at])
        picked_all[:, at] = picked
        totals = [0.0] * 4
        for j in range(GROUP):
            span = slice(j * atoms, (j + 1) * atoms)
            here = span_of((step * GROUP + j) * atoms, atoms)
            p = [picked[a * width : (a + 1) * width, span] for a in range(4)]
            r = [weights_all[a * width : (a + 1) * width, here] for a in range(4)]
            u = units(first, j)
            along = p[1] * u[0] + p[2] * u[1] + p[3] * u[2]
            totals[0] = totals[0] + (r[0] * p[0] + r[3] * along)
            q = r[1] * p[0]
            for a in range(3):
                totals[a + 1] = totals[a + 1] + (q * u[a] + r[2] * p[a + 1])
        for a in range(4):
            sums[a] += totals[a]
        return carry

    over_groups(slots // GROUP, forward, 0)

    scalar_sum = sums[0]
    vectors = [sums[1], sums[2], sums[3]]
    squares = vectors[0] * vectors[0] + vectors[1] * vectors[1] + vectors[2] * vectors[2]
    mixed = jnp.concatenate([scalar_sum, scalar_sum * scalar_sum, squares], axis=0)
    second = scalars[...] + product((forward_high[...], forward_low[...]), mixed)
    units_out = heads.shape[0] - 8
    readout_hidden = heads[:units_out]
    readout_linear, readout_out = heads[units_out : units_out + 1], heads[units_out + 1 : units_out + 2, :units_out]
    hidden_in = product(parts(readout_hidden), second)
    hidden_gate = sigmoid(hidden_in)
    hidden = hidden_in * hidden_gate
    shift = heads[units_out + 2 : units_out + 3]
    energy[...] = shift + exact(readout_linear, scalars[...]) + exact(readout_out, hidden)
    hidden_pull = column(readout_out) * (hidden_gate + hidden * (1.0 - hidden_gate))
    second_pull = exact(readout_hidden, hidden_pull, ((0,), (0,)))
    scalar_pull[...] = second_pull
    spread = product((backward_high[...], backward_low[...]), second_pull)
    double = 2.0 * spread[2 * width :]
    sums[0] = spread[:width] + 2.0 * scalar_sum * spread[width : 2 * width]
    for a in range(3):
        sums[a + 1] = vectors[a] * double
    pulled[...] = jnp.zeros_like(pulled)

    def backward(step, carry):
        first = step * GROUP
        at = span_of(step * GROUP * atoms, GROUP * atoms)
        highs, lows = [], []
        for j in range(GROUP):
            here = span_of((step * GROUP + j) * atoms, atoms)
            r = [weights_all[a * width : (a + 1) * width, here] for a in range(4)]
            u = units(first, j)
            ga = [sums[a] for a in range(4)]
            flow = ga[1] * u[0] + ga[2] * u[1] + ga[3] * u[2]
            pull = r[3] * ga[0]
            given = [r[0] * ga[0] + r[1] * flow] + [pull * u[a] + r[2] * ga[a + 1] for a in range(3)]
            high, low = parts(jnp.concatenate(given, axis=0))
            highs.append(high)
            lows.append(low)
        split = jnp.concatenate(highs + lows, axis=1)
        chosen = jnp.concatenate([onehot[:atoms, at], onehot[2 * atoms : 2 * atoms + ghost_rows, at]], axis=0)
        pulled[...] += dot_nt(jnp.concatenate([chosen, chosen], axis=1), split)
        return carry

    over_groups(slots // GROUP, backward, 0)
    own_pull[...] = pulled[:atoms]
    start = atoms
    fill = jnp.zeros((8, depth - extras.shape[2]), f32)
    for out, which in ((back_minus, 1), (back_plus, 0), (back_prev, 3), (back_next, 2)):
        count = out.shape[0] - 8
        out[:count] = pulled[start : start + count]
        out[count:] = jnp.concatenate([extras[which], fill], axis=1)
        start += count


def edge_kernel(geo, slopes, outer, picked_all, weights_all, sums, geo_pull):
    slots, atoms = geo.shape[1], geo.shape[2]
    width = sums.shape[1]

    def group(step, carry):
        first = step * GROUP
        slope = dot(outer[...], slopes[:, span_of(step * GROUP * atoms, GROUP * atoms)])
        for j in range(GROUP):
            span = slice(j * atoms, (j + 1) * atoms)
            here = span_of((step * GROUP + j) * atoms, atoms)
            p = [picked_all[a * width : (a + 1) * width, here] for a in range(4)]
            r = [weights_all[a * width : (a + 1) * width, here] for a in (1, 3)]
            s = [slope[a * width : (a + 1) * width, span] for a in range(4)]
            u = [geo[a, pl.ds(first + j, 1), :] for a in range(3)]
            ga = [sums[a] for a in range(4)]
            along = p[1] * u[0] + p[2] * u[1] + p[3] * u[2]
            flow = ga[1] * u[0] + ga[2] * u[1] + ga[3] * u[2]
            cross = p[1] * ga[1] + p[2] * ga[2] + p[3] * ga[3]
            stretch = p[0] * (s[0] * ga[0] + s[1] * flow) + s[2] * cross + s[3] * (along * ga[0])
            geo_pull[0, pl.ds(first + j, 1), :] = jnp.sum(stretch, axis=0, keepdims=True)
            lean = r[0] * p[0]
            pull = r[1] * ga[0]
            for a in range(3):
                turn = lean * ga[a + 1] + pull * p[a + 1]
                geo_pull[a + 1, pl.ds(first + j, 1), :] = jnp.sum(turn, axis=0, keepdims=True)
        return carry

    over_groups(slots // GROUP, group, 0)


def slope_kernel(
    geo, waves, kinds, after, embedding, radial_in, radial_mid, radial_out, node_one, node_two, readout_linear,
    scalar_slope, vector_slope, vector_value, turned_high, turned_low, linear,
):
    slots, atoms = kinds.shape
    width = node_one.shape[1]
    species_count, basis_count = embedding.shape[0], radial_in.shape[0]
    inner = weight_stack_t(radial_in[...])
    mid_a, mid_b = weight_stack(radial_mid[0]), weight_stack(radial_mid[1])
    outer = weight_stack_t(radial_out[...])
    lifted = species_matrix(node_one[0], embedding[...])
    linear[...] = jnp.broadcast_to(column(readout_linear[...]), linear.shape)
    mixings = [node_one[i] for i in (1, 2, 3, 4, 5)] + [node_two[0], node_two[1]]
    turned = jnp.concatenate([jnp.transpose(m) for m in mixings], axis=0)
    turned_high[...], turned_low[...] = parts(turned)

    def group(step, carry):
        first = step * GROUP
        at = span_of(step * GROUP * atoms, GROUP * atoms)
        value, slope = (basis_group(waves, first, i * basis_count, basis_count) for i in range(2))
        h, dh = hidden_pairs(value, slope, inner, mid_a, mid_b)
        picked = picked_group(lifted, geo, kinds, first, species_count)
        weights_slope = dot(outer, value_stack(dh))
        scalar_slope[:, at] = weights_slope[:width] * picked
        vector_slope[:, at] = weights_slope[width:] * picked
        vector_value[:, at] = dot(outer[width:], value_stack(h)) * picked
        return carry

    over_groups(slots // GROUP, group, 0)


def third_kernel(
    facts, geo, sums, geo_pull, scalar_pull, own_pull, ret_minus, ret_plus, ret_prev, ret_next,
    onehot, scalar_slope, vector_slope, vector_value, turned_high, turned_low, linear,
    everyone, came,
    pieces, pulls, flat, *, moves, slab_rows, sub_rows,
):
    slots, atoms = geo.shape[1], geo.shape[2]
    width = scalar_pull.shape[0]
    pick = send_onehot(facts, 0, slab_rows, sub_rows).astype(bf16)
    returned = jnp.concatenate(
        [ret_plus[:slab_rows], ret_minus[:slab_rows], ret_next[:sub_rows], ret_prev[:sub_rows]], axis=0
    )
    high, low = parts(returned)
    total = jnp.transpose(own_pull[...] + dot(pick, high) + dot(pick, low))
    x_pull = total[:width]
    y_pull = jnp.concatenate([total[a * width : (a + 1) * width] for a in (1, 2, 3)], axis=1)

    def turned(i, count=1):
        at = slice(i * width, (i + count) * width)
        return turned_high[at, :], turned_low[at, :]

    scalars = product(turned(5), x_pull) + linear[...] + scalar_pull[...]
    moved = product(turned(6), y_pull)
    gv = [moved[:, a * atoms : (a + 1) * atoms] for a in range(3)]
    scalar_sum, gate = sums[0], sums[4]
    vectors = [sums[1], sums[2], sums[3]]
    spread = product(turned(0, 3), scalars)
    mixed = product(turned(3), moved)
    gated = product(turned(4), gv[0] * vectors[0] + gv[1] * vectors[1] + gv[2] * vectors[2])
    pulls[0] = spread[:width] + 2.0 * scalar_sum * spread[width : 2 * width] + gated
    double = 2.0 * spread[2 * width :]
    for a in range(3):
        pulls[a + 1] = vectors[a] * double + mixed[:, a * atoms : (a + 1) * atoms] + gate * gv[a]

    def contract(step, carry):
        first = step * GROUP
        for j in range(GROUP):
            here = span_of((step * GROUP + j) * atoms, atoms)
            row = pl.ds(first + j, 1)
            ga = [pulls[a] for a in range(4)]
            u = [geo[a, row, :] for a in range(3)]
            flow = ga[1] * u[0] + ga[2] * u[1] + ga[3] * u[2]
            stretch = scalar_slope[:, here] * ga[0] + vector_slope[:, here] * flow
            value = vector_value[:, here]
            flat[0, row, :] = jnp.sum(stretch, axis=0, keepdims=True)
            for a in range(3):
                flat[a + 1, row, :] = jnp.sum(value * ga[a + 1], axis=0, keepdims=True)
        return carry

    over_groups(slots // GROUP, contract, 0)
    stretch = flat[0] + geo_pull[0]
    turn = [flat[a + 1] + geo_pull[a + 1] for a in range(3)]
    u = [geo[a] for a in range(3)]
    inner = turn[0] * u[0] + turn[1] * u[1] + turn[2] * u[2]
    gradient = [stretch * u[a] + (turn[a] - inner * u[a]) * geo[5] for a in range(3)]
    at_row = iota((8, atoms), 0)
    own = jnp.zeros((8, atoms), f32)
    for a in range(3):
        flat[a] = gradient[a]
        own = jnp.where(at_row == a, jnp.sum(gradient[a], axis=0, keepdims=True), own)

    def push(step, carry):
        blocks = []
        for j in range(GROUP):
            row = pl.ds(step * GROUP + j, 1)
            block = jnp.where(at_row == 0, flat[0, row, :], jnp.where(at_row == 1, flat[1, row, :], flat[2, row, :]))
            blocks.append(block)
        block = jnp.concatenate(blocks, axis=1)
        top = block.astype(bf16).astype(f32)
        rest = block - top
        mid = rest.astype(bf16).astype(f32)
        split = jnp.concatenate([top, mid, rest - mid], axis=0).astype(bf16)
        at = span_of(step * GROUP * atoms, GROUP * atoms)
        chosen = jnp.concatenate([onehot[:atoms, at], onehot[2 * atoms : 2 * atoms + ghost_rows, at]], axis=0)
        return carry + dot_nt(chosen, split)

    ghost_rows = onehot.shape[0] // 2 - atoms
    zero = jnp.zeros((onehot.shape[0] // 2, 24), f32)
    pushed = over_groups(slots // GROUP, push, zero)
    pushed = jnp.transpose(pushed)
    pushed = (pushed[:8] + pushed[8:16] + pushed[16:]) * (1.0 / neighbor_norm)
    own = own - pushed[:, :atoms]
    velocities, mass = facts[1:4], facts[8:9]
    pieces[0:3] = (own * facts[7:8])[:3]
    blocks = ((ret_minus, slab_rows), (ret_plus, slab_rows), (ret_prev, sub_rows), (ret_next, sub_rows))
    start = atoms
    ghost_lines = [[0.0] * 3 for _ in range(3)]
    for i, (ref, count) in enumerate(blocks):
        told = ref[count : count + 8, :count]
        force = -pushed[:, start : start + count]
        start += count
        for a in range(3):
            for b in range(3):
                ghost_lines[a][b] = ghost_lines[a][b] + told[a + 1 : a + 2] * force[b : b + 1]
        scaled = force * told[7:8]
        top = scaled.astype(bf16).astype(f32)
        rest = scaled - top
        mid = rest.astype(bf16).astype(f32)
        split = jnp.concatenate([top, mid, rest - mid], axis=0).astype(bf16)
        place = (iota((atoms, count), 0) == told[0:1].astype(jnp.int32)).astype(bf16)
        spread = dot_nt(split, place)
        pieces[3 * i + 3 : 3 * i + 6] = (spread[:8] + spread[8:16] + spread[16:])[:3]
    came[...] = jnp.zeros_like(came)
    for i, (ref, count) in enumerate(blocks):
        came[:, i * moves : (i + 1) * moves] = ref[count : count + 8, atoms : atoms + moves]

    def line(a, b):
        start = velocities[a : a + 1] * velocities[b : b + 1] * mass
        mixed = velocities[a : a + 1] * own[b : b + 1] + velocities[b : b + 1] * own[a : a + 1]
        return start + time_step * mixed - jnp.sum(u[a] * geo[4] * gradient[b], axis=0, keepdims=True)

    lines = jnp.concatenate([line(a, b) for a in range(3) for b in range(3)] + [jnp.zeros((7, atoms), f32)], axis=0)
    ghosts = [time_step * (ghost_lines[a][b] + ghost_lines[b][a]) for a in range(3) for b in range(3)]
    ghosts = jnp.concatenate(ghosts + [jnp.zeros((7, slab_rows), f32)], axis=0)
    summed = jnp.sum(lines, axis=1, keepdims=True) + jnp.sum(ghosts, axis=1, keepdims=True)
    row = jnp.zeros((1, atoms), f32)
    for i in range(9):
        row = jnp.where(iota((1, atoms), 1) == i, summed[i : i + 1], row)
    pieces[15:16] = row
    for i in range(everyone.shape[0]):
        everyone[i] = pieces[...]


def determinant(m):
    return (
        m[0][0] * (m[1][1] * m[2][2] - m[1][2] * m[2][1])
        - m[0][1] * (m[1][0] * m[2][2] - m[1][2] * m[2][0])
        + m[0][2] * (m[1][0] * m[2][1] - m[1][1] * m[2][0])
    )


def inverse(m):
    whole = determinant(m)
    return [
        [
            (
                m[(j + 1) % 3][(i + 1) % 3] * m[(j + 2) % 3][(i + 2) % 3]
                - m[(j + 1) % 3][(i + 2) % 3] * m[(j + 2) % 3][(i + 1) % 3]
            )
            / whole
            for j in range(3)
        ]
        for i in range(3)
    ]


def fifth_kernel(
    pieces, own_facts, came, box, box_speed,
    forces_out, velocities_out, positions_out, arrivals, new_box, new_box_speed,
    whole, *, atoms_all, slab_count, sub_count,
):
    atoms = own_facts.shape[1]
    velocities, positions = own_facts[1:4], own_facts[4:7]
    devices = slab_count * sub_count
    sub = lax.rem(iota((devices, atoms), 0), sub_count)

    def row_of_all(r):
        return pieces[:, r, :]

    def piece(i, a):
        return row_of_all(3 * i + a)

    def moved(x, step):
        return pltpu.roll(x, (-step) % devices, 0)

    for a in range(3):
        total = piece(0, a) + moved(piece(1, a), sub_count) + moved(piece(2, a), -sub_count)
        x = piece(3, a)
        total = total + jnp.where(sub == sub_count - 1, moved(x, 1 - sub_count), moved(x, 1))
        x = piece(4, a)
        whole[a] = total + jnp.where(sub == 0, moved(x, sub_count - 1), moved(x, -1))
    squares = {}
    for a in range(3):
        for b in range(a, 3):
            squares[a, b] = jnp.sum(whole[a] * whole[b], axis=0, keepdims=True)
    order = list(squares)
    squares = jnp.concatenate([squares[k] for k in order] + [jnp.zeros((2, atoms), f32)], axis=0)
    squares = jnp.sum(squares, axis=1, keepdims=True)
    rest = jnp.sum(row_of_all(15), axis=0, keepdims=True)
    stress = [[None] * 3 for _ in range(3)]
    for i in range(3):
        for j in range(3):
            at = order.index((min(i, j), max(i, j)))
            stress[i][j] = rest[:, 3 * i + j : 3 * i + j + 1] + (time_step * time_step) * squares[at : at + 1]
    slab_at, sub_at = lax.axis_index("slab"), lax.axis_index("sub")
    mine = slab_at * sub_count + sub_at
    root, mass = own_facts[7:8], own_facts[8:9]
    for a in range(3):
        force = whole[a, pl.ds(mine, 1), :] * (mass * root)
        forces_out[a : a + 1, :] = force
        velocities_out[a : a + 1, :] = velocities[a : a + 1, :] + time_step * force / mass
    lane, row = iota((8, atoms), 1), iota((8, atoms), 0)
    facts = came[...]
    index = jnp.broadcast_to(facts[0:1].astype(jnp.int32), (8, atoms))
    count = arrivals.shape[1] // 4
    picked = jnp.zeros((8, atoms), f32)
    for i, (slab_step, sub_step) in enumerate(((-1, 0), (1, 0), (0, -1), (0, 1))):
        slab = lax.rem(slab_at + (slab_step + slab_count), slab_count)
        source = slab * sub_count + lax.rem(sub_at + (sub_step + sub_count), sub_count)
        force = [whole[a, pl.ds(source, 1), :] for a in range(3)]
        force = jnp.where(row == 0, force[0], jnp.where(row == 1, force[1], force[2]))
        found = jnp.take_along_axis(force, index, axis=1)
        picked = jnp.where((lane >= i * count) & (lane < (i + 1) * count), found, picked)
    speeds = [facts[1 + a : 2 + a] + time_step * picked[a : a + 1] * facts[7:8] for a in range(3)]

    def spread(value):
        return jnp.full((1, atoms), value, f32)

    old = [[spread(box[i, j]) for j in range(3)] for i in range(3)]
    volume = determinant(old)
    old_inverse = inverse(old)
    for i in range(3):
        stress[i][i] = stress[i][i] - outside_pressure * volume
    fresh = [[None] * 3 for _ in range(3)]
    for i in range(3):
        for j in range(3):
            push = stress[i][0] * old_inverse[j][0] + stress[i][1] * old_inverse[j][1] + stress[i][2] * old_inverse[j][2]
            speed = spread(box_speed[i, j]) + time_step * push / (box_mass * atoms_all)
            fresh[i][j] = old[i][j] + time_step * speed
            new_box_speed[i : i + 1, j : j + 1] = speed[:, :1]
            new_box[i : i + 1, j : j + 1] = fresh[i][j][:, :1]
    new_inverse = inverse(fresh)
    for i in range(3):
        move = sum(new_inverse[i][j] * velocities_out[j : j + 1, :] for j in range(3))
        positions_out[i : i + 1, :] = positions[i : i + 1, :] + time_step * move
    for i in range(3):
        move = sum(new_inverse[i][j] * speeds[j] for j in range(3))
        arrivals[i : i + 1, :] = (facts[4 + i : 5 + i] + time_step * move)[:, : 4 * count]
        arrivals[3 + i : 4 + i, :] = speeds[i][:, : 4 * count]


VM = pl.BlockSpec(memory_space=pltpu.VMEM)
HB = pl.BlockSpec(memory_space=pltpu.HBM)
SM = pl.BlockSpec(memory_space=pltpu.SMEM)


def shape(*dims, dtype=f32):
    return jax.ShapeDtypeStruct(dims, dtype)


def call(kernel, outs, scalar_inputs=(), far_inputs=False, far_outputs=(), scratch=(), flops=0, vmem=16, name=None):
    def run(*args):
        moved = sum(math.prod(x.shape) * x.dtype.itemsize for x in list(args) + list(outs))
        return pl.pallas_call(
            kernel,
            out_shape=tuple(outs),
            in_specs=[HB if far_inputs else SM if i in scalar_inputs else VM for i in range(len(args))],
            out_specs=tuple(HB if i in far_outputs else VM for i in range(len(outs))),
            scratch_shapes=list(scratch),
            compiler_params=pltpu.CompilerParams(vmem_limit_bytes=vmem * 1024 * 1024),
            cost_estimate=pl.CostEstimate(flops=flops, bytes_accessed=moved, transcendentals=0),
            name=name,
        )(*args)

    return run


def body(
    positions, velocities, species, ghost_species, neighbours, slot_mask, edge_vectors, send_slab, send_sub, migrants,
    embedding, energy_shift, masses, radial_one_in, radial_one_mid, radial_one_out, node_one,
    radial_two_in, radial_two_mid, radial_two_out, node_two, readout_linear, readout_hidden, readout_out,
    box_matrix, box_velocity,
):
    slots, atoms = neighbours.shape
    width = node_one.shape[1]
    hidden = radial_one_mid.shape[1]
    depth = 4 * width
    ghost_slab, ghost_sub = send_slab.shape[1], send_sub.shape[1]
    extended = atoms + 2 * ghost_slab + 2 * ghost_sub
    edges = slots * atoms
    devices = lax.axis_size("slab") * lax.axis_size("sub")
    species_row = species.reshape(1, atoms)
    ghost_row = ghost_species.reshape(1, -1)
    linear_row = readout_linear.reshape(1, -1)
    out_row = readout_out.reshape(1, -1)
    radial_one_in, radial_one_out = jnp.transpose(radial_one_in), jnp.transpose(radial_one_out)
    radial_two_in, radial_two_out = jnp.transpose(radial_two_in), jnp.transpose(radial_two_out)

    first_inputs = (
        edge_vectors, slot_mask, neighbours, species_row, ghost_row, embedding,
        radial_one_in, radial_one_mid, radial_one_out, node_one, send_slab, send_sub,
        velocities, positions, migrants, masses.reshape(1, -1), energy_shift.reshape(1, -1),
        readout_hidden, linear_row, out_row, radial_two_in, radial_two_mid, radial_two_out, node_two,
    )
    packed_rows = (
        8 * width + 6 * packed_step(slots) + FACTS + 6 * hidden + radial_two_in.shape[0] + packed_step(slots)
        + readout_hidden.shape[0] + 8 + 2 * radial_one_in.shape[0] * packed_step(slots)
    )
    kinds, sums, packed, to_minus, to_plus, to_prev, to_next = call(
        first_kernel,
        (
            shape(slots, atoms, dtype=jnp.int32),
            shape(5, width, atoms),
            shape(packed_rows, atoms),
            shape(ghost_slab, depth),
            shape(ghost_slab, depth),
            shape(ghost_sub, depth),
            shape(ghost_sub, depth),
        ),
        far_inputs=True,
        far_outputs=(1, 2),
        scratch=(
            pltpu.VMEM((6, slots, atoms), f32),
            pltpu.VMEM((2 * radial_one_in.shape[0], slots, atoms), f32),
            pltpu.VMEM((packed_rows, atoms), f32),
            pltpu.VMEM((5, width, atoms), f32),
        )
        + tuple(pltpu.VMEM(x.shape, x.dtype) for x in first_inputs)
        + (pltpu.SemaphoreType.DMA((FIRST_INPUTS,)), pltpu.SemaphoreType.DMA((4,))),
        flops=6 * edges * 26000,
        vmem=56,
        name="layer_one",
    )(
        *first_inputs
    )
    from_minus, from_plus, from_prev, from_next = trade(to_minus, to_plus, to_prev, to_next)

    def radial(*refs):
        radial_kernel(
            *refs,
            slab_rows=ghost_slab,
            sub_rows=ghost_sub,
            moves=migrants.shape[1],
            basis_count=radial_two_in.shape[0],
        )

    (
        weights_all, slopes, onehot, outer, forward_high, forward_low, backward_high, backward_low,
        geo, own_table, scalars, extras, facts, heads, waves,
    ) = call(
        radial,
        (
            shape(depth, edges),
            shape(3 * hidden, edges, dtype=bf16),
            shape(2 * extended, edges, dtype=bf16),
            shape(depth, 3 * hidden, dtype=bf16),
            shape(width, 3 * width, dtype=bf16),
            shape(width, 3 * width, dtype=bf16),
            shape(3 * width, width, dtype=bf16),
            shape(3 * width, width, dtype=bf16),
            shape(6, slots, atoms),
            shape(depth, 2 * atoms, dtype=bf16),
            shape(width, atoms),
            shape(4, 8, 2 * atoms),
            shape(FACTS, atoms),
            shape(readout_hidden.shape[0] + 8, atoms),
            shape(2 * radial_two_in.shape[0], slots, atoms),
        ),
        flops=12 * edges * 10000,
        vmem=12,
        name="radial_two",
    )(
        packed,
    )

    energy, scalar_pull, picked_all, pulls, own_pull, back_minus, back_plus, back_prev, back_next = call(
        second_kernel,
        (
            shape(1, atoms),
            shape(width, atoms),
            shape(depth, edges),
            shape(4, width, atoms),
            shape(atoms, depth),
            shape(ghost_slab + 8, depth),
            shape(ghost_slab + 8, depth),
            shape(ghost_sub + 8, depth),
            shape(ghost_sub + 8, depth),
        ),
        scratch=(pltpu.VMEM((depth, 2 * extended), bf16), pltpu.VMEM((extended, depth), f32)),
        flops=4 * edges * depth * extended * 2,
        vmem=28,
        name="layer_two",
    )(
        geo, own_table, from_minus, from_plus, from_prev, from_next, scalars, extras,
        weights_all, onehot, forward_high, forward_low, backward_high, backward_low, heads,
    )
    ret_minus, ret_plus, ret_prev, ret_next = trade(back_minus, back_plus, back_prev, back_next)
    (geo_pull,) = call(
        edge_kernel,
        (shape(4, slots, atoms),),
        flops=edges * depth * 400,
        vmem=16,
        name="edge_two",
    )(geo, slopes, outer, picked_all, weights_all, pulls)
    scalar_slope, vector_slope, vector_value, turned_high, turned_low, linear = call(
        slope_kernel,
        (
            shape(width, edges),
            shape(width, edges),
            shape(width, edges),
            shape(7 * width, width, dtype=bf16),
            shape(7 * width, width, dtype=bf16),
            shape(width, atoms),
        ),
        flops=12 * edges * 20000,
        vmem=12,
        name="radial_one",
    )(
        geo, waves, kinds, scalar_pull, embedding, radial_one_in, radial_one_mid, radial_one_out, node_one, node_two, linear_row,
    )


    def back(*refs):
        third_kernel(*refs, moves=migrants.shape[1], slab_rows=ghost_slab, sub_rows=ghost_sub)

    everyone, came = call(
        back,
        (shape(devices, 16, atoms), shape(8, atoms)),
        scratch=(
            pltpu.VMEM((16, atoms), f32),
            pltpu.VMEM((4, width, atoms), f32),
            pltpu.VMEM((4, slots, atoms), f32),
        ),
        flops=6 * edges * 1000,
        vmem=12,
        name="layer_one_back",
    )(
        facts, geo, sums, geo_pull, scalar_pull, own_pull, ret_minus, ret_plus, ret_prev, ret_next,
        onehot, scalar_slope, vector_slope, vector_value, turned_high, turned_low, linear,
    )
    everyone = lax.all_to_all(everyone, ("slab", "sub"), 0, 0, tiled=True)

    def last(*refs):
        fifth_kernel(
            *refs, atoms_all=atoms * devices, slab_count=lax.axis_size("slab"), sub_count=lax.axis_size("sub")
        )

    forces, new_velocities, new_positions, arrivals, new_box, new_box_velocity = call(
        last,
        (
            shape(3, atoms), shape(3, atoms), shape(3, atoms), shape(6, 4 * migrants.shape[1]),
            shape(3, 3), shape(3, 3),
        ),
        scalar_inputs=(3, 4),
        scratch=(pltpu.VMEM((3, devices, atoms), f32),),
        flops=1000000,
        vmem=8,
        name="box",
    )(everyone, facts, came, box_matrix, box_velocity)
    return energy.reshape(atoms), forces, new_velocities, new_positions, arrivals, new_box, new_box_velocity


def solution(mesh):
    split = ("slab", "sub")
    one, two, three, copied = P(split), P(None, split), P(None, None, split), P()
    placed = (two, two, one, one, two, two, three, two, two, two) + (copied,) * 16
    return jax.shard_map(
        body,
        mesh=mesh,
        in_specs=placed,
        out_specs=(one, two, two, two, two, copied, copied),
        check_vma=False,
    )
```

```python
import math

import jax
import jax.numpy as jnp
from jax import lax
from jax.experimental import pallas as pl
from jax.experimental.pallas import tpu as pltpu
from jax.sharding import PartitionSpec as P

cutoff = 5.0
neighbor_norm = 0.125
time_step = 0.5
outside_pressure = 0.5
box_mass = 0.125
highest = lax.Precision.HIGHEST
f32 = jnp.float32
bf16 = jnp.bfloat16
GROUP = 4


def shifted(block, axis, distance):
    count = lax.axis_size(axis)
    return lax.ppermute(block, axis, [((i - distance) % count, i) for i in range(count)])


def trade(to_minus, to_plus, to_prev, to_next):
    from_minus, from_plus = shifted(to_plus, "slab", 1), shifted(to_minus, "slab", -1)
    return from_minus, from_plus, shifted(to_next, "sub", 1), shifted(to_prev, "sub", -1)


def parts(x):
    high = x.astype(bf16)
    return high, (x - high.astype(f32)).astype(bf16)


def dot(a, b):
    return jnp.dot(a, b, preferred_element_type=f32)


def dot_nt(a, b):
    return lax.dot_general(a, b, (((1,), (1,)), ((), ())), preferred_element_type=f32)


def exact(a, b, dims=((1,), (0,))):
    return lax.dot_general(a, b, (dims, ((), ())), precision=highest, preferred_element_type=f32)


def product(weight, x):
    high, low = parts(x)
    return dot(weight[0], high) + dot(weight[0], low) + dot(weight[1], high)


def weight_stack(w):
    high = w.astype(bf16).astype(f32)
    return jnp.concatenate([high, high, w - high], axis=1).astype(bf16)


def weight_stack_t(w):
    high = w.astype(bf16).astype(f32)
    return jnp.transpose(jnp.concatenate([high, high, w - high], axis=0)).astype(bf16)


def value_stack(x):
    high, low = parts(x)
    return jnp.concatenate([high, low, high], axis=0)


def value_stack_small(x):
    high = x.astype(bf16).astype(f32)
    return jnp.concatenate([high, x - high, high], axis=0).astype(bf16)


def over_groups(count, step, carry):
    for i in range(count):
        carry = step(i, carry)
    return carry


def span_of(first, count):
    if isinstance(first, int):
        return pl.ds(first, count)
    return pl.ds(pl.multiple_of(first, count), count)


def iota(shape, axis):
    return lax.broadcasted_iota(jnp.int32, shape, axis)


def column(row):
    n = row.shape[1]
    return jnp.sum(jnp.where(iota((n, n), 0) == iota((n, n), 1), row, 0.0), axis=1, keepdims=True)


def sigmoid(x):
    return 0.5 + 0.5 * jnp.tanh(0.5 * x)


def basis(distance, inverse_distance, count):
    scaled = distance * (1.0 / cutoff)
    second = scaled * scaled
    fourth = second * second
    fifth = fourth * scaled
    sixth = fourth * second
    scale = math.sqrt(2.0 / cutoff)
    envelope = 1.0 + sixth * (-28.0 + scaled * (48.0 - 21.0 * scaled))
    front = scale * envelope * inverse_distance
    slope_envelope = fifth * (-168.0 + scaled * (336.0 - 168.0 * scaled)) * (1.0 / cutoff)
    slope_front = scale * inverse_distance * (slope_envelope - envelope * inverse_distance)
    angle = math.pi * scaled
    first_sine, first_cosine = jnp.sin(angle), jnp.cos(angle)
    sine, cosine = first_sine, first_cosine
    values, slopes = [], []
    for order in range(1, count + 1):
        if order > 1:
            sine, cosine = (
                sine * first_cosine + cosine * first_sine,
                cosine * first_cosine - sine * first_sine,
            )
        values.append(sine * front)
        slopes.append(sine * slope_front + cosine * (front * (order * math.pi / cutoff)))
    return values, slopes


def basis_group(waves, first, start, count):
    return jnp.concatenate([waves[start : start + count, first + j, :] for j in range(GROUP)], axis=1)


def hidden_values(value, inner, mid_a, mid_b):
    x = dot(inner, value_stack_small(value))
    for mid in (mid_a, mid_b, None):
        h = x * sigmoid(x)
        if mid is not None:
            x = dot(mid, value_stack(h))
    return h


def hidden_pairs(value, slope, inner, mid_a, mid_b):
    x, dx = dot(inner, value_stack_small(value)), dot(inner, value_stack_small(slope))
    for mid in (mid_a, mid_b, None):
        gate = sigmoid(x)
        h = x * gate
        dh = (gate + h * (1.0 - gate)) * dx
        if mid is not None:
            x, dx = dot(mid, value_stack(h)), dot(mid, value_stack(dh))
    return h, dh


def species_matrix(first_mixing, embedding):
    lifted = exact(first_mixing, embedding, ((1,), (1,)))
    high = lifted.astype(bf16).astype(f32)
    rest = lifted - high
    mid = rest.astype(bf16).astype(f32)
    return jnp.concatenate([high, mid, rest - mid], axis=1).astype(bf16)


def picked_group(lifted, geo, kinds, first, species_count):
    blocks = []
    for j in range(GROUP):
        kind = kinds[pl.ds(first + j, 1), :]
        weight = geo[3, pl.ds(first + j, 1), :]
        blocks.append(jnp.where(iota((species_count, kind.shape[1]), 0) == kind, weight, 0.0))
    block = jnp.concatenate(blocks, axis=1)
    return dot(lifted, jnp.concatenate([block, block, block], axis=0).astype(bf16))


def send_onehot(facts, first, slab_rows, sub_rows):
    atoms = facts.shape[1]
    lengths = (slab_rows, slab_rows, sub_rows, sub_rows)
    rows = [facts[first + 9 + i : first + 10 + i, :n] for i, n in enumerate(lengths)]
    rows = jnp.concatenate(rows, axis=1)
    return (iota((atoms, rows.shape[1]), 0).astype(f32) == rows).astype(f32)


FIRST_INPUTS = 24
FACTS = 16


def packed_step(slots):
    return -(-slots // 8) * 8


def first_kernel(
    *refs,
):
    count = FIRST_INPUTS
    buffers, ready, gone = refs[-count - 2 : -2], refs[-2], refs[-1]
    copies = [pltpu.make_async_copy(refs[i], buffers[i], ready.at[i]) for i in range(count)]
    for copy in copies:
        copy.start()
    (
        edges, mask, neighbours, species, ghosts, embedding, radial_in, radial_mid, radial_out, node_one,
        send_slab, send_sub, velocities, positions, migrants, masses, shifts,
        hidden_head, linear_head, out_head, next_in, next_mid, next_out, node_two,
    ) = buffers
    (
        kinds, far_sums, far_packed, to_minus, to_plus, to_prev, to_next,
        geo, waves, packed, sums,
    ) = refs[count : -count - 2]
    for copy in copies[:2]:
        copy.wait()
    slots, atoms = mask.shape
    width = node_one.shape[1]
    species_count, basis_count = embedding.shape[0], radial_in.shape[0]
    ex, ey, ez = edges[0], edges[1], edges[2]
    square = ex * ex + ey * ey + ez * ez
    distance = jnp.sqrt(square)
    inverse_distance = 1.0 / distance
    for a, e in enumerate((ex, ey, ez)):
        geo[a] = e * inverse_distance
    geo[3] = mask[...].astype(f32) * neighbor_norm
    geo[4] = distance
    geo[5] = inverse_distance
    base = 5 * width
    step = packed_step(slots)
    values, slopes = basis(distance, inverse_distance, radial_in.shape[0])
    for i, wave in enumerate(values + slopes):
        waves[i] = wave
    for a in range(6):
        packed[base + a * step : base + a * step + slots] = geo[a]
    for copy in copies[2:5]:
        copy.wait()
    ghost_row = ghosts[...]
    extra = -ghost_row.shape[1] % atoms
    if extra:
        ghost_row = jnp.concatenate([ghost_row, jnp.zeros((1, extra), jnp.int32)], axis=1)
    tables = [species[...]] + [ghost_row[:, i : i + atoms] for i in range(0, ghost_row.shape[1], atoms)]
    pad = -slots % 8
    rows = neighbours[...]
    if pad:
        rows = jnp.concatenate([rows, jnp.zeros((pad, atoms), jnp.int32)], axis=0)
    inner_index = lax.rem(rows, atoms)
    block_index = lax.div(rows, atoms)
    found = jnp.zeros_like(rows)
    for i, table in enumerate(tables):
        spread = jnp.broadcast_to(table, rows.shape)
        got = jnp.take_along_axis(spread, inner_index, axis=1)
        found = jnp.where(block_index == i, got, found)
    kinds[...] = found[:slots]

    for copy in copies[5:10]:
        copy.wait()
    inner = weight_stack_t(radial_in[...])
    mid_a, mid_b = weight_stack(radial_mid[0]), weight_stack(radial_mid[1])
    outer = weight_stack_t(radial_out[...])
    lifted = species_matrix(node_one[0], embedding[...])
    for copy in copies[10:]:
        copy.wait()
    mass = shift = jnp.zeros((1, atoms), f32)
    for i in range(masses.shape[1]):
        mass = jnp.where(species[...] == i, masses[:, i : i + 1], mass)
        shift = jnp.where(species[...] == i, shifts[:, i : i + 1], shift)
    facts = base + 6 * step
    packed[facts : facts + 1] = iota((1, atoms), 1).astype(f32)
    packed[facts + 1 : facts + 4] = velocities[...]
    packed[facts + 4 : facts + 7] = positions[...]
    packed[facts + 7 : facts + 8] = 1.0 / jnp.sqrt(mass)
    packed[facts + 8 : facts + 9] = mass
    packed[facts + 9 : facts + FACTS] = jnp.zeros((FACTS - 9, atoms), f32)
    for i, (lists, at) in enumerate(((send_slab, 1), (send_slab, 0), (send_sub, 1), (send_sub, 0))):
        packed[facts + 9 + i : facts + 10 + i, : lists.shape[1]] = lists[at : at + 1, :].astype(f32)
    count = migrants.shape[1]
    for i, at in enumerate((1, 0, 3, 2)):
        packed[facts + 13 : facts + 14, i * count : (i + 1) * count] = migrants[at : at + 1, :].astype(f32)
    inner_rows = next_mid.shape[1]
    start = facts + FACTS
    for i in range(3):
        packed[start : start + width] = node_two[i + 2]
        start += width
    for i in range(next_out.shape[1] // atoms):
        packed[start : start + inner_rows] = next_out[:, i * atoms : (i + 1) * atoms]
        start += inner_rows
    for i in range(2):
        packed[start : start + inner_rows, :inner_rows] = next_mid[i]
        start += inner_rows
    packed[start : start + next_in.shape[0], :inner_rows] = next_in[...]
    start += next_in.shape[0]
    packed[start : start + slots] = neighbours[...].astype(f32)
    start += step
    count = hidden_head.shape[0]
    packed[start : start + count] = hidden_head[...]
    packed[start + count : start + count + 1] = linear_head[...]
    packed[start + count + 1 : start + count + 2, : out_head.shape[1]] = out_head[...]
    packed[start + count + 2 : start + count + 3] = shift
    start += count + 8
    for i in range(waves.shape[0]):
        packed[start + i * step : start + i * step + slots] = waves[i]
    sums[...] = jnp.zeros_like(sums)

    def group(step, carry):
        first = step * GROUP
        value = basis_group(waves, first, 0, basis_count)
        h = hidden_values(value, inner, mid_a, mid_b)
        weights = dot(outer, value_stack(h))
        picked = picked_group(lifted, geo, kinds, first, species_count)
        totals = [0.0] * 4
        for j in range(GROUP):
            at = slice(j * atoms, (j + 1) * atoms)
            p = picked[:, at]
            totals[0] = totals[0] + weights[:width, at] * p
            q = weights[width:, at] * p
            for a in range(3):
                totals[a + 1] = totals[a + 1] + q * geo[a, pl.ds(first + j, 1), :]
        for a in range(4):
            sums[a] += totals[a]
        return carry

    over_groups(slots // GROUP, group, 0)

    early_sums = pltpu.make_async_copy(sums.at[:4], far_sums.at[:4], gone.at[2])
    early_sums.start()
    early = pltpu.make_async_copy(packed.at[base:], far_packed.at[base:], gone.at[0])
    early.start()
    own_onehot = (iota((species_count, atoms), 0) == species[...]).astype(f32)
    own = exact(embedding[...], own_onehot, ((0,), (0,)))
    scalar_sum = sums[0]
    vectors = [sums[1], sums[2], sums[3]]
    squares = vectors[0] * vectors[0] + vectors[1] * vectors[1] + vectors[2] * vectors[2]
    scalars = (
        own
        + product(parts(node_one[1]), scalar_sum)
        + product(parts(node_one[2]), scalar_sum * scalar_sum)
        + product(parts(node_one[3]), squares)
    )
    gate = product(parts(node_one[5]), scalar_sum)
    sums[4] = gate
    late_sums = pltpu.make_async_copy(sums.at[4:], far_sums.at[4:], gone.at[3])
    late_sums.start()
    turned = product(parts(node_one[4]), jnp.concatenate(vectors, axis=1))
    moved = turned + jnp.concatenate([gate * v for v in vectors], axis=1)
    packed[:width] = scalars
    x = product(parts(node_two[0]), scalars)
    y = product(parts(node_two[1]), moved)
    table = jnp.concatenate([x] + [y[:, a * atoms : (a + 1) * atoms] for a in range(3)], axis=0)
    packed[width : 5 * width] = table
    late = pltpu.make_async_copy(packed.at[:base], far_packed.at[:base], gone.at[1])
    late.start()
    pick = send_onehot(packed, facts, send_slab.shape[1], send_sub.shape[1]).astype(bf16)
    high, low = parts(table)
    sent = jnp.transpose(dot(high, pick) + dot(low, pick))
    slab_rows = send_slab.shape[1]
    to_plus[...] = sent[:slab_rows]
    to_minus[...] = sent[slab_rows : 2 * slab_rows]
    sub_rows = send_sub.shape[1]
    to_next[...] = sent[2 * slab_rows : 2 * slab_rows + sub_rows]
    to_prev[...] = sent[2 * slab_rows + sub_rows :]
    for copy in (early, late, early_sums, late_sums):
        copy.wait()


def radial_kernel(
    packed,
    weights_all, slopes, onehot, outer, fold_high, fold_low, back_high, back_low,
    geo, table, scalars, extras, facts, heads, waves, *, slab_rows, sub_rows, moves, basis_count,
):
    slots, atoms = geo.shape[1:]
    width = scalars.shape[0]
    depth = 4 * width
    inner_rows = slopes.shape[0] // 3
    scalars[...] = packed[:width]
    first_fact = 5 * width + 6 * packed_step(slots)
    start = first_fact + FACTS
    mixings = [packed[start + i * width : start + (i + 1) * width] for i in range(3)]
    start += 3 * width
    pieces = depth // atoms
    radial_out = [packed[start + i * inner_rows : start + (i + 1) * inner_rows] for i in range(pieces)]
    radial_out = jnp.concatenate(radial_out, axis=1)
    start += pieces * inner_rows
    radial_mid = [packed[start + i * inner_rows : start + (i + 1) * inner_rows, :inner_rows] for i in range(2)]
    start += 2 * inner_rows
    radial_in = packed[start : start + basis_count, :inner_rows]
    first_row = start + basis_count
    start = first_row + packed_step(slots)
    heads[...] = packed[start : start + heads.shape[0]]
    start += heads.shape[0]
    for i in range(2 * basis_count):
        waves[i] = packed[start + i * packed_step(slots) : start + i * packed_step(slots) + slots]
    table[:, :atoms], table[:, atoms:] = parts(packed[width : 5 * width])
    for a in range(6):
        start = 5 * width + a * packed_step(slots)
        geo[a] = packed[start : start + slots]
    facts[...] = packed[first_fact : first_fact + FACTS]
    listed = exact(facts[:8], send_onehot(facts, 0, slab_rows, sub_rows))
    moving = exact(facts[:8], (iota((atoms, 4 * moves), 0).astype(f32) == facts[13:14, : 4 * moves]).astype(f32))
    start = 0
    extras[...] = jnp.zeros_like(extras)
    for i, length in enumerate((slab_rows, slab_rows, sub_rows, sub_rows)):
        extras[i, :, :length] = listed[:, start : start + length]
        extras[i, :, atoms : atoms + moves] = moving[:, i * moves : (i + 1) * moves]
        start += length
    rows = onehot.shape[0] // 2
    outer[...] = weight_stack_t(radial_out)
    folded = product(parts(heads[: heads.shape[0] - 8]), jnp.concatenate(mixings, axis=1))
    fold_high[...], fold_low[...] = parts(folded)
    back_high[...], back_low[...] = parts(jnp.transpose(folded))
    inner = weight_stack_t(radial_in)
    mid_a, mid_b = weight_stack(radial_mid[0]), weight_stack(radial_mid[1])

    def group(step, carry):
        first = step * GROUP
        at = span_of(step * GROUP * atoms, GROUP * atoms)
        value, slope = (basis_group(waves, first, i * basis_count, basis_count) for i in range(2))
        h, dh = hidden_pairs(value, slope, inner, mid_a, mid_b)
        slopes[:, at] = value_stack(dh)
        blocks = []
        for j in range(GROUP):
            row = packed[first_row + first + j : first_row + first + j + 1]
            weight = geo[3, pl.ds(first + j, 1), :]
            row = row.astype(jnp.int32)
            blocks.append(jnp.where(iota((rows, atoms), 0) == row, weight, 0.0).astype(bf16))
        block = jnp.concatenate(blocks, axis=1)
        own, ghosts = block[:atoms], block[atoms:]
        onehot[:, at] = jnp.concatenate([own, own, ghosts, ghosts], axis=0)
        weights_all[:, at] = dot(outer[...], value_stack(h))
        return carry

    over_groups(slots // GROUP, group, 0)


def second_kernel(
    geo, own_table, from_minus, from_plus, from_prev, from_next, scalars, extras,
    weights_all, onehot, fold_high, fold_low, back_high, back_low, heads,
    energy, scalar_pull, picked_all, sums, own_pull, back_minus, back_plus, back_prev, back_next,
    table, pulled,
):
    slots, atoms = geo.shape[1], geo.shape[2]
    width = scalars.shape[0]
    depth = 4 * width
    ghosts = jnp.concatenate([from_minus[...], from_plus[...], from_prev[...], from_next[...]], axis=0)
    high = ghosts.astype(bf16).astype(f32)
    table[:, : 2 * atoms] = own_table[...]
    table[:, 2 * atoms :] = jnp.transpose(jnp.concatenate([high, ghosts - high], axis=0)).astype(bf16)
    ghost_rows = ghosts.shape[0]
    sums[...] = jnp.zeros_like(sums)

    def units(first, j):
        return [geo[a, pl.ds(first + j, 1), :] for a in range(3)]

    def forward(step, carry):
        first = step * GROUP
        at = span_of(step * GROUP * atoms, GROUP * atoms)
        picked = dot(table[...], onehot[:, at])
        picked_all[:, at] = picked
        totals = [0.0] * 4
        for j in range(GROUP):
            span = slice(j * atoms, (j + 1) * atoms)
            here = span_of((step * GROUP + j) * atoms, atoms)
            p = [picked[a * width : (a + 1) * width, span] for a in range(4)]
            r = [weights_all[a * width : (a + 1) * width, here] for a in range(4)]
            u = units(first, j)
            along = p[1] * u[0] + p[2] * u[1] + p[3] * u[2]
            totals[0] = totals[0] + (r[0] * p[0] + r[3] * along)
            q = r[1] * p[0]
            for a in range(3):
                totals[a + 1] = totals[a + 1] + (q * u[a] + r[2] * p[a + 1])
        for a in range(4):
            sums[a] += totals[a]
        return carry

    over_groups(slots // GROUP, forward, 0)

    scalar_sum = sums[0]
    vectors = [sums[1], sums[2], sums[3]]
    squares = vectors[0] * vectors[0] + vectors[1] * vectors[1] + vectors[2] * vectors[2]
    mixed = jnp.concatenate([scalar_sum, scalar_sum * scalar_sum, squares], axis=0)
    units_out = heads.shape[0] - 8
    readout_hidden = heads[:units_out]
    readout_linear, readout_out = heads[units_out : units_out + 1], heads[units_out + 1 : units_out + 2, :units_out]
    hidden_in = product(parts(readout_hidden), scalars[...]) + product((fold_high[...], fold_low[...]), mixed)
    hidden_gate = sigmoid(hidden_in)
    hidden = hidden_in * hidden_gate
    shift = heads[units_out + 2 : units_out + 3]
    energy[...] = shift + exact(readout_linear, scalars[...]) + exact(readout_out, hidden)
    hidden_pull = column(readout_out) * (hidden_gate + hidden * (1.0 - hidden_gate))
    scalar_pull[...] = exact(readout_hidden, hidden_pull, ((0,), (0,)))
    spread = product((back_high[...], back_low[...]), hidden_pull)
    double = 2.0 * spread[2 * width :]
    sums[0] = spread[:width] + 2.0 * scalar_sum * spread[width : 2 * width]
    for a in range(3):
        sums[a + 1] = vectors[a] * double
    pulled[...] = jnp.zeros_like(pulled)

    def backward(step, carry):
        first = step * GROUP
        at = span_of(step * GROUP * atoms, GROUP * atoms)
        highs, lows = [], []
        for j in range(GROUP):
            here = span_of((step * GROUP + j) * atoms, atoms)
            r = [weights_all[a * width : (a + 1) * width, here] for a in range(4)]
            u = units(first, j)
            ga = [sums[a] for a in range(4)]
            flow = ga[1] * u[0] + ga[2] * u[1] + ga[3] * u[2]
            pull = r[3] * ga[0]
            given = [r[0] * ga[0] + r[1] * flow] + [pull * u[a] + r[2] * ga[a + 1] for a in range(3)]
            high, low = parts(jnp.concatenate(given, axis=0))
            highs.append(high)
            lows.append(low)
        split = jnp.concatenate(highs + lows, axis=1)
        chosen = jnp.concatenate([onehot[:atoms, at], onehot[2 * atoms : 2 * atoms + ghost_rows, at]], axis=0)
        pulled[...] += dot_nt(jnp.concatenate([chosen, chosen], axis=1), split)
        return carry

    over_groups(slots // GROUP, backward, 0)
    own_pull[...] = pulled[:atoms]
    start = atoms
    fill = jnp.zeros((8, depth - extras.shape[2]), f32)
    for out, which in ((back_minus, 1), (back_plus, 0), (back_prev, 3), (back_next, 2)):
        count = out.shape[0] - 8
        out[:count] = pulled[start : start + count]
        out[count:] = jnp.concatenate([extras[which], fill], axis=1)
        start += count


def window_kernel(
    slopes, outer_two, picked_all, weights_all, sums,
    geo, waves, kinds, scalar_pull, embedding, radial_in, radial_mid, radial_out, node_one, node_two, readout_linear,
    geo_pull, scalar_slope, vector_slope, vector_value, turned_high, turned_low, base,
):
    slots, atoms = kinds.shape
    width = node_one.shape[1]
    species_count, basis_count = embedding.shape[0], radial_in.shape[0]
    inner = weight_stack_t(radial_in[...])
    mid_a, mid_b = weight_stack(radial_mid[0]), weight_stack(radial_mid[1])
    outer = weight_stack_t(radial_out[...])
    lifted = species_matrix(node_one[0], embedding[...])
    scalar_mixing = jnp.concatenate([jnp.transpose(node_one[i]) for i in (1, 2, 3)], axis=0)
    base[...] = column(readout_linear[...]) + scalar_pull[...]
    turned = [scalar_mixing] + [jnp.transpose(m) for m in (node_two[1], node_one[4], node_one[5], node_two[0])]
    turned_high[...], turned_low[...] = parts(jnp.concatenate(turned, axis=0))

    def group(step, carry):
        first = step * GROUP
        at = span_of(step * GROUP * atoms, GROUP * atoms)
        value, slope = (basis_group(waves, first, i * basis_count, basis_count) for i in range(2))
        h, dh = hidden_pairs(value, slope, inner, mid_a, mid_b)
        picked = picked_group(lifted, geo, kinds, first, species_count)
        weights_slope = dot(outer, value_stack(dh))
        scalar_slope[:, at] = weights_slope[:width] * picked
        vector_slope[:, at] = weights_slope[width:] * picked
        vector_value[:, at] = dot(outer[width:], value_stack(h)) * picked
        return carry

    def edge_group(step, carry):
        first = step * GROUP
        slope = dot(outer_two[...], slopes[:, span_of(step * GROUP * atoms, GROUP * atoms)])
        for j in range(GROUP):
            span = slice(j * atoms, (j + 1) * atoms)
            here = span_of((step * GROUP + j) * atoms, atoms)
            p = [picked_all[a * width : (a + 1) * width, here] for a in range(4)]
            r = [weights_all[a * width : (a + 1) * width, here] for a in (1, 3)]
            s = [slope[a * width : (a + 1) * width, span] for a in range(4)]
            u = [geo[a, pl.ds(first + j, 1), :] for a in range(3)]
            ga = [sums[a] for a in range(4)]
            along = p[1] * u[0] + p[2] * u[1] + p[3] * u[2]
            flow = ga[1] * u[0] + ga[2] * u[1] + ga[3] * u[2]
            cross = p[1] * ga[1] + p[2] * ga[2] + p[3] * ga[3]
            stretch = p[0] * (s[0] * ga[0] + s[1] * flow) + s[2] * cross + s[3] * (along * ga[0])
            geo_pull[0, pl.ds(first + j, 1), :] = jnp.sum(stretch, axis=0, keepdims=True)
            lean = r[0] * p[0]
            pull = r[1] * ga[0]
            for a in range(3):
                turn = lean * ga[a + 1] + pull * p[a + 1]
                geo_pull[a + 1, pl.ds(first + j, 1), :] = jnp.sum(turn, axis=0, keepdims=True)
        return carry

    for step in range(slots // GROUP):
        group(step, 0)
        edge_group(step, 0)


def third_kernel(
    facts, geo, sums, geo_pull, own_pull, ret_minus, ret_plus, ret_prev, ret_next,
    onehot, scalar_slope, vector_slope, vector_value, turned_high, turned_low, base,
    everyone, came,
    pieces, pulls, flat, *, moves, slab_rows, sub_rows,
):
    slots, atoms = geo.shape[1], geo.shape[2]
    width = sums.shape[1]
    pick = send_onehot(facts, 0, slab_rows, sub_rows).astype(bf16)
    returned = jnp.concatenate(
        [ret_plus[:slab_rows], ret_minus[:slab_rows], ret_next[:sub_rows], ret_prev[:sub_rows]], axis=0
    )
    high, low = parts(returned)
    total = jnp.transpose(own_pull[...] + dot(pick, high) + dot(pick, low))
    x_pull = total[:width]
    y_pull = jnp.concatenate([total[a * width : (a + 1) * width] for a in (1, 2, 3)], axis=1)

    def turned(i, count=1):
        at = slice(i * width, (i + count) * width)
        return turned_high[at, :], turned_low[at, :]

    moved = product(turned(3), y_pull)
    gv = [moved[:, a * atoms : (a + 1) * atoms] for a in range(3)]
    scalar_sum, gate = sums[0], sums[4]
    vectors = [sums[1], sums[2], sums[3]]
    scalars = product(turned(6), x_pull) + base[...]
    spread = product(turned(0, 3), scalars)
    mixed = product(turned(4), moved)
    gated = product(turned(5), gv[0] * vectors[0] + gv[1] * vectors[1] + gv[2] * vectors[2])
    pulls[0] = spread[:width] + 2.0 * scalar_sum * spread[width : 2 * width] + gated
    double = 2.0 * spread[2 * width :]
    for a in range(3):
        pulls[a + 1] = vectors[a] * double + mixed[:, a * atoms : (a + 1) * atoms] + gate * gv[a]

    def contract(step, carry):
        first = step * GROUP
        for j in range(GROUP):
            here = span_of((step * GROUP + j) * atoms, atoms)
            row = pl.ds(first + j, 1)
            ga = [pulls[a] for a in range(4)]
            u = [geo[a, row, :] for a in range(3)]
            flow = ga[1] * u[0] + ga[2] * u[1] + ga[3] * u[2]
            stretch = scalar_slope[:, here] * ga[0] + vector_slope[:, here] * flow
            value = vector_value[:, here]
            flat[0, row, :] = jnp.sum(stretch, axis=0, keepdims=True)
            for a in range(3):
                flat[a + 1, row, :] = jnp.sum(value * ga[a + 1], axis=0, keepdims=True)
        return carry

    over_groups(slots // GROUP, contract, 0)
    stretch = flat[0] + geo_pull[0]
    turn = [flat[a + 1] + geo_pull[a + 1] for a in range(3)]
    u = [geo[a] for a in range(3)]
    inner = turn[0] * u[0] + turn[1] * u[1] + turn[2] * u[2]
    gradient = [stretch * u[a] + (turn[a] - inner * u[a]) * geo[5] for a in range(3)]
    at_row = iota((8, atoms), 0)
    own = jnp.zeros((8, atoms), f32)
    for a in range(3):
        flat[a] = gradient[a]
        own = jnp.where(at_row == a, jnp.sum(gradient[a], axis=0, keepdims=True), own)

    def push(step, carry):
        blocks = []
        for j in range(GROUP):
            row = pl.ds(step * GROUP + j, 1)
            block = jnp.where(at_row == 0, flat[0, row, :], jnp.where(at_row == 1, flat[1, row, :], flat[2, row, :]))
            blocks.append(block)
        block = jnp.concatenate(blocks, axis=1)
        top = block.astype(bf16).astype(f32)
        rest = block - top
        mid = rest.astype(bf16).astype(f32)
        split = jnp.concatenate([top, mid, rest - mid], axis=0).astype(bf16)
        at = span_of(step * GROUP * atoms, GROUP * atoms)
        chosen = jnp.concatenate([onehot[:atoms, at], onehot[2 * atoms : 2 * atoms + ghost_rows, at]], axis=0)
        return carry + dot_nt(chosen, split)

    ghost_rows = onehot.shape[0] // 2 - atoms
    zero = jnp.zeros((onehot.shape[0] // 2, 24), f32)
    pushed = over_groups(slots // GROUP, push, zero)
    pushed = jnp.transpose(pushed)
    pushed = (pushed[:8] + pushed[8:16] + pushed[16:]) * (1.0 / neighbor_norm)
    own = own - pushed[:, :atoms]
    velocities, mass = facts[1:4], facts[8:9]
    pieces[0:3] = (own * facts[7:8])[:3]
    blocks = ((ret_minus, slab_rows), (ret_plus, slab_rows), (ret_prev, sub_rows), (ret_next, sub_rows))
    start = atoms
    ghost_lines = [[0.0] * 3 for _ in range(3)]
    for i, (ref, count) in enumerate(blocks):
        told = ref[count : count + 8, :count]
        force = -pushed[:, start : start + count]
        start += count
        for a in range(3):
            for b in range(3):
                ghost_lines[a][b] = ghost_lines[a][b] + told[a + 1 : a + 2] * force[b : b + 1]
        scaled = force * told[7:8]
        top = scaled.astype(bf16).astype(f32)
        rest = scaled - top
        mid = rest.astype(bf16).astype(f32)
        split = jnp.concatenate([top, mid, rest - mid], axis=0).astype(bf16)
        place = (iota((atoms, count), 0) == told[0:1].astype(jnp.int32)).astype(bf16)
        spread = dot_nt(split, place)
        pieces[3 * i + 3 : 3 * i + 6] = (spread[:8] + spread[8:16] + spread[16:])[:3]
    came[...] = jnp.zeros_like(came)
    for i, (ref, count) in enumerate(blocks):
        came[:, i * moves : (i + 1) * moves] = ref[count : count + 8, atoms : atoms + moves]

    def line(a, b):
        start = velocities[a : a + 1] * velocities[b : b + 1] * mass
        mixed = velocities[a : a + 1] * own[b : b + 1] + velocities[b : b + 1] * own[a : a + 1]
        return start + time_step * mixed - jnp.sum(u[a] * geo[4] * gradient[b], axis=0, keepdims=True)

    lines = jnp.concatenate([line(a, b) for a in range(3) for b in range(3)] + [jnp.zeros((7, atoms), f32)], axis=0)
    ghosts = [time_step * (ghost_lines[a][b] + ghost_lines[b][a]) for a in range(3) for b in range(3)]
    ghosts = jnp.concatenate(ghosts + [jnp.zeros((7, slab_rows), f32)], axis=0)
    summed = jnp.sum(lines, axis=1, keepdims=True) + jnp.sum(ghosts, axis=1, keepdims=True)
    row = jnp.zeros((1, atoms), f32)
    for i in range(9):
        row = jnp.where(iota((1, atoms), 1) == i, summed[i : i + 1], row)
    pieces[15:16] = row
    for i in range(everyone.shape[0]):
        everyone[i] = pieces[...]


def determinant(m):
    return (
        m[0][0] * (m[1][1] * m[2][2] - m[1][2] * m[2][1])
        - m[0][1] * (m[1][0] * m[2][2] - m[1][2] * m[2][0])
        + m[0][2] * (m[1][0] * m[2][1] - m[1][1] * m[2][0])
    )


def inverse(m):
    whole = determinant(m)
    return [
        [
            (
                m[(j + 1) % 3][(i + 1) % 3] * m[(j + 2) % 3][(i + 2) % 3]
                - m[(j + 1) % 3][(i + 2) % 3] * m[(j + 2) % 3][(i + 1) % 3]
            )
            / whole
            for j in range(3)
        ]
        for i in range(3)
    ]


def fifth_kernel(
    pieces, own_facts, came, box, box_speed,
    forces_out, velocities_out, positions_out, arrivals, new_box, new_box_speed,
    whole, *, atoms_all, slab_count, sub_count,
):
    atoms = own_facts.shape[1]
    velocities, positions = own_facts[1:4], own_facts[4:7]
    devices = slab_count * sub_count
    sub = lax.rem(iota((devices, atoms), 0), sub_count)

    def row_of_all(r):
        return pieces[:, r, :]

    def piece(i, a):
        return row_of_all(3 * i + a)

    def moved(x, step):
        return pltpu.roll(x, (-step) % devices, 0)

    for a in range(3):
        total = piece(0, a) + moved(piece(1, a), sub_count) + moved(piece(2, a), -sub_count)
        x = piece(3, a)
        total = total + jnp.where(sub == sub_count - 1, moved(x, 1 - sub_count), moved(x, 1))
        x = piece(4, a)
        whole[a] = total + jnp.where(sub == 0, moved(x, sub_count - 1), moved(x, -1))
    squares = {}
    for a in range(3):
        for b in range(a, 3):
            squares[a, b] = jnp.sum(whole[a] * whole[b], axis=0, keepdims=True)
    order = list(squares)
    squares = jnp.concatenate([squares[k] for k in order] + [jnp.zeros((2, atoms), f32)], axis=0)
    squares = jnp.sum(squares, axis=1, keepdims=True)
    rest = jnp.sum(row_of_all(15), axis=0, keepdims=True)
    stress = [[None] * 3 for _ in range(3)]
    for i in range(3):
        for j in range(3):
            at = order.index((min(i, j), max(i, j)))
            stress[i][j] = rest[:, 3 * i + j : 3 * i + j + 1] + (time_step * time_step) * squares[at : at + 1]
    slab_at, sub_at = lax.axis_index("slab"), lax.axis_index("sub")
    mine = slab_at * sub_count + sub_at
    root, mass = own_facts[7:8], own_facts[8:9]
    for a in range(3):
        force = whole[a, pl.ds(mine, 1), :] * (mass * root)
        forces_out[a : a + 1, :] = force
        velocities_out[a : a + 1, :] = velocities[a : a + 1, :] + time_step * force / mass
    lane, row = iota((8, atoms), 1), iota((8, atoms), 0)
    facts = came[...]
    index = jnp.broadcast_to(facts[0:1].astype(jnp.int32), (8, atoms))
    count = arrivals.shape[1] // 4
    picked = jnp.zeros((8, atoms), f32)
    for i, (slab_step, sub_step) in enumerate(((-1, 0), (1, 0), (0, -1), (0, 1))):
        slab = lax.rem(slab_at + (slab_step + slab_count), slab_count)
        source = slab * sub_count + lax.rem(sub_at + (sub_step + sub_count), sub_count)
        force = [whole[a, pl.ds(source, 1), :] for a in range(3)]
        force = jnp.where(row == 0, force[0], jnp.where(row == 1, force[1], force[2]))
        found = jnp.take_along_axis(force, index, axis=1)
        picked = jnp.where((lane >= i * count) & (lane < (i + 1) * count), found, picked)
    speeds = [facts[1 + a : 2 + a] + time_step * picked[a : a + 1] * facts[7:8] for a in range(3)]

    def spread(value):
        return jnp.full((1, atoms), value, f32)

    old = [[spread(box[i, j]) for j in range(3)] for i in range(3)]
    volume = determinant(old)
    old_inverse = inverse(old)
    for i in range(3):
        stress[i][i] = stress[i][i] - outside_pressure * volume
    fresh = [[None] * 3 for _ in range(3)]
    for i in range(3):
        for j in range(3):
            push = stress[i][0] * old_inverse[j][0] + stress[i][1] * old_inverse[j][1] + stress[i][2] * old_inverse[j][2]
            speed = spread(box_speed[i, j]) + time_step * push / (box_mass * atoms_all)
            fresh[i][j] = old[i][j] + time_step * speed
            new_box_speed[i : i + 1, j : j + 1] = speed[:, :1]
            new_box[i : i + 1, j : j + 1] = fresh[i][j][:, :1]
    new_inverse = inverse(fresh)
    for i in range(3):
        move = sum(new_inverse[i][j] * velocities_out[j : j + 1, :] for j in range(3))
        positions_out[i : i + 1, :] = positions[i : i + 1, :] + time_step * move
    for i in range(3):
        move = sum(new_inverse[i][j] * speeds[j] for j in range(3))
        arrivals[i : i + 1, :] = (facts[4 + i : 5 + i] + time_step * move)[:, : 4 * count]
        arrivals[3 + i : 4 + i, :] = speeds[i][:, : 4 * count]


VM = pl.BlockSpec(memory_space=pltpu.VMEM)
HB = pl.BlockSpec(memory_space=pltpu.HBM)
SM = pl.BlockSpec(memory_space=pltpu.SMEM)


def shape(*dims, dtype=f32):
    return jax.ShapeDtypeStruct(dims, dtype)


def call(kernel, outs, scalar_inputs=(), far_inputs=False, far_outputs=(), scratch=(), flops=0, vmem=16, name=None):
    def run(*args):
        moved = sum(math.prod(x.shape) * x.dtype.itemsize for x in list(args) + list(outs))
        return pl.pallas_call(
            kernel,
            out_shape=tuple(outs),
            in_specs=[HB if far_inputs else SM if i in scalar_inputs else VM for i in range(len(args))],
            out_specs=tuple(HB if i in far_outputs else VM for i in range(len(outs))),
            scratch_shapes=list(scratch),
            compiler_params=pltpu.CompilerParams(vmem_limit_bytes=vmem * 1024 * 1024),
            cost_estimate=pl.CostEstimate(flops=flops, bytes_accessed=moved, transcendentals=0),
            name=name,
        )(*args)

    return run


def body(
    positions, velocities, species, ghost_species, neighbours, slot_mask, edge_vectors, send_slab, send_sub, migrants,
    embedding, energy_shift, masses, radial_one_in, radial_one_mid, radial_one_out, node_one,
    radial_two_in, radial_two_mid, radial_two_out, node_two, readout_linear, readout_hidden, readout_out,
    box_matrix, box_velocity,
):
    slots, atoms = neighbours.shape
    width = node_one.shape[1]
    hidden = radial_one_mid.shape[1]
    depth = 4 * width
    ghost_slab, ghost_sub = send_slab.shape[1], send_sub.shape[1]
    extended = atoms + 2 * ghost_slab + 2 * ghost_sub
    edges = slots * atoms
    devices = lax.axis_size("slab") * lax.axis_size("sub")
    species_row = species.reshape(1, atoms)
    ghost_row = ghost_species.reshape(1, -1)
    linear_row = readout_linear.reshape(1, -1)
    out_row = readout_out.reshape(1, -1)
    radial_one_in, radial_one_out = jnp.transpose(radial_one_in), jnp.transpose(radial_one_out)
    radial_two_in, radial_two_out = jnp.transpose(radial_two_in), jnp.transpose(radial_two_out)

    first_inputs = (
        edge_vectors, slot_mask, neighbours, species_row, ghost_row, embedding,
        radial_one_in, radial_one_mid, radial_one_out, node_one, send_slab, send_sub,
        velocities, positions, migrants, masses.reshape(1, -1), energy_shift.reshape(1, -1),
        readout_hidden, linear_row, out_row, radial_two_in, radial_two_mid, radial_two_out, node_two,
    )
    packed_rows = (
        8 * width + 6 * packed_step(slots) + FACTS + 6 * hidden + radial_two_in.shape[0] + packed_step(slots)
        + readout_hidden.shape[0] + 8 + 2 * radial_one_in.shape[0] * packed_step(slots)
    )
    kinds, sums, packed, to_minus, to_plus, to_prev, to_next = call(
        first_kernel,
        (
            shape(slots, atoms, dtype=jnp.int32),
            shape(5, width, atoms),
            shape(packed_rows, atoms),
            shape(ghost_slab, depth),
            shape(ghost_slab, depth),
            shape(ghost_sub, depth),
            shape(ghost_sub, depth),
        ),
        far_inputs=True,
        far_outputs=(1, 2),
        scratch=(
            pltpu.VMEM((6, slots, atoms), f32),
            pltpu.VMEM((2 * radial_one_in.shape[0], slots, atoms), f32),
            pltpu.VMEM((packed_rows, atoms), f32),
            pltpu.VMEM((5, width, atoms), f32),
        )
        + tuple(pltpu.VMEM(x.shape, x.dtype) for x in first_inputs)
        + (pltpu.SemaphoreType.DMA((FIRST_INPUTS,)), pltpu.SemaphoreType.DMA((4,))),
        flops=6 * edges * 26000,
        vmem=56,
        name="layer_one",
    )(
        *first_inputs
    )
    from_minus, from_plus, from_prev, from_next = trade(to_minus, to_plus, to_prev, to_next)

    def radial(*refs):
        radial_kernel(
            *refs,
            slab_rows=ghost_slab,
            sub_rows=ghost_sub,
            moves=migrants.shape[1],
            basis_count=radial_two_in.shape[0],
        )

    (
        weights_all, slopes, onehot, outer, fold_high, fold_low, back_high, back_low,
        geo, own_table, scalars, extras, facts, heads, waves,
    ) = call(
        radial,
        (
            shape(depth, edges),
            shape(3 * hidden, edges, dtype=bf16),
            shape(2 * extended, edges, dtype=bf16),
            shape(depth, 3 * hidden, dtype=bf16),
            shape(readout_hidden.shape[0], 3 * width, dtype=bf16),
            shape(readout_hidden.shape[0], 3 * width, dtype=bf16),
            shape(3 * width, readout_hidden.shape[0], dtype=bf16),
            shape(3 * width, readout_hidden.shape[0], dtype=bf16),
            shape(6, slots, atoms),
            shape(depth, 2 * atoms, dtype=bf16),
            shape(width, atoms),
            shape(4, 8, 2 * atoms),
            shape(FACTS, atoms),
            shape(readout_hidden.shape[0] + 8, atoms),
            shape(2 * radial_two_in.shape[0], slots, atoms),
        ),
        flops=12 * edges * 10000,
        vmem=12,
        name="radial_two",
    )(
        packed,
    )

    energy, scalar_pull, picked_all, pulls, own_pull, back_minus, back_plus, back_prev, back_next = call(
        second_kernel,
        (
            shape(1, atoms),
            shape(width, atoms),
            shape(depth, edges),
            shape(4, width, atoms),
            shape(atoms, depth),
            shape(ghost_slab + 8, depth),
            shape(ghost_slab + 8, depth),
            shape(ghost_sub + 8, depth),
            shape(ghost_sub + 8, depth),
        ),
        scratch=(pltpu.VMEM((depth, 2 * extended), bf16), pltpu.VMEM((extended, depth), f32)),
        flops=4 * edges * depth * extended * 2,
        vmem=28,
        name="layer_two",
    )(
        geo, own_table, from_minus, from_plus, from_prev, from_next, scalars, extras,
        weights_all, onehot, fold_high, fold_low, back_high, back_low, heads,
    )
    ret_minus, ret_plus, ret_prev, ret_next = trade(back_minus, back_plus, back_prev, back_next)
    geo_pull, scalar_slope, vector_slope, vector_value, turned_high, turned_low, base = call(
        window_kernel,
        (
            shape(4, slots, atoms),
            shape(width, edges),
            shape(width, edges),
            shape(width, edges),
            shape(7 * width, width, dtype=bf16),
            shape(7 * width, width, dtype=bf16),
            shape(width, atoms),
        ),
        flops=12 * edges * 12000,
        vmem=20,
        name="radial_one",
    )(
        slopes, outer, picked_all, weights_all, pulls,
        geo, waves, kinds, scalar_pull, embedding,
        radial_one_in, radial_one_mid, radial_one_out, node_one, node_two, linear_row,
    )

    def back(*refs):
        third_kernel(*refs, moves=migrants.shape[1], slab_rows=ghost_slab, sub_rows=ghost_sub)

    everyone, came = call(
        back,
        (shape(devices, 16, atoms), shape(8, atoms)),
        scratch=(
            pltpu.VMEM((16, atoms), f32),
            pltpu.VMEM((4, width, atoms), f32),
            pltpu.VMEM((4, slots, atoms), f32),
        ),
        flops=6 * edges * 1000,
        vmem=12,
        name="layer_one_back",
    )(
        facts, geo, sums, geo_pull, own_pull, ret_minus, ret_plus, ret_prev, ret_next,
        onehot, scalar_slope, vector_slope, vector_value, turned_high, turned_low, base,
    )
    everyone = lax.all_to_all(everyone, ("slab", "sub"), 0, 0, tiled=True)

    def last(*refs):
        fifth_kernel(
            *refs, atoms_all=atoms * devices, slab_count=lax.axis_size("slab"), sub_count=lax.axis_size("sub")
        )

    forces, new_velocities, new_positions, arrivals, new_box, new_box_velocity = call(
        last,
        (
            shape(3, atoms), shape(3, atoms), shape(3, atoms), shape(6, 4 * migrants.shape[1]),
            shape(3, 3), shape(3, 3),
        ),
        scalar_inputs=(3, 4),
        scratch=(pltpu.VMEM((3, devices, atoms), f32),),
        flops=1000000,
        vmem=8,
        name="box",
    )(everyone, facts, came, box_matrix, box_velocity)
    return energy.reshape(atoms), forces, new_velocities, new_positions, arrivals, new_box, new_box_velocity


def solution(mesh):
    split = ("slab", "sub")
    one, two, three, copied = P(split), P(None, split), P(None, None, split), P()
    placed = (two, two, one, one, two, two, three, two, two, two) + (copied,) * 16
    return jax.shard_map(
        body,
        mesh=mesh,
        in_specs=placed,
        out_specs=(one, two, two, two, two, copied, copied),
        check_vma=False,
    )
```

```python
import math

import jax
import jax.numpy as jnp
from jax import lax
from jax.experimental import pallas as pl
from jax.experimental.pallas import tpu as pltpu
from jax.sharding import PartitionSpec as P

cutoff = 5.0
neighbor_norm = 0.125
time_step = 0.5
outside_pressure = 0.5
box_mass = 0.125
highest = lax.Precision.HIGHEST
f32 = jnp.float32
bf16 = jnp.bfloat16
GROUP = 4


def shifted(block, axis, distance):
    count = lax.axis_size(axis)
    return lax.ppermute(block, axis, [((i - distance) % count, i) for i in range(count)])


def trade(to_minus, to_plus, to_sub, first):
    from_minus, from_plus = shifted(to_plus, "slab", 1), shifted(to_minus, "slab", -1)
    if lax.axis_size("sub") == 2:
        return from_minus, from_plus, shifted(to_sub, "sub", 1)
    one, two = jnp.split(to_sub, 2, axis=0)
    from_sub = jnp.concatenate([shifted(one, "sub", first), shifted(two, "sub", -first)], axis=0)
    return from_minus, from_plus, from_sub


def parts(x):
    high = x.astype(bf16)
    return high, (x - high.astype(f32)).astype(bf16)


def dot(a, b):
    return jnp.dot(a, b, preferred_element_type=f32)


def dot_nt(a, b):
    return lax.dot_general(a, b, (((1,), (1,)), ((), ())), preferred_element_type=f32)


def exact(a, b, dims=((1,), (0,))):
    return lax.dot_general(a, b, (dims, ((), ())), precision=highest, preferred_element_type=f32)


def product(weight, x):
    high, low = parts(x)
    return dot(weight[0], high) + dot(weight[0], low) + dot(weight[1], high)


def weight_stack(w):
    high = w.astype(bf16).astype(f32)
    return jnp.concatenate([high, high, w - high], axis=1).astype(bf16)


def weight_stack_t(w):
    high = w.astype(bf16).astype(f32)
    return jnp.transpose(jnp.concatenate([high, high, w - high], axis=0)).astype(bf16)


def value_stack(x):
    high, low = parts(x)
    return jnp.concatenate([high, low, high], axis=0)


def value_stack_small(x):
    high = x.astype(bf16).astype(f32)
    return jnp.concatenate([high, x - high, high], axis=0).astype(bf16)


def over_groups(count, step, carry):
    for i in range(count):
        carry = step(i, carry)
    return carry


def span_of(first, count):
    if isinstance(first, int):
        return pl.ds(first, count)
    return pl.ds(pl.multiple_of(first, count), count)


def iota(shape, axis):
    return lax.broadcasted_iota(jnp.int32, shape, axis)


def column(row):
    n = row.shape[1]
    return jnp.sum(jnp.where(iota((n, n), 0) == iota((n, n), 1), row, 0.0), axis=1, keepdims=True)


def sigmoid(x):
    return 0.5 + 0.5 * jnp.tanh(0.5 * x)


def basis(distance, inverse_distance, count):
    scaled = distance * (1.0 / cutoff)
    second = scaled * scaled
    fourth = second * second
    fifth = fourth * scaled
    sixth = fourth * second
    scale = math.sqrt(2.0 / cutoff)
    envelope = 1.0 + sixth * (-28.0 + scaled * (48.0 - 21.0 * scaled))
    front = scale * envelope * inverse_distance
    slope_envelope = fifth * (-168.0 + scaled * (336.0 - 168.0 * scaled)) * (1.0 / cutoff)
    slope_front = scale * inverse_distance * (slope_envelope - envelope * inverse_distance)
    angle = math.pi * scaled
    first_sine, first_cosine = jnp.sin(angle), jnp.cos(angle)
    sine, cosine = first_sine, first_cosine
    values, slopes = [], []
    for order in range(1, count + 1):
        if order > 1:
            sine, cosine = (
                sine * first_cosine + cosine * first_sine,
                cosine * first_cosine - sine * first_sine,
            )
        values.append(sine * front)
        slopes.append(sine * slope_front + cosine * (front * (order * math.pi / cutoff)))
    return values, slopes


def basis_group(waves, first, start, count):
    return jnp.concatenate([waves[start : start + count, first + j, :] for j in range(GROUP)], axis=1)


def hidden_values(value, inner, mid_a, mid_b):
    x = dot(inner, value_stack_small(value))
    for mid in (mid_a, mid_b, None):
        h = x * sigmoid(x)
        if mid is not None:
            x = dot(mid, value_stack(h))
    return h


def hidden_pairs(value, slope, inner, mid_a, mid_b):
    x, dx = dot(inner, value_stack_small(value)), dot(inner, value_stack_small(slope))
    for mid in (mid_a, mid_b, None):
        gate = sigmoid(x)
        h = x * gate
        dh = (gate + h * (1.0 - gate)) * dx
        if mid is not None:
            x, dx = dot(mid, value_stack(h)), dot(mid, value_stack(dh))
    return h, dh


def species_matrix(first_mixing, embedding):
    lifted = exact(first_mixing, embedding, ((1,), (1,)))
    high = lifted.astype(bf16).astype(f32)
    rest = lifted - high
    mid = rest.astype(bf16).astype(f32)
    return jnp.concatenate([high, mid, rest - mid], axis=1).astype(bf16)


def picked_group(lifted, geo, kinds, first, species_count):
    blocks = []
    for j in range(GROUP):
        kind = kinds[pl.ds(first + j, 1), :]
        weight = geo[3, pl.ds(first + j, 1), :]
        blocks.append(jnp.where(iota((species_count, kind.shape[1]), 0) == kind, weight, 0.0))
    block = jnp.concatenate(blocks, axis=1)
    return dot(lifted, jnp.concatenate([block, block, block], axis=0).astype(bf16))


def send_onehot(facts, first, slab_rows, sub_rows):
    atoms = facts.shape[1]
    lengths = (slab_rows, slab_rows, sub_rows, sub_rows)
    rows = [facts[first + 9 + i : first + 10 + i, :n] for i, n in enumerate(lengths)]
    rows = jnp.concatenate(rows, axis=1)
    return (iota((atoms, rows.shape[1]), 0).astype(f32) == rows).astype(f32)


FIRST_INPUTS = 24
FACTS = 16


def packed_step(slots):
    return -(-slots // 8) * 8


def first_kernel(
    *refs,
):
    count = FIRST_INPUTS
    buffers, ready, gone = refs[-count - 2 : -2], refs[-2], refs[-1]
    copies = [pltpu.make_async_copy(refs[i], buffers[i], ready.at[i]) for i in range(count)]
    for copy in copies:
        copy.start()
    (
        edges, mask, neighbours, species, ghosts, embedding, radial_in, radial_mid, radial_out, node_one,
        send_slab, send_sub, velocities, positions, migrants, masses, shifts,
        hidden_head, linear_head, out_head, next_in, next_mid, next_out, node_two,
    ) = buffers
    (
        kinds, far_sums, far_packed, to_minus, to_plus, to_sub,
        geo, waves, packed, sums,
    ) = refs[count : -count - 2]
    for copy in copies[:2]:
        copy.wait()
    slots, atoms = mask.shape
    width = node_one.shape[1]
    species_count, basis_count = embedding.shape[0], radial_in.shape[0]
    ex, ey, ez = edges[0], edges[1], edges[2]
    square = ex * ex + ey * ey + ez * ez
    distance = jnp.sqrt(square)
    inverse_distance = 1.0 / distance
    for a, e in enumerate((ex, ey, ez)):
        geo[a] = e * inverse_distance
    geo[3] = mask[...].astype(f32) * neighbor_norm
    geo[4] = distance
    geo[5] = inverse_distance
    base = 5 * width
    step = packed_step(slots)
    values, slopes = basis(distance, inverse_distance, radial_in.shape[0])
    for i, wave in enumerate(values + slopes):
        waves[i] = wave
    for a in range(6):
        packed[base + a * step : base + a * step + slots] = geo[a]
    for copy in copies[2:5]:
        copy.wait()
    ghost_row = ghosts[...]
    extra = -ghost_row.shape[1] % atoms
    if extra:
        ghost_row = jnp.concatenate([ghost_row, jnp.zeros((1, extra), jnp.int32)], axis=1)
    tables = [species[...]] + [ghost_row[:, i : i + atoms] for i in range(0, ghost_row.shape[1], atoms)]
    pad = -slots % 8
    rows = neighbours[...]
    if pad:
        rows = jnp.concatenate([rows, jnp.zeros((pad, atoms), jnp.int32)], axis=0)
    inner_index = lax.rem(rows, atoms)
    block_index = lax.div(rows, atoms)
    found = jnp.zeros_like(rows)
    for i, table in enumerate(tables):
        spread = jnp.broadcast_to(table, rows.shape)
        got = jnp.take_along_axis(spread, inner_index, axis=1)
        found = jnp.where(block_index == i, got, found)
    kinds[...] = found[:slots]

    for copy in copies[5:10]:
        copy.wait()
    inner = weight_stack_t(radial_in[...])
    mid_a, mid_b = weight_stack(radial_mid[0]), weight_stack(radial_mid[1])
    outer = weight_stack_t(radial_out[...])
    lifted = species_matrix(node_one[0], embedding[...])
    sums[...] = jnp.zeros_like(sums)

    def group(step, carry):
        first = step * GROUP
        value = basis_group(waves, first, 0, basis_count)
        h = hidden_values(value, inner, mid_a, mid_b)
        weights = dot(outer, value_stack(h))
        picked = picked_group(lifted, geo, kinds, first, species_count)
        totals = [0.0] * 4
        for j in range(GROUP):
            at = slice(j * atoms, (j + 1) * atoms)
            p = picked[:, at]
            totals[0] = totals[0] + weights[:width, at] * p
            q = weights[width:, at] * p
            for a in range(3):
                totals[a + 1] = totals[a + 1] + q * geo[a, pl.ds(first + j, 1), :]
        for a in range(4):
            sums[a] += totals[a]
        return carry

    over_groups(slots // GROUP, group, 0)

    early_sums = pltpu.make_async_copy(sums.at[:4], far_sums.at[:4], gone.at[2])
    early_sums.start()
    for copy in copies[10:]:
        copy.wait()
    mass = shift = jnp.zeros((1, atoms), f32)
    for i in range(masses.shape[1]):
        mass = jnp.where(species[...] == i, masses[:, i : i + 1], mass)
        shift = jnp.where(species[...] == i, shifts[:, i : i + 1], shift)
    facts = base + 6 * step
    packed[facts : facts + 1] = iota((1, atoms), 1).astype(f32)
    packed[facts + 1 : facts + 4] = velocities[...]
    packed[facts + 4 : facts + 7] = positions[...]
    packed[facts + 7 : facts + 8] = 1.0 / jnp.sqrt(mass)
    packed[facts + 8 : facts + 9] = mass
    packed[facts + 9 : facts + FACTS] = jnp.zeros((FACTS - 9, atoms), f32)
    for i, (lists, at) in enumerate(((send_slab, 1), (send_slab, 0), (send_sub, 1), (send_sub, 0))):
        packed[facts + 9 + i : facts + 10 + i, : lists.shape[1]] = lists[at : at + 1, :].astype(f32)
    count = migrants.shape[1]
    for i, at in enumerate((1, 0, 3, 2)):
        packed[facts + 13 : facts + 14, i * count : (i + 1) * count] = migrants[at : at + 1, :].astype(f32)
    inner_rows = next_mid.shape[1]
    start = facts + FACTS
    for i in range(3):
        packed[start : start + width] = node_two[i + 2]
        start += width
    for i in range(next_out.shape[1] // atoms):
        packed[start : start + inner_rows] = next_out[:, i * atoms : (i + 1) * atoms]
        start += inner_rows
    for i in range(2):
        packed[start : start + inner_rows, :inner_rows] = next_mid[i]
        start += inner_rows
    packed[start : start + next_in.shape[0], :inner_rows] = next_in[...]
    start += next_in.shape[0]
    packed[start : start + slots] = neighbours[...].astype(f32)
    start += step
    count = hidden_head.shape[0]
    packed[start : start + count] = hidden_head[...]
    packed[start + count : start + count + 1] = linear_head[...]
    packed[start + count + 1 : start + count + 2, : out_head.shape[1]] = out_head[...]
    packed[start + count + 2 : start + count + 3] = shift
    start += count + 8
    for i in range(waves.shape[0]):
        packed[start + i * step : start + i * step + slots] = waves[i]
    early = pltpu.make_async_copy(packed.at[base:], far_packed.at[base:], gone.at[0])
    early.start()
    own_onehot = (iota((species_count, atoms), 0) == species[...]).astype(f32)
    own = exact(embedding[...], own_onehot, ((0,), (0,)))
    scalar_sum = sums[0]
    vectors = [sums[1], sums[2], sums[3]]
    squares = vectors[0] * vectors[0] + vectors[1] * vectors[1] + vectors[2] * vectors[2]
    scalars = (
        own
        + product(parts(node_one[1]), scalar_sum)
        + product(parts(node_one[2]), scalar_sum * scalar_sum)
        + product(parts(node_one[3]), squares)
    )
    gate = product(parts(node_one[5]), scalar_sum)
    sums[4] = gate
    late_sums = pltpu.make_async_copy(sums.at[4:], far_sums.at[4:], gone.at[3])
    late_sums.start()
    turned = product(parts(node_one[4]), jnp.concatenate(vectors, axis=1))
    moved = turned + jnp.concatenate([gate * v for v in vectors], axis=1)
    packed[:width] = scalars
    x = product(parts(node_two[0]), scalars)
    y = product(parts(node_two[1]), moved)
    table = jnp.concatenate([x] + [y[:, a * atoms : (a + 1) * atoms] for a in range(3)], axis=0)
    packed[width : 5 * width] = table
    late = pltpu.make_async_copy(packed.at[:base], far_packed.at[:base], gone.at[1])
    late.start()
    pick = send_onehot(packed, facts, send_slab.shape[1], send_sub.shape[1]).astype(bf16)
    high, low = parts(table)
    sent = jnp.transpose(dot(high, pick) + dot(low, pick))
    slab_rows = send_slab.shape[1]
    to_plus[...] = sent[:slab_rows]
    to_minus[...] = sent[slab_rows : 2 * slab_rows]
    to_sub[...] = sent[2 * slab_rows :]
    for copy in (early, late, early_sums, late_sums):
        copy.wait()


def radial_kernel(
    packed,
    weights_all, slopes, onehot, outer, fold_high, fold_low, back_high, back_low,
    geo, table, scalars, extras, facts, heads, waves, *, slab_rows, sub_rows, moves, basis_count,
):
    slots, atoms = geo.shape[1:]
    width = scalars.shape[0]
    depth = 4 * width
    inner_rows = slopes.shape[0] // 3
    scalars[...] = packed[:width]
    first_fact = 5 * width + 6 * packed_step(slots)
    start = first_fact + FACTS
    mixings = [packed[start + i * width : start + (i + 1) * width] for i in range(3)]
    start += 3 * width
    pieces = depth // atoms
    radial_out = [packed[start + i * inner_rows : start + (i + 1) * inner_rows] for i in range(pieces)]
    radial_out = jnp.concatenate(radial_out, axis=1)
    start += pieces * inner_rows
    radial_mid = [packed[start + i * inner_rows : start + (i + 1) * inner_rows, :inner_rows] for i in range(2)]
    start += 2 * inner_rows
    radial_in = packed[start : start + basis_count, :inner_rows]
    first_row = start + basis_count
    start = first_row + packed_step(slots)
    heads[...] = packed[start : start + heads.shape[0]]
    start += heads.shape[0]
    for i in range(2 * basis_count):
        waves[i] = packed[start + i * packed_step(slots) : start + i * packed_step(slots) + slots]
    table[:, :atoms], table[:, atoms:] = parts(packed[width : 5 * width])
    for a in range(6):
        start = 5 * width + a * packed_step(slots)
        geo[a] = packed[start : start + slots]
    facts[...] = packed[first_fact : first_fact + FACTS]
    listed = exact(facts[:8], send_onehot(facts, 0, slab_rows, sub_rows))
    moving = exact(facts[:8], (iota((atoms, 4 * moves), 0).astype(f32) == facts[13:14, : 4 * moves]).astype(f32))
    start = 0
    extras[...] = jnp.zeros_like(extras)
    for i, length in enumerate((slab_rows, slab_rows, sub_rows, sub_rows)):
        extras[i, :, :length] = listed[:, start : start + length]
        extras[i, :, atoms : atoms + moves] = moving[:, i * moves : (i + 1) * moves]
        start += length
    rows = onehot.shape[0] // 2
    outer[...] = weight_stack_t(radial_out)
    folded = product(parts(heads[: heads.shape[0] - 8]), jnp.concatenate(mixings, axis=1))
    fold_high[...], fold_low[...] = parts(folded)
    back_high[...], back_low[...] = parts(jnp.transpose(folded))
    inner = weight_stack_t(radial_in)
    mid_a, mid_b = weight_stack(radial_mid[0]), weight_stack(radial_mid[1])

    def group(step, carry):
        first = step * GROUP
        at = span_of(step * GROUP * atoms, GROUP * atoms)
        value, slope = (basis_group(waves, first, i * basis_count, basis_count) for i in range(2))
        h, dh = hidden_pairs(value, slope, inner, mid_a, mid_b)
        slopes[:, at] = value_stack(dh)
        blocks = []
        for j in range(GROUP):
            row = packed[first_row + first + j : first_row + first + j + 1]
            weight = geo[3, pl.ds(first + j, 1), :]
            row = row.astype(jnp.int32)
            blocks.append(jnp.where(iota((rows, atoms), 0) == row, weight, 0.0).astype(bf16))
        block = jnp.concatenate(blocks, axis=1)
        own, ghosts = block[:atoms], block[atoms:]
        onehot[:, at] = jnp.concatenate([own, own, ghosts, ghosts], axis=0)
        weights_all[:, at] = dot(outer[...], value_stack(h))
        return carry

    over_groups(slots // GROUP, group, 0)


def second_kernel(
    geo, own_table, from_minus, from_plus, from_sub, scalars, extras,
    weights_all, onehot, fold_high, fold_low, back_high, back_low, heads,
    energy, scalar_pull, picked_all, sums, own_pull, back_minus, back_plus, back_sub,
    table, pulled,
):
    slots, atoms = geo.shape[1], geo.shape[2]
    width = scalars.shape[0]
    depth = 4 * width
    ghosts = jnp.concatenate([from_minus[...], from_plus[...], from_sub[...]], axis=0)
    high = ghosts.astype(bf16).astype(f32)
    table[:, : 2 * atoms] = own_table[...]
    table[:, 2 * atoms :] = jnp.transpose(jnp.concatenate([high, ghosts - high], axis=0)).astype(bf16)
    ghost_rows = ghosts.shape[0]
    sums[...] = jnp.zeros_like(sums)

    def units(first, j):
        return [geo[a, pl.ds(first + j, 1), :] for a in range(3)]

    def forward(step, carry):
        first = step * GROUP
        at = span_of(step * GROUP * atoms, GROUP * atoms)
        picked = dot(table[...], onehot[:, at])
        picked_all[:, at] = picked
        totals = [0.0] * 4
        for j in range(GROUP):
            span = slice(j * atoms, (j + 1) * atoms)
            here = span_of((step * GROUP + j) * atoms, atoms)
            p = [picked[a * width : (a + 1) * width, span] for a in range(4)]
            r = [weights_all[a * width : (a + 1) * width, here] for a in range(4)]
            u = units(first, j)
            along = p[1] * u[0] + p[2] * u[1] + p[3] * u[2]
            totals[0] = totals[0] + (r[0] * p[0] + r[3] * along)
            q = r[1] * p[0]
            for a in range(3):
                totals[a + 1] = totals[a + 1] + (q * u[a] + r[2] * p[a + 1])
        for a in range(4):
            sums[a] += totals[a]
        return carry

    over_groups(slots // GROUP, forward, 0)

    scalar_sum = sums[0]
    vectors = [sums[1], sums[2], sums[3]]
    squares = vectors[0] * vectors[0] + vectors[1] * vectors[1] + vectors[2] * vectors[2]
    mixed = jnp.concatenate([scalar_sum, scalar_sum * scalar_sum, squares], axis=0)
    units_out = heads.shape[0] - 8
    readout_hidden = heads[:units_out]
    readout_linear, readout_out = heads[units_out : units_out + 1], heads[units_out + 1 : units_out + 2, :units_out]
    hidden_in = product(parts(readout_hidden), scalars[...]) + product((fold_high[...], fold_low[...]), mixed)
    hidden_gate = sigmoid(hidden_in)
    hidden = hidden_in * hidden_gate
    shift = heads[units_out + 2 : units_out + 3]
    energy[...] = shift + exact(readout_linear, scalars[...]) + exact(readout_out, hidden)
    hidden_pull = column(readout_out) * (hidden_gate + hidden * (1.0 - hidden_gate))
    scalar_pull[...] = exact(readout_hidden, hidden_pull, ((0,), (0,)))
    spread = product((back_high[...], back_low[...]), hidden_pull)
    double = 2.0 * spread[2 * width :]
    sums[0] = spread[:width] + 2.0 * scalar_sum * spread[width : 2 * width]
    for a in range(3):
        sums[a + 1] = vectors[a] * double
    pulled[...] = jnp.zeros_like(pulled)

    def backward(step, carry):
        first = step * GROUP
        at = span_of(step * GROUP * atoms, GROUP * atoms)
        highs, lows = [], []
        for j in range(GROUP):
            here = span_of((step * GROUP + j) * atoms, atoms)
            r = [weights_all[a * width : (a + 1) * width, here] for a in range(4)]
            u = units(first, j)
            ga = [sums[a] for a in range(4)]
            flow = ga[1] * u[0] + ga[2] * u[1] + ga[3] * u[2]
            pull = r[3] * ga[0]
            given = [r[0] * ga[0] + r[1] * flow] + [pull * u[a] + r[2] * ga[a + 1] for a in range(3)]
            high, low = parts(jnp.concatenate(given, axis=0))
            highs.append(high)
            lows.append(low)
        split = jnp.concatenate(highs + lows, axis=1)
        chosen = jnp.concatenate([onehot[:atoms, at], onehot[2 * atoms : 2 * atoms + ghost_rows, at]], axis=0)
        pulled[...] += dot_nt(jnp.concatenate([chosen, chosen], axis=1), split)
        return carry

    over_groups(slots // GROUP, backward, 0)
    own_pull[...] = pulled[:atoms]
    start = atoms
    fill = jnp.zeros((8, depth - extras.shape[2]), f32)
    half = back_sub.shape[0] // 2
    for out, offset, size, which in (
        (back_minus, 0, back_minus.shape[0], 1),
        (back_plus, 0, back_plus.shape[0], 0),
        (back_sub, 0, half, 3),
        (back_sub, half, half, 2),
    ):
        count = size - 8
        out[offset : offset + count] = pulled[start : start + count]
        out[offset + count : offset + size] = jnp.concatenate([extras[which], fill], axis=1)
        start += count


def window_kernel(
    slopes, outer_two, picked_all, weights_all, sums,
    geo, waves, kinds, scalar_pull, embedding, radial_in, radial_mid, radial_out, node_one, node_two, readout_linear,
    geo_pull, scalar_slope, vector_slope, vector_value, turned_high, turned_low, base,
):
    slots, atoms = kinds.shape
    width = node_one.shape[1]
    species_count, basis_count = embedding.shape[0], radial_in.shape[0]
    inner = weight_stack_t(radial_in[...])
    mid_a, mid_b = weight_stack(radial_mid[0]), weight_stack(radial_mid[1])
    outer = weight_stack_t(radial_out[...])
    lifted = species_matrix(node_one[0], embedding[...])
    scalar_mixing = jnp.concatenate([jnp.transpose(node_one[i]) for i in (1, 2, 3)], axis=0)
    base[...] = column(readout_linear[...]) + scalar_pull[...]
    turned = [scalar_mixing] + [jnp.transpose(m) for m in (node_two[1], node_one[4], node_one[5], node_two[0])]
    turned_high[...], turned_low[...] = parts(jnp.concatenate(turned, axis=0))

    def group(step, carry):
        first = step * GROUP
        at = span_of(step * GROUP * atoms, GROUP * atoms)
        value, slope = (basis_group(waves, first, i * basis_count, basis_count) for i in range(2))
        h, dh = hidden_pairs(value, slope, inner, mid_a, mid_b)
        picked = picked_group(lifted, geo, kinds, first, species_count)
        weights_slope = dot(outer, value_stack(dh))
        scalar_slope[:, at] = weights_slope[:width] * picked
        vector_slope[:, at] = weights_slope[width:] * picked
        vector_value[:, at] = dot(outer[width:], value_stack(h)) * picked
        return carry

    def edge_group(step, carry):
        first = step * GROUP
        slope = dot(outer_two[...], slopes[:, span_of(step * GROUP * atoms, GROUP * atoms)])
        for j in range(GROUP):
            span = slice(j * atoms, (j + 1) * atoms)
            here = span_of((step * GROUP + j) * atoms, atoms)
            p = [picked_all[a * width : (a + 1) * width, here] for a in range(4)]
            r = [weights_all[a * width : (a + 1) * width, here] for a in (1, 3)]
            s = [slope[a * width : (a + 1) * width, span] for a in range(4)]
            u = [geo[a, pl.ds(first + j, 1), :] for a in range(3)]
            ga = [sums[a] for a in range(4)]
            along = p[1] * u[0] + p[2] * u[1] + p[3] * u[2]
            flow = ga[1] * u[0] + ga[2] * u[1] + ga[3] * u[2]
            cross = p[1] * ga[1] + p[2] * ga[2] + p[3] * ga[3]
            stretch = p[0] * (s[0] * ga[0] + s[1] * flow) + s[2] * cross + s[3] * (along * ga[0])
            geo_pull[0, pl.ds(first + j, 1), :] = jnp.sum(stretch, axis=0, keepdims=True)
            lean = r[0] * p[0]
            pull = r[1] * ga[0]
            for a in range(3):
                turn = lean * ga[a + 1] + pull * p[a + 1]
                geo_pull[a + 1, pl.ds(first + j, 1), :] = jnp.sum(turn, axis=0, keepdims=True)
        return carry

    for step in range(slots // GROUP):
        group(step, 0)
        edge_group(step, 0)


def third_kernel(
    facts, geo, sums, geo_pull, own_pull, ret_minus, ret_plus, ret_sub,
    onehot, scalar_slope, vector_slope, vector_value, turned_high, turned_low, base,
    everyone, came,
    pieces, pulls, flat, *, moves, slab_rows, sub_rows,
):
    slots, atoms = geo.shape[1], geo.shape[2]
    width = sums.shape[1]
    half = sub_rows + 8
    ret_next, ret_prev = ret_sub.at[:half], ret_sub.at[half:]
    pick = send_onehot(facts, 0, slab_rows, sub_rows).astype(bf16)
    returned = jnp.concatenate(
        [ret_plus[:slab_rows], ret_minus[:slab_rows], ret_next[:sub_rows], ret_prev[:sub_rows]], axis=0
    )
    high, low = parts(returned)
    total = jnp.transpose(own_pull[...] + dot(pick, high) + dot(pick, low))
    x_pull = total[:width]
    y_pull = jnp.concatenate([total[a * width : (a + 1) * width] for a in (1, 2, 3)], axis=1)

    def turned(i, count=1):
        at = slice(i * width, (i + count) * width)
        return turned_high[at, :], turned_low[at, :]

    moved = product(turned(3), y_pull)
    gv = [moved[:, a * atoms : (a + 1) * atoms] for a in range(3)]
    scalar_sum, gate = sums[0], sums[4]
    vectors = [sums[1], sums[2], sums[3]]
    scalars = product(turned(6), x_pull) + base[...]
    spread = product(turned(0, 3), scalars)
    mixed = product(turned(4), moved)
    gated = product(turned(5), gv[0] * vectors[0] + gv[1] * vectors[1] + gv[2] * vectors[2])
    pulls[0] = spread[:width] + 2.0 * scalar_sum * spread[width : 2 * width] + gated
    double = 2.0 * spread[2 * width :]
    for a in range(3):
        pulls[a + 1] = vectors[a] * double + mixed[:, a * atoms : (a + 1) * atoms] + gate * gv[a]

    def contract(step, carry):
        first = step * GROUP
        for j in range(GROUP):
            here = span_of((step * GROUP + j) * atoms, atoms)
            row = pl.ds(first + j, 1)
            ga = [pulls[a] for a in range(4)]
            u = [geo[a, row, :] for a in range(3)]
            flow = ga[1] * u[0] + ga[2] * u[1] + ga[3] * u[2]
            stretch = scalar_slope[:, here] * ga[0] + vector_slope[:, here] * flow
            value = vector_value[:, here]
            flat[0, row, :] = jnp.sum(stretch, axis=0, keepdims=True)
            for a in range(3):
                flat[a + 1, row, :] = jnp.sum(value * ga[a + 1], axis=0, keepdims=True)
        return carry

    over_groups(slots // GROUP, contract, 0)
    stretch = flat[0] + geo_pull[0]
    turn = [flat[a + 1] + geo_pull[a + 1] for a in range(3)]
    u = [geo[a] for a in range(3)]
    inner = turn[0] * u[0] + turn[1] * u[1] + turn[2] * u[2]
    gradient = [stretch * u[a] + (turn[a] - inner * u[a]) * geo[5] for a in range(3)]
    at_row = iota((8, atoms), 0)
    own = jnp.zeros((8, atoms), f32)
    for a in range(3):
        flat[a] = gradient[a]
        own = jnp.where(at_row == a, jnp.sum(gradient[a], axis=0, keepdims=True), own)

    def push(step, carry):
        blocks = []
        for j in range(GROUP):
            row = pl.ds(step * GROUP + j, 1)
            block = jnp.where(at_row == 0, flat[0, row, :], jnp.where(at_row == 1, flat[1, row, :], flat[2, row, :]))
            blocks.append(block)
        block = jnp.concatenate(blocks, axis=1)
        top = block.astype(bf16).astype(f32)
        rest = block - top
        mid = rest.astype(bf16).astype(f32)
        split = jnp.concatenate([top, mid, rest - mid], axis=0).astype(bf16)
        at = span_of(step * GROUP * atoms, GROUP * atoms)
        chosen = jnp.concatenate([onehot[:atoms, at], onehot[2 * atoms : 2 * atoms + ghost_rows, at]], axis=0)
        return carry + dot_nt(chosen, split)

    ghost_rows = onehot.shape[0] // 2 - atoms
    zero = jnp.zeros((onehot.shape[0] // 2, 24), f32)
    pushed = over_groups(slots // GROUP, push, zero)
    pushed = jnp.transpose(pushed)
    pushed = (pushed[:8] + pushed[8:16] + pushed[16:]) * (1.0 / neighbor_norm)
    own = own - pushed[:, :atoms]
    velocities, mass = facts[1:4], facts[8:9]
    pieces[0:3] = (own * facts[7:8])[:3]
    blocks = ((ret_minus, slab_rows), (ret_plus, slab_rows), (ret_prev, sub_rows), (ret_next, sub_rows))
    start = atoms
    ghost_lines = [[0.0] * 3 for _ in range(3)]
    for i, (ref, count) in enumerate(blocks):
        told = ref[count : count + 8, :count]
        force = -pushed[:, start : start + count]
        start += count
        for a in range(3):
            for b in range(3):
                ghost_lines[a][b] = ghost_lines[a][b] + told[a + 1 : a + 2] * force[b : b + 1]
        scaled = force * told[7:8]
        top = scaled.astype(bf16).astype(f32)
        rest = scaled - top
        mid = rest.astype(bf16).astype(f32)
        split = jnp.concatenate([top, mid, rest - mid], axis=0).astype(bf16)
        place = (iota((atoms, count), 0) == told[0:1].astype(jnp.int32)).astype(bf16)
        spread = dot_nt(split, place)
        pieces[3 * i + 3 : 3 * i + 6] = (spread[:8] + spread[8:16] + spread[16:])[:3]
    came[...] = jnp.zeros_like(came)
    for i, (ref, count) in enumerate(blocks):
        came[:, i * moves : (i + 1) * moves] = ref[count : count + 8, atoms : atoms + moves]

    def line(a, b):
        start = velocities[a : a + 1] * velocities[b : b + 1] * mass
        mixed = velocities[a : a + 1] * own[b : b + 1] + velocities[b : b + 1] * own[a : a + 1]
        return start + time_step * mixed - jnp.sum(u[a] * geo[4] * gradient[b], axis=0, keepdims=True)

    lines = jnp.concatenate([line(a, b) for a in range(3) for b in range(3)] + [jnp.zeros((7, atoms), f32)], axis=0)
    ghosts = [time_step * (ghost_lines[a][b] + ghost_lines[b][a]) for a in range(3) for b in range(3)]
    ghosts = jnp.concatenate(ghosts + [jnp.zeros((7, slab_rows), f32)], axis=0)
    summed = jnp.sum(lines, axis=1, keepdims=True) + jnp.sum(ghosts, axis=1, keepdims=True)
    row = jnp.zeros((1, atoms), f32)
    for i in range(9):
        row = jnp.where(iota((1, atoms), 1) == i, summed[i : i + 1], row)
    pieces[15:16] = row
    for i in range(everyone.shape[0]):
        everyone[i] = pieces[...]


def determinant(m):
    return (
        m[0][0] * (m[1][1] * m[2][2] - m[1][2] * m[2][1])
        - m[0][1] * (m[1][0] * m[2][2] - m[1][2] * m[2][0])
        + m[0][2] * (m[1][0] * m[2][1] - m[1][1] * m[2][0])
    )


def inverse(m):
    whole = determinant(m)
    return [
        [
            (
                m[(j + 1) % 3][(i + 1) % 3] * m[(j + 2) % 3][(i + 2) % 3]
                - m[(j + 1) % 3][(i + 2) % 3] * m[(j + 2) % 3][(i + 1) % 3]
            )
            / whole
            for j in range(3)
        ]
        for i in range(3)
    ]


def fifth_kernel(
    pieces, own_facts, came, box, box_speed,
    forces_out, velocities_out, positions_out, arrivals, new_box, new_box_speed,
    whole, *, atoms_all, slab_count, sub_count,
):
    atoms = own_facts.shape[1]
    velocities, positions = own_facts[1:4], own_facts[4:7]
    devices = slab_count * sub_count
    sub = lax.rem(iota((devices, atoms), 0), sub_count)

    def row_of_all(r):
        return pieces[:, r, :]

    def piece(i, a):
        return row_of_all(3 * i + a)

    def moved(x, step):
        return pltpu.roll(x, (-step) % devices, 0)

    for a in range(3):
        total = piece(0, a) + moved(piece(1, a), sub_count) + moved(piece(2, a), -sub_count)
        x = piece(3, a)
        total = total + jnp.where(sub == sub_count - 1, moved(x, 1 - sub_count), moved(x, 1))
        x = piece(4, a)
        whole[a] = total + jnp.where(sub == 0, moved(x, sub_count - 1), moved(x, -1))
    squares = {}
    for a in range(3):
        for b in range(a, 3):
            squares[a, b] = jnp.sum(whole[a] * whole[b], axis=0, keepdims=True)
    order = list(squares)
    squares = jnp.concatenate([squares[k] for k in order] + [jnp.zeros((2, atoms), f32)], axis=0)
    squares = jnp.sum(squares, axis=1, keepdims=True)
    rest = jnp.sum(row_of_all(15), axis=0, keepdims=True)
    stress = [[None] * 3 for _ in range(3)]
    for i in range(3):
        for j in range(3):
            at = order.index((min(i, j), max(i, j)))
            stress[i][j] = rest[:, 3 * i + j : 3 * i + j + 1] + (time_step * time_step) * squares[at : at + 1]
    slab_at, sub_at = lax.axis_index("slab"), lax.axis_index("sub")
    mine = slab_at * sub_count + sub_at
    root, mass = own_facts[7:8], own_facts[8:9]
    for a in range(3):
        force = whole[a, pl.ds(mine, 1), :] * (mass * root)
        forces_out[a : a + 1, :] = force
        velocities_out[a : a + 1, :] = velocities[a : a + 1, :] + time_step * force / mass
    lane, row = iota((8, atoms), 1), iota((8, atoms), 0)
    facts = came[...]
    index = jnp.broadcast_to(facts[0:1].astype(jnp.int32), (8, atoms))
    count = arrivals.shape[1] // 4
    picked = jnp.zeros((8, atoms), f32)
    for i, (slab_step, sub_step) in enumerate(((-1, 0), (1, 0), (0, -1), (0, 1))):
        slab = lax.rem(slab_at + (slab_step + slab_count), slab_count)
        source = slab * sub_count + lax.rem(sub_at + (sub_step + sub_count), sub_count)
        force = [whole[a, pl.ds(source, 1), :] for a in range(3)]
        force = jnp.where(row == 0, force[0], jnp.where(row == 1, force[1], force[2]))
        found = jnp.take_along_axis(force, index, axis=1)
        picked = jnp.where((lane >= i * count) & (lane < (i + 1) * count), found, picked)
    speeds = [facts[1 + a : 2 + a] + time_step * picked[a : a + 1] * facts[7:8] for a in range(3)]

    def spread(value):
        return jnp.full((1, atoms), value, f32)

    old = [[spread(box[i, j]) for j in range(3)] for i in range(3)]
    volume = determinant(old)
    old_inverse = inverse(old)
    for i in range(3):
        stress[i][i] = stress[i][i] - outside_pressure * volume
    fresh = [[None] * 3 for _ in range(3)]
    for i in range(3):
        for j in range(3):
            push = stress[i][0] * old_inverse[j][0] + stress[i][1] * old_inverse[j][1] + stress[i][2] * old_inverse[j][2]
            speed = spread(box_speed[i, j]) + time_step * push / (box_mass * atoms_all)
            fresh[i][j] = old[i][j] + time_step * speed
            new_box_speed[i : i + 1, j : j + 1] = speed[:, :1]
            new_box[i : i + 1, j : j + 1] = fresh[i][j][:, :1]
    new_inverse = inverse(fresh)
    for i in range(3):
        move = sum(new_inverse[i][j] * velocities_out[j : j + 1, :] for j in range(3))
        positions_out[i : i + 1, :] = positions[i : i + 1, :] + time_step * move
    for i in range(3):
        move = sum(new_inverse[i][j] * speeds[j] for j in range(3))
        arrivals[i : i + 1, :] = (facts[4 + i : 5 + i] + time_step * move)[:, : 4 * count]
        arrivals[3 + i : 4 + i, :] = speeds[i][:, : 4 * count]


VM = pl.BlockSpec(memory_space=pltpu.VMEM)
HB = pl.BlockSpec(memory_space=pltpu.HBM)
SM = pl.BlockSpec(memory_space=pltpu.SMEM)


def shape(*dims, dtype=f32):
    return jax.ShapeDtypeStruct(dims, dtype)


def call(kernel, outs, scalar_inputs=(), far_inputs=False, far_outputs=(), scratch=(), flops=0, vmem=16, name=None):
    def run(*args):
        moved = sum(math.prod(x.shape) * x.dtype.itemsize for x in list(args) + list(outs))
        return pl.pallas_call(
            kernel,
            out_shape=tuple(outs),
            in_specs=[HB if far_inputs else SM if i in scalar_inputs else VM for i in range(len(args))],
            out_specs=tuple(HB if i in far_outputs else VM for i in range(len(outs))),
            scratch_shapes=list(scratch),
            compiler_params=pltpu.CompilerParams(vmem_limit_bytes=vmem * 1024 * 1024),
            cost_estimate=pl.CostEstimate(flops=flops, bytes_accessed=moved, transcendentals=0),
            name=name,
        )(*args)

    return run


def body(
    positions, velocities, species, ghost_species, neighbours, slot_mask, edge_vectors, send_slab, send_sub, migrants,
    embedding, energy_shift, masses, radial_one_in, radial_one_mid, radial_one_out, node_one,
    radial_two_in, radial_two_mid, radial_two_out, node_two, readout_linear, readout_hidden, readout_out,
    box_matrix, box_velocity,
):
    slots, atoms = neighbours.shape
    width = node_one.shape[1]
    hidden = radial_one_mid.shape[1]
    depth = 4 * width
    ghost_slab, ghost_sub = send_slab.shape[1], send_sub.shape[1]
    extended = atoms + 2 * ghost_slab + 2 * ghost_sub
    edges = slots * atoms
    devices = lax.axis_size("slab") * lax.axis_size("sub")
    species_row = species.reshape(1, atoms)
    ghost_row = ghost_species.reshape(1, -1)
    linear_row = readout_linear.reshape(1, -1)
    out_row = readout_out.reshape(1, -1)
    radial_one_in, radial_one_out = jnp.transpose(radial_one_in), jnp.transpose(radial_one_out)
    radial_two_in, radial_two_out = jnp.transpose(radial_two_in), jnp.transpose(radial_two_out)

    first_inputs = (
        edge_vectors, slot_mask, neighbours, species_row, ghost_row, embedding,
        radial_one_in, radial_one_mid, radial_one_out, node_one, send_slab, send_sub,
        velocities, positions, migrants, masses.reshape(1, -1), energy_shift.reshape(1, -1),
        readout_hidden, linear_row, out_row, radial_two_in, radial_two_mid, radial_two_out, node_two,
    )
    packed_rows = (
        8 * width + 6 * packed_step(slots) + FACTS + 6 * hidden + radial_two_in.shape[0] + packed_step(slots)
        + readout_hidden.shape[0] + 8 + 2 * radial_one_in.shape[0] * packed_step(slots)
    )
    kinds, sums, packed, to_minus, to_plus, to_sub = call(
        first_kernel,
        (
            shape(slots, atoms, dtype=jnp.int32),
            shape(5, width, atoms),
            shape(packed_rows, atoms),
            shape(ghost_slab, depth),
            shape(ghost_slab, depth),
            shape(2 * ghost_sub, depth),
        ),
        far_inputs=True,
        far_outputs=(1, 2),
        scratch=(
            pltpu.VMEM((6, slots, atoms), f32),
            pltpu.VMEM((2 * radial_one_in.shape[0], slots, atoms), f32),
            pltpu.VMEM((packed_rows, atoms), f32),
            pltpu.VMEM((5, width, atoms), f32),
        )
        + tuple(pltpu.VMEM(x.shape, x.dtype) for x in first_inputs)
        + (pltpu.SemaphoreType.DMA((FIRST_INPUTS,)), pltpu.SemaphoreType.DMA((4,))),
        flops=6 * edges * 26000,
        vmem=56,
        name="layer_one",
    )(
        *first_inputs
    )
    from_minus, from_plus, from_sub = trade(to_minus, to_plus, to_sub, 1)

    def radial(*refs):
        radial_kernel(
            *refs,
            slab_rows=ghost_slab,
            sub_rows=ghost_sub,
            moves=migrants.shape[1],
            basis_count=radial_two_in.shape[0],
        )

    (
        weights_all, slopes, onehot, outer, fold_high, fold_low, back_high, back_low,
        geo, own_table, scalars, extras, facts, heads, waves,
    ) = call(
        radial,
        (
            shape(depth, edges),
            shape(3 * hidden, edges, dtype=bf16),
            shape(2 * extended, edges, dtype=bf16),
            shape(depth, 3 * hidden, dtype=bf16),
            shape(readout_hidden.shape[0], 3 * width, dtype=bf16),
            shape(readout_hidden.shape[0], 3 * width, dtype=bf16),
            shape(3 * width, readout_hidden.shape[0], dtype=bf16),
            shape(3 * width, readout_hidden.shape[0], dtype=bf16),
            shape(6, slots, atoms),
            shape(depth, 2 * atoms, dtype=bf16),
            shape(width, atoms),
            shape(4, 8, 2 * atoms),
            shape(FACTS, atoms),
            shape(readout_hidden.shape[0] + 8, atoms),
            shape(2 * radial_two_in.shape[0], slots, atoms),
        ),
        flops=12 * edges * 10000,
        vmem=12,
        name="radial_two",
    )(
        packed,
    )

    energy, scalar_pull, picked_all, pulls, own_pull, back_minus, back_plus, back_sub = call(
        second_kernel,
        (
            shape(1, atoms),
            shape(width, atoms),
            shape(depth, edges),
            shape(4, width, atoms),
            shape(atoms, depth),
            shape(ghost_slab + 8, depth),
            shape(ghost_slab + 8, depth),
            shape(2 * (ghost_sub + 8), depth),
        ),
        scratch=(pltpu.VMEM((depth, 2 * extended), bf16), pltpu.VMEM((extended, depth), f32)),
        flops=4 * edges * depth * extended * 2,
        vmem=28,
        name="layer_two",
    )(
        geo, own_table, from_minus, from_plus, from_sub, scalars, extras,
        weights_all, onehot, fold_high, fold_low, back_high, back_low, heads,
    )
    ret_minus, ret_plus, ret_sub = trade(back_minus, back_plus, back_sub, -1)
    geo_pull, scalar_slope, vector_slope, vector_value, turned_high, turned_low, base = call(
        window_kernel,
        (
            shape(4, slots, atoms),
            shape(width, edges),
            shape(width, edges),
            shape(width, edges),
            shape(7 * width, width, dtype=bf16),
            shape(7 * width, width, dtype=bf16),
            shape(width, atoms),
        ),
        flops=12 * edges * 12000,
        vmem=20,
        name="radial_one",
    )(
        slopes, outer, picked_all, weights_all, pulls,
        geo, waves, kinds, scalar_pull, embedding,
        radial_one_in, radial_one_mid, radial_one_out, node_one, node_two, linear_row,
    )

    def back(*refs):
        third_kernel(*refs, moves=migrants.shape[1], slab_rows=ghost_slab, sub_rows=ghost_sub)

    everyone, came = call(
        back,
        (shape(devices, 16, atoms), shape(8, atoms)),
        scratch=(
            pltpu.VMEM((16, atoms), f32),
            pltpu.VMEM((4, width, atoms), f32),
            pltpu.VMEM((4, slots, atoms), f32),
        ),
        flops=6 * edges * 1000,
        vmem=12,
        name="layer_one_back",
    )(
        facts, geo, sums, geo_pull, own_pull, ret_minus, ret_plus, ret_sub,
        onehot, scalar_slope, vector_slope, vector_value, turned_high, turned_low, base,
    )
    everyone = lax.all_to_all(everyone, ("slab", "sub"), 0, 0, tiled=True)

    def last(*refs):
        fifth_kernel(
            *refs, atoms_all=atoms * devices, slab_count=lax.axis_size("slab"), sub_count=lax.axis_size("sub")
        )

    forces, new_velocities, new_positions, arrivals, new_box, new_box_velocity = call(
        last,
        (
            shape(3, atoms), shape(3, atoms), shape(3, atoms), shape(6, 4 * migrants.shape[1]),
            shape(3, 3), shape(3, 3),
        ),
        scalar_inputs=(3, 4),
        scratch=(pltpu.VMEM((3, devices, atoms), f32),),
        flops=1000000,
        vmem=8,
        name="box",
    )(everyone, facts, came, box_matrix, box_velocity)
    return energy.reshape(atoms), forces, new_velocities, new_positions, arrivals, new_box, new_box_velocity


def solution(mesh):
    split = ("slab", "sub")
    one, two, three, copied = P(split), P(None, split), P(None, None, split), P()
    placed = (two, two, one, one, two, two, three, two, two, two) + (copied,) * 16
    return jax.shard_map(
        body,
        mesh=mesh,
        in_specs=placed,
        out_specs=(one, two, two, two, two, copied, copied),
        check_vma=False,
    )
```

```python
import math

import jax
import jax.numpy as jnp
from jax import lax
from jax.experimental import pallas as pl
from jax.experimental.pallas import tpu as pltpu
from jax.sharding import PartitionSpec as P

cutoff = 5.0
neighbor_norm = 0.125
time_step = 0.5
outside_pressure = 0.5
box_mass = 0.125
highest = lax.Precision.HIGHEST
f32 = jnp.float32
bf16 = jnp.bfloat16
GROUP = 4


def shifted(block, axis, distance):
    count = lax.axis_size(axis)
    return lax.ppermute(block, axis, [((i - distance) % count, i) for i in range(count)])


def trade(to_minus, to_plus, to_sub, first):
    from_minus, from_plus = shifted(to_plus, "slab", 1), shifted(to_minus, "slab", -1)
    if lax.axis_size("sub") == 2:
        return from_minus, from_plus, shifted(to_sub, "sub", 1)
    one, two = jnp.split(to_sub, 2, axis=0)
    from_sub = jnp.concatenate([shifted(one, "sub", first), shifted(two, "sub", -first)], axis=0)
    return from_minus, from_plus, from_sub


def parts(x):
    high = x.astype(bf16)
    return high, (x - high.astype(f32)).astype(bf16)


def dot(a, b):
    return jnp.dot(a, b, preferred_element_type=f32)


def dot_nt(a, b):
    return lax.dot_general(a, b, (((1,), (1,)), ((), ())), preferred_element_type=f32)


def exact(a, b, dims=((1,), (0,))):
    return lax.dot_general(a, b, (dims, ((), ())), precision=highest, preferred_element_type=f32)


def product(weight, x):
    high, low = parts(x)
    return dot(weight[0], high) + dot(weight[0], low) + dot(weight[1], high)


def weight_stack(w):
    high = w.astype(bf16).astype(f32)
    return jnp.concatenate([high, high, w - high], axis=1).astype(bf16)


def weight_stack_t(w):
    high = w.astype(bf16).astype(f32)
    return jnp.transpose(jnp.concatenate([high, high, w - high], axis=0)).astype(bf16)


def value_stack(x):
    high, low = parts(x)
    return jnp.concatenate([high, low, high], axis=0)


def value_stack_small(x):
    high = x.astype(bf16).astype(f32)
    return jnp.concatenate([high, x - high, high], axis=0).astype(bf16)


def over_groups(count, step, carry):
    for i in range(count):
        carry = step(i, carry)
    return carry


def span_of(first, count):
    if isinstance(first, int):
        return pl.ds(first, count)
    return pl.ds(pl.multiple_of(first, count), count)


def iota(shape, axis):
    return lax.broadcasted_iota(jnp.int32, shape, axis)


def column(row):
    n = row.shape[1]
    return jnp.sum(jnp.where(iota((n, n), 0) == iota((n, n), 1), row, 0.0), axis=1, keepdims=True)


def sigmoid(x):
    return 0.5 + 0.5 * jnp.tanh(0.5 * x)


def basis(distance, inverse_distance, count):
    scaled = distance * (1.0 / cutoff)
    second = scaled * scaled
    fourth = second * second
    fifth = fourth * scaled
    sixth = fourth * second
    scale = math.sqrt(2.0 / cutoff)
    envelope = 1.0 + sixth * (-28.0 + scaled * (48.0 - 21.0 * scaled))
    front = scale * envelope * inverse_distance
    slope_envelope = fifth * (-168.0 + scaled * (336.0 - 168.0 * scaled)) * (1.0 / cutoff)
    slope_front = scale * inverse_distance * (slope_envelope - envelope * inverse_distance)
    angle = math.pi * scaled
    first_sine, first_cosine = jnp.sin(angle), jnp.cos(angle)
    sine, cosine = first_sine, first_cosine
    values, slopes = [], []
    for order in range(1, count + 1):
        if order > 1:
            sine, cosine = (
                sine * first_cosine + cosine * first_sine,
                cosine * first_cosine - sine * first_sine,
            )
        values.append(sine * front)
        slopes.append(sine * slope_front + cosine * (front * (order * math.pi / cutoff)))
    return values, slopes


def basis_group(waves, first, start, count):
    return jnp.concatenate([waves[start : start + count, first + j, :] for j in range(GROUP)], axis=1)


def hidden_values(values, inner, mid_a, mid_b):
    xs = [dot(inner, value_stack_small(value)) for value in values]
    for mid in (mid_a, mid_b):
        xs = [dot(mid, value_stack(x * sigmoid(x))) for x in xs]
    return [x * sigmoid(x) for x in xs]


def hidden_pairs(values, slopes, inner, mid_a, mid_b, between=()):
    between = list(between)

    def activated(x, dx):
        gate = sigmoid(x)
        h = x * gate
        return h, (gate + h * (1.0 - gate)) * dx

    pairs = [
        (dot(inner, value_stack_small(value)), dot(inner, value_stack_small(slope)))
        for value, slope in zip(values, slopes)
    ]
    for mid in (mid_a, mid_b):
        after = []
        for i, (x, dx) in enumerate(pairs):
            h, dh = activated(x, dx)
            after.append((dot(mid, value_stack(h)), dot(mid, value_stack(dh))))
            if between and i % 2:
                between.pop(0)()
        pairs = after
    pairs = [activated(x, dx) for x, dx in pairs]
    for work in between:
        work()
    return pairs


def species_matrix(first_mixing, embedding):
    lifted = exact(first_mixing, embedding, ((1,), (1,)))
    high = lifted.astype(bf16).astype(f32)
    rest = lifted - high
    mid = rest.astype(bf16).astype(f32)
    return jnp.concatenate([high, mid, rest - mid], axis=1).astype(bf16)


def picked_group(lifted, geo, kinds, first, species_count):
    blocks = []
    for j in range(GROUP):
        kind = kinds[pl.ds(first + j, 1), :]
        weight = geo[3, pl.ds(first + j, 1), :]
        blocks.append(jnp.where(iota((species_count, kind.shape[1]), 0) == kind, weight, 0.0))
    block = jnp.concatenate(blocks, axis=1)
    return dot(lifted, jnp.concatenate([block, block, block], axis=0).astype(bf16))


def send_onehot(facts, first, slab_rows, sub_rows):
    atoms = facts.shape[1]
    lengths = (slab_rows, slab_rows, sub_rows, sub_rows)
    rows = [facts[first + 9 + i : first + 10 + i, :n] for i, n in enumerate(lengths)]
    rows = jnp.concatenate(rows, axis=1)
    return (iota((atoms, rows.shape[1]), 0).astype(f32) == rows).astype(f32)


FIRST_INPUTS = 24
FACTS = 16


def packed_step(slots):
    return -(-slots // 8) * 8


def first_kernel(
    *refs,
):
    count = FIRST_INPUTS
    buffers, ready, gone = refs[-count - 2 : -2], refs[-2], refs[-1]
    copies = [pltpu.make_async_copy(refs[i], buffers[i], ready.at[i]) for i in range(count)]
    for copy in copies:
        copy.start()
    (
        edges, mask, neighbours, species, ghosts, embedding, radial_in, radial_mid, radial_out, node_one,
        send_slab, send_sub, velocities, positions, migrants, masses, shifts,
        hidden_head, linear_head, out_head, next_in, next_mid, next_out, node_two,
    ) = buffers
    (
        kinds, far_sums, far_packed, to_minus, to_plus, to_sub,
        geo, waves, packed, sums,
    ) = refs[count : -count - 2]
    for copy in copies[:2]:
        copy.wait()
    slots, atoms = mask.shape
    width = node_one.shape[1]
    species_count, basis_count = embedding.shape[0], radial_in.shape[0]
    ex, ey, ez = edges[0], edges[1], edges[2]
    square = ex * ex + ey * ey + ez * ez
    distance = jnp.sqrt(square)
    inverse_distance = 1.0 / distance
    for a, e in enumerate((ex, ey, ez)):
        geo[a] = e * inverse_distance
    geo[3] = mask[...].astype(f32) * neighbor_norm
    geo[4] = distance
    geo[5] = inverse_distance
    base = 5 * width
    step = packed_step(slots)
    values, slopes = basis(distance, inverse_distance, radial_in.shape[0])
    for i, wave in enumerate(values + slopes):
        waves[i] = wave
    for a in range(6):
        packed[base + a * step : base + a * step + slots] = geo[a]
    for copy in copies[2:5]:
        copy.wait()
    ghost_row = ghosts[...]
    extra = -ghost_row.shape[1] % atoms
    if extra:
        ghost_row = jnp.concatenate([ghost_row, jnp.zeros((1, extra), jnp.int32)], axis=1)
    tables = [species[...]] + [ghost_row[:, i : i + atoms] for i in range(0, ghost_row.shape[1], atoms)]
    pad = -slots % 8
    rows = neighbours[...]
    if pad:
        rows = jnp.concatenate([rows, jnp.zeros((pad, atoms), jnp.int32)], axis=0)
    inner_index = lax.rem(rows, atoms)
    block_index = lax.div(rows, atoms)
    found = jnp.zeros_like(rows)
    for i, table in enumerate(tables):
        spread = jnp.broadcast_to(table, rows.shape)
        got = jnp.take_along_axis(spread, inner_index, axis=1)
        found = jnp.where(block_index == i, got, found)
    kinds[...] = found[:slots]

    for copy in copies[5:10]:
        copy.wait()
    inner = weight_stack_t(radial_in[...])
    mid_a, mid_b = weight_stack(radial_mid[0]), weight_stack(radial_mid[1])
    outer = weight_stack_t(radial_out[...])
    lifted = species_matrix(node_one[0], embedding[...])
    sums[...] = jnp.zeros_like(sums)

    values = [basis_group(waves, i * GROUP, 0, basis_count) for i in range(slots // GROUP)]
    hidden = hidden_values(values, inner, mid_a, mid_b)

    def group(step, carry):
        first = step * GROUP
        weights = dot(outer, value_stack(hidden[step]))
        picked = picked_group(lifted, geo, kinds, first, species_count)
        totals = [0.0] * 4
        for j in range(GROUP):
            at = slice(j * atoms, (j + 1) * atoms)
            p = picked[:, at]
            totals[0] = totals[0] + weights[:width, at] * p
            q = weights[width:, at] * p
            for a in range(3):
                totals[a + 1] = totals[a + 1] + q * geo[a, pl.ds(first + j, 1), :]
        for a in range(4):
            sums[a] += totals[a]
        return carry

    over_groups(slots // GROUP, group, 0)

    early_sums = pltpu.make_async_copy(sums.at[:4], far_sums.at[:4], gone.at[2])
    early_sums.start()
    for copy in copies[10:]:
        copy.wait()
    mass = shift = jnp.zeros((1, atoms), f32)
    for i in range(masses.shape[1]):
        mass = jnp.where(species[...] == i, masses[:, i : i + 1], mass)
        shift = jnp.where(species[...] == i, shifts[:, i : i + 1], shift)
    facts = base + 6 * step
    packed[facts : facts + 1] = iota((1, atoms), 1).astype(f32)
    packed[facts + 1 : facts + 4] = velocities[...]
    packed[facts + 4 : facts + 7] = positions[...]
    packed[facts + 7 : facts + 8] = 1.0 / jnp.sqrt(mass)
    packed[facts + 8 : facts + 9] = mass
    packed[facts + 9 : facts + FACTS] = jnp.zeros((FACTS - 9, atoms), f32)
    for i, (lists, at) in enumerate(((send_slab, 1), (send_slab, 0), (send_sub, 1), (send_sub, 0))):
        packed[facts + 9 + i : facts + 10 + i, : lists.shape[1]] = lists[at : at + 1, :].astype(f32)
    count = migrants.shape[1]
    for i, at in enumerate((1, 0, 3, 2)):
        packed[facts + 13 : facts + 14, i * count : (i + 1) * count] = migrants[at : at + 1, :].astype(f32)
    inner_rows = next_mid.shape[1]
    start = facts + FACTS
    for i in range(3):
        packed[start : start + width] = node_two[i + 2]
        start += width
    for i in range(next_out.shape[1] // atoms):
        packed[start : start + inner_rows] = next_out[:, i * atoms : (i + 1) * atoms]
        start += inner_rows
    for i in range(2):
        packed[start : start + inner_rows, :inner_rows] = next_mid[i]
        start += inner_rows
    packed[start : start + next_in.shape[0], :inner_rows] = next_in[...]
    start += next_in.shape[0]
    packed[start : start + slots] = neighbours[...].astype(f32)
    start += step
    count = hidden_head.shape[0]
    packed[start : start + count] = hidden_head[...]
    packed[start + count : start + count + 1] = linear_head[...]
    packed[start + count + 1 : start + count + 2, : out_head.shape[1]] = out_head[...]
    packed[start + count + 2 : start + count + 3] = shift
    start += count + 8
    for i in range(waves.shape[0]):
        packed[start + i * step : start + i * step + slots] = waves[i]
    early = pltpu.make_async_copy(packed.at[base:], far_packed.at[base:], gone.at[0])
    early.start()
    own_onehot = (iota((species_count, atoms), 0) == species[...]).astype(f32)
    own = exact(embedding[...], own_onehot, ((0,), (0,)))
    scalar_sum = sums[0]
    vectors = [sums[1], sums[2], sums[3]]
    squares = vectors[0] * vectors[0] + vectors[1] * vectors[1] + vectors[2] * vectors[2]
    scalars = (
        own
        + product(parts(node_one[1]), scalar_sum)
        + product(parts(node_one[2]), scalar_sum * scalar_sum)
        + product(parts(node_one[3]), squares)
    )
    gate = product(parts(node_one[5]), scalar_sum)
    sums[4] = gate
    late_sums = pltpu.make_async_copy(sums.at[4:], far_sums.at[4:], gone.at[3])
    late_sums.start()
    turned = product(parts(node_one[4]), jnp.concatenate(vectors, axis=1))
    moved = turned + jnp.concatenate([gate * v for v in vectors], axis=1)
    packed[:width] = scalars
    x = product(parts(node_two[0]), scalars)
    y = product(parts(node_two[1]), moved)
    table = jnp.concatenate([x] + [y[:, a * atoms : (a + 1) * atoms] for a in range(3)], axis=0)
    packed[width : 5 * width] = table
    late = pltpu.make_async_copy(packed.at[:base], far_packed.at[:base], gone.at[1])
    late.start()
    pick = send_onehot(packed, facts, send_slab.shape[1], send_sub.shape[1]).astype(bf16)
    high, low = parts(table)
    sent = jnp.transpose(dot(high, pick) + dot(low, pick))
    slab_rows = send_slab.shape[1]
    to_plus[...] = sent[:slab_rows]
    to_minus[...] = sent[slab_rows : 2 * slab_rows]
    to_sub[...] = sent[2 * slab_rows :]
    for copy in (early, late, early_sums, late_sums):
        copy.wait()


def radial_kernel(
    packed,
    weights_all, slopes, onehot, outer, fold_high, fold_low, back_high, back_low,
    geo, picked_own, scalars, extras, facts, heads, waves, *, slab_rows, sub_rows, moves, basis_count,
):
    slots, atoms = geo.shape[1:]
    width = scalars.shape[0]
    depth = 4 * width
    inner_rows = slopes.shape[0] // 3
    scalars[...] = packed[:width]
    first_fact = 5 * width + 6 * packed_step(slots)
    start = first_fact + FACTS
    mixings = [packed[start + i * width : start + (i + 1) * width] for i in range(3)]
    start += 3 * width
    pieces = depth // atoms
    radial_out = [packed[start + i * inner_rows : start + (i + 1) * inner_rows] for i in range(pieces)]
    radial_out = jnp.concatenate(radial_out, axis=1)
    start += pieces * inner_rows
    radial_mid = [packed[start + i * inner_rows : start + (i + 1) * inner_rows, :inner_rows] for i in range(2)]
    start += 2 * inner_rows
    radial_in = packed[start : start + basis_count, :inner_rows]
    first_row = start + basis_count
    start = first_row + packed_step(slots)
    heads[...] = packed[start : start + heads.shape[0]]
    start += heads.shape[0]
    for i in range(2 * basis_count):
        waves[i] = packed[start + i * packed_step(slots) : start + i * packed_step(slots) + slots]
    table = jnp.concatenate(parts(packed[width : 5 * width]), axis=1)
    for a in range(6):
        start = 5 * width + a * packed_step(slots)
        geo[a] = packed[start : start + slots]
    facts[...] = packed[first_fact : first_fact + FACTS]
    listed = exact(facts[:8], send_onehot(facts, 0, slab_rows, sub_rows))
    moving = exact(facts[:8], (iota((atoms, 4 * moves), 0).astype(f32) == facts[13:14, : 4 * moves]).astype(f32))
    start = 0
    extras[...] = jnp.zeros_like(extras)
    for i, length in enumerate((slab_rows, slab_rows, sub_rows, sub_rows)):
        extras[i, :, :length] = listed[:, start : start + length]
        extras[i, :, atoms : atoms + moves] = moving[:, i * moves : (i + 1) * moves]
        start += length
    rows = onehot.shape[0] // 2
    outer[...] = weight_stack_t(radial_out)
    folded = product(parts(heads[: heads.shape[0] - 8]), jnp.concatenate(mixings, axis=1))
    fold_high[...], fold_low[...] = parts(folded)
    back_high[...], back_low[...] = parts(jnp.transpose(folded))
    inner = weight_stack_t(radial_in)
    mid_a, mid_b = weight_stack(radial_mid[0]), weight_stack(radial_mid[1])

    values, slopes_in = (
        [basis_group(waves, i * GROUP, start, basis_count) for i in range(slots // GROUP)] for start in (0, basis_count)
    )
    hidden = hidden_pairs(values, slopes_in, inner, mid_a, mid_b)

    def group(step, carry):
        first = step * GROUP
        at = span_of(step * GROUP * atoms, GROUP * atoms)
        h, dh = hidden[step]
        slopes[:, at] = value_stack(dh)
        blocks = []
        for j in range(GROUP):
            row = packed[first_row + first + j : first_row + first + j + 1]
            weight = geo[3, pl.ds(first + j, 1), :]
            row = row.astype(jnp.int32)
            blocks.append(jnp.where(iota((rows, atoms), 0) == row, weight, 0.0).astype(bf16))
        block = jnp.concatenate(blocks, axis=1)
        own, ghosts = block[:atoms], block[atoms:]
        both = jnp.concatenate([own, own], axis=0)
        onehot[:, at] = jnp.concatenate([both, ghosts, ghosts], axis=0)
        picked_own[:, at] = dot(table, both)
        weights_all[:, at] = dot(outer[...], value_stack(h))
        return carry

    over_groups(slots // GROUP, group, 0)


def second_kernel(
    geo, picked_own, from_minus, from_plus, from_sub, scalars, extras,
    weights_all, onehot, fold_high, fold_low, back_high, back_low, heads,
    energy, scalar_pull, picked_all, sums, own_pull, back_minus, back_plus, back_sub,
    table, pulled,
):
    slots, atoms = geo.shape[1], geo.shape[2]
    width = scalars.shape[0]
    depth = 4 * width
    ghosts = jnp.concatenate([from_minus[...], from_plus[...], from_sub[...]], axis=0)
    high = ghosts.astype(bf16).astype(f32)
    table[...] = jnp.transpose(jnp.concatenate([high, ghosts - high], axis=0)).astype(bf16)
    ghost_rows = ghosts.shape[0]
    sums[...] = jnp.zeros_like(sums)

    def units(first, j):
        return [geo[a, pl.ds(first + j, 1), :] for a in range(3)]

    def forward(step, carry):
        first = step * GROUP
        at = span_of(step * GROUP * atoms, GROUP * atoms)
        picked = picked_own[:, at] + dot(table[...], onehot[2 * atoms :, at])
        picked_all[:, at] = picked
        totals = [0.0] * 4
        for j in range(GROUP):
            span = slice(j * atoms, (j + 1) * atoms)
            here = span_of((step * GROUP + j) * atoms, atoms)
            p = [picked[a * width : (a + 1) * width, span] for a in range(4)]
            r = [weights_all[a * width : (a + 1) * width, here] for a in range(4)]
            u = units(first, j)
            along = p[1] * u[0] + p[2] * u[1] + p[3] * u[2]
            totals[0] = totals[0] + (r[0] * p[0] + r[3] * along)
            q = r[1] * p[0]
            for a in range(3):
                totals[a + 1] = totals[a + 1] + (q * u[a] + r[2] * p[a + 1])
        for a in range(4):
            sums[a] += totals[a]
        return carry

    over_groups(slots // GROUP, forward, 0)

    scalar_sum = sums[0]
    vectors = [sums[1], sums[2], sums[3]]
    squares = vectors[0] * vectors[0] + vectors[1] * vectors[1] + vectors[2] * vectors[2]
    mixed = jnp.concatenate([scalar_sum, scalar_sum * scalar_sum, squares], axis=0)
    units_out = heads.shape[0] - 8
    readout_hidden = heads[:units_out]
    readout_linear, readout_out = heads[units_out : units_out + 1], heads[units_out + 1 : units_out + 2, :units_out]
    hidden_in = product(parts(readout_hidden), scalars[...]) + product((fold_high[...], fold_low[...]), mixed)
    hidden_gate = sigmoid(hidden_in)
    hidden = hidden_in * hidden_gate
    shift = heads[units_out + 2 : units_out + 3]
    energy[...] = shift + exact(readout_linear, scalars[...]) + exact(readout_out, hidden)
    hidden_pull = column(readout_out) * (hidden_gate + hidden * (1.0 - hidden_gate))
    scalar_pull[...] = exact(readout_hidden, hidden_pull, ((0,), (0,)))
    spread = product((back_high[...], back_low[...]), hidden_pull)
    double = 2.0 * spread[2 * width :]
    sums[0] = spread[:width] + 2.0 * scalar_sum * spread[width : 2 * width]
    for a in range(3):
        sums[a + 1] = vectors[a] * double
    pulled[...] = jnp.zeros_like(pulled)

    def backward(step, carry):
        first = step * GROUP
        at = span_of(step * GROUP * atoms, GROUP * atoms)
        highs, lows = [], []
        for j in range(GROUP):
            here = span_of((step * GROUP + j) * atoms, atoms)
            r = [weights_all[a * width : (a + 1) * width, here] for a in range(4)]
            u = units(first, j)
            ga = [sums[a] for a in range(4)]
            flow = ga[1] * u[0] + ga[2] * u[1] + ga[3] * u[2]
            pull = r[3] * ga[0]
            given = [r[0] * ga[0] + r[1] * flow] + [pull * u[a] + r[2] * ga[a + 1] for a in range(3)]
            high, low = parts(jnp.concatenate(given, axis=0))
            highs.append(high)
            lows.append(low)
        split = jnp.concatenate(highs + lows, axis=1)
        chosen = jnp.concatenate([onehot[:atoms, at], onehot[2 * atoms : 2 * atoms + ghost_rows, at]], axis=0)
        pulled[...] += dot_nt(jnp.concatenate([chosen, chosen], axis=1), split)
        return carry

    over_groups(slots // GROUP, backward, 0)
    own_pull[...] = pulled[:atoms]
    start = atoms
    fill = jnp.zeros((8, depth - extras.shape[2]), f32)
    half = back_sub.shape[0] // 2
    for out, offset, size, which in (
        (back_minus, 0, back_minus.shape[0], 1),
        (back_plus, 0, back_plus.shape[0], 0),
        (back_sub, 0, half, 3),
        (back_sub, half, half, 2),
    ):
        count = size - 8
        out[offset : offset + count] = pulled[start : start + count]
        out[offset + count : offset + size] = jnp.concatenate([extras[which], fill], axis=1)
        start += count


def window_kernel(
    slopes, outer_two, picked_all, weights_all, sums,
    geo, waves, kinds, scalar_pull, embedding, radial_in, radial_mid, radial_out, node_one, node_two, readout_linear,
    geo_pull, scalar_slope, vector_slope, vector_value, turned_high, turned_low, base,
):
    slots, atoms = kinds.shape
    width = node_one.shape[1]
    species_count, basis_count = embedding.shape[0], radial_in.shape[0]
    inner = weight_stack_t(radial_in[...])
    mid_a, mid_b = weight_stack(radial_mid[0]), weight_stack(radial_mid[1])
    outer = weight_stack_t(radial_out[...])
    lifted = species_matrix(node_one[0], embedding[...])
    scalar_mixing = jnp.concatenate([jnp.transpose(node_one[i]) for i in (1, 2, 3)], axis=0)
    base[...] = column(readout_linear[...]) + scalar_pull[...]
    turned = [scalar_mixing] + [jnp.transpose(m) for m in (node_two[1], node_one[4], node_one[5], node_two[0])]
    turned_high[...], turned_low[...] = parts(jnp.concatenate(turned, axis=0))

    def group(step, carry):
        first = step * GROUP
        at = span_of(step * GROUP * atoms, GROUP * atoms)
        h, dh = hidden[step]
        picked = picked_group(lifted, geo, kinds, first, species_count)
        weights_slope = dot(outer, value_stack(dh))
        scalar_slope[:, at] = weights_slope[:width] * picked
        vector_slope[:, at] = weights_slope[width:] * picked
        vector_value[:, at] = dot(outer[width:], value_stack(h)) * picked
        return carry

    def edge_group(step, carry):
        first = step * GROUP
        slope = dot(outer_two[...], slopes[:, span_of(step * GROUP * atoms, GROUP * atoms)])
        for j in range(GROUP):
            span = slice(j * atoms, (j + 1) * atoms)
            here = span_of((step * GROUP + j) * atoms, atoms)
            p = [picked_all[a * width : (a + 1) * width, here] for a in range(4)]
            r = [weights_all[a * width : (a + 1) * width, here] for a in (1, 3)]
            s = [slope[a * width : (a + 1) * width, span] for a in range(4)]
            u = [geo[a, pl.ds(first + j, 1), :] for a in range(3)]
            ga = [sums[a] for a in range(4)]
            along = p[1] * u[0] + p[2] * u[1] + p[3] * u[2]
            flow = ga[1] * u[0] + ga[2] * u[1] + ga[3] * u[2]
            cross = p[1] * ga[1] + p[2] * ga[2] + p[3] * ga[3]
            stretch = p[0] * (s[0] * ga[0] + s[1] * flow) + s[2] * cross + s[3] * (along * ga[0])
            geo_pull[0, pl.ds(first + j, 1), :] = jnp.sum(stretch, axis=0, keepdims=True)
            lean = r[0] * p[0]
            pull = r[1] * ga[0]
            for a in range(3):
                turn = lean * ga[a + 1] + pull * p[a + 1]
                geo_pull[a + 1, pl.ds(first + j, 1), :] = jnp.sum(turn, axis=0, keepdims=True)
        return carry

    values, slopes_in = (
        [basis_group(waves, i * GROUP, start, basis_count) for i in range(slots // GROUP)] for start in (0, basis_count)
    )
    works = [lambda i=i: edge_group(i, 0) for i in range(slots // GROUP)]
    hidden = hidden_pairs(values, slopes_in, inner, mid_a, mid_b, works)
    over_groups(slots // GROUP, group, 0)


def third_kernel(
    facts, geo, sums, geo_pull, own_pull, ret_minus, ret_plus, ret_sub,
    onehot, scalar_slope, vector_slope, vector_value, turned_high, turned_low, base,
    everyone, came,
    pieces, pulls, flat, *, moves, slab_rows, sub_rows,
):
    slots, atoms = geo.shape[1], geo.shape[2]
    width = sums.shape[1]
    half = sub_rows + 8
    ret_next, ret_prev = ret_sub.at[:half], ret_sub.at[half:]
    pick = send_onehot(facts, 0, slab_rows, sub_rows).astype(bf16)
    returned = jnp.concatenate(
        [ret_plus[:slab_rows], ret_minus[:slab_rows], ret_next[:sub_rows], ret_prev[:sub_rows]], axis=0
    )
    high, low = parts(returned)
    total = jnp.transpose(own_pull[...] + dot(pick, high) + dot(pick, low))
    x_pull = total[:width]
    y_pull = jnp.concatenate([total[a * width : (a + 1) * width] for a in (1, 2, 3)], axis=1)

    def turned(i, count=1):
        at = slice(i * width, (i + count) * width)
        return turned_high[at, :], turned_low[at, :]

    moved = product(turned(3), y_pull)
    gv = [moved[:, a * atoms : (a + 1) * atoms] for a in range(3)]
    scalar_sum, gate = sums[0], sums[4]
    vectors = [sums[1], sums[2], sums[3]]
    scalars = product(turned(6), x_pull) + base[...]
    spread = product(turned(0, 3), scalars)
    mixed = product(turned(4), moved)
    gated = product(turned(5), gv[0] * vectors[0] + gv[1] * vectors[1] + gv[2] * vectors[2])
    pulls[0] = spread[:width] + 2.0 * scalar_sum * spread[width : 2 * width] + gated
    double = 2.0 * spread[2 * width :]
    for a in range(3):
        pulls[a + 1] = vectors[a] * double + mixed[:, a * atoms : (a + 1) * atoms] + gate * gv[a]

    def contract(step, carry):
        first = step * GROUP
        for j in range(GROUP):
            here = span_of((step * GROUP + j) * atoms, atoms)
            row = pl.ds(first + j, 1)
            ga = [pulls[a] for a in range(4)]
            u = [geo[a, row, :] for a in range(3)]
            flow = ga[1] * u[0] + ga[2] * u[1] + ga[3] * u[2]
            stretch = scalar_slope[:, here] * ga[0] + vector_slope[:, here] * flow
            value = vector_value[:, here]
            flat[0, row, :] = jnp.sum(stretch, axis=0, keepdims=True)
            for a in range(3):
                flat[a + 1, row, :] = jnp.sum(value * ga[a + 1], axis=0, keepdims=True)
        return carry

    over_groups(slots // GROUP, contract, 0)
    stretch = flat[0] + geo_pull[0]
    turn = [flat[a + 1] + geo_pull[a + 1] for a in range(3)]
    u = [geo[a] for a in range(3)]
    inner = turn[0] * u[0] + turn[1] * u[1] + turn[2] * u[2]
    gradient = [stretch * u[a] + (turn[a] - inner * u[a]) * geo[5] for a in range(3)]
    at_row = iota((8, atoms), 0)
    own = jnp.zeros((8, atoms), f32)
    for a in range(3):
        flat[a] = gradient[a]
        own = jnp.where(at_row == a, jnp.sum(gradient[a], axis=0, keepdims=True), own)

    def push(step, carry):
        blocks = []
        for j in range(GROUP):
            row = pl.ds(step * GROUP + j, 1)
            block = jnp.where(at_row == 0, flat[0, row, :], jnp.where(at_row == 1, flat[1, row, :], flat[2, row, :]))
            blocks.append(block)
        block = jnp.concatenate(blocks, axis=1)
        top = block.astype(bf16).astype(f32)
        rest = block - top
        mid = rest.astype(bf16).astype(f32)
        split = jnp.concatenate([top, mid, rest - mid], axis=0).astype(bf16)
        at = span_of(step * GROUP * atoms, GROUP * atoms)
        chosen = jnp.concatenate([onehot[:atoms, at], onehot[2 * atoms : 2 * atoms + ghost_rows, at]], axis=0)
        return carry + dot_nt(chosen, split)

    ghost_rows = onehot.shape[0] // 2 - atoms
    zero = jnp.zeros((onehot.shape[0] // 2, 24), f32)
    pushed = over_groups(slots // GROUP, push, zero)
    pushed = jnp.transpose(pushed)
    pushed = (pushed[:8] + pushed[8:16] + pushed[16:]) * (1.0 / neighbor_norm)
    own = own - pushed[:, :atoms]
    velocities, mass = facts[1:4], facts[8:9]
    pieces[0:3] = (own * facts[7:8])[:3]
    blocks = ((ret_minus, slab_rows), (ret_plus, slab_rows), (ret_prev, sub_rows), (ret_next, sub_rows))
    start = atoms
    ghost_lines = [[0.0] * 3 for _ in range(3)]
    for i, (ref, count) in enumerate(blocks):
        told = ref[count : count + 8, :count]
        force = -pushed[:, start : start + count]
        start += count
        for a in range(3):
            for b in range(3):
                ghost_lines[a][b] = ghost_lines[a][b] + told[a + 1 : a + 2] * force[b : b + 1]
        scaled = force * told[7:8]
        top = scaled.astype(bf16).astype(f32)
        rest = scaled - top
        mid = rest.astype(bf16).astype(f32)
        split = jnp.concatenate([top, mid, rest - mid], axis=0).astype(bf16)
        place = (iota((atoms, count), 0) == told[0:1].astype(jnp.int32)).astype(bf16)
        spread = dot_nt(split, place)
        pieces[3 * i + 3 : 3 * i + 6] = (spread[:8] + spread[8:16] + spread[16:])[:3]
    came[...] = jnp.zeros_like(came)
    for i, (ref, count) in enumerate(blocks):
        came[:, i * moves : (i + 1) * moves] = ref[count : count + 8, atoms : atoms + moves]

    def line(a, b):
        start = velocities[a : a + 1] * velocities[b : b + 1] * mass
        mixed = velocities[a : a + 1] * own[b : b + 1] + velocities[b : b + 1] * own[a : a + 1]
        return start + time_step * mixed - jnp.sum(u[a] * geo[4] * gradient[b], axis=0, keepdims=True)

    lines = jnp.concatenate([line(a, b) for a in range(3) for b in range(3)] + [jnp.zeros((7, atoms), f32)], axis=0)
    ghosts = [time_step * (ghost_lines[a][b] + ghost_lines[b][a]) for a in range(3) for b in range(3)]
    ghosts = jnp.concatenate(ghosts + [jnp.zeros((7, slab_rows), f32)], axis=0)
    summed = jnp.sum(lines, axis=1, keepdims=True) + jnp.sum(ghosts, axis=1, keepdims=True)
    row = jnp.zeros((1, atoms), f32)
    for i in range(9):
        row = jnp.where(iota((1, atoms), 1) == i, summed[i : i + 1], row)
    pieces[15:16] = row
    for i in range(everyone.shape[0]):
        everyone[i] = pieces[...]


def determinant(m):
    return (
        m[0][0] * (m[1][1] * m[2][2] - m[1][2] * m[2][1])
        - m[0][1] * (m[1][0] * m[2][2] - m[1][2] * m[2][0])
        + m[0][2] * (m[1][0] * m[2][1] - m[1][1] * m[2][0])
    )


def inverse(m):
    whole = determinant(m)
    return [
        [
            (
                m[(j + 1) % 3][(i + 1) % 3] * m[(j + 2) % 3][(i + 2) % 3]
                - m[(j + 1) % 3][(i + 2) % 3] * m[(j + 2) % 3][(i + 1) % 3]
            )
            / whole
            for j in range(3)
        ]
        for i in range(3)
    ]


def fifth_kernel(
    pieces, own_facts, came, box, box_speed,
    forces_out, velocities_out, positions_out, arrivals, new_box, new_box_speed,
    whole, *, atoms_all, slab_count, sub_count,
):
    atoms = own_facts.shape[1]
    velocities, positions = own_facts[1:4], own_facts[4:7]
    devices = slab_count * sub_count
    sub = lax.rem(iota((devices, atoms), 0), sub_count)

    def row_of_all(r):
        return pieces[:, r, :]

    def piece(i, a):
        return row_of_all(3 * i + a)

    def moved(x, step):
        return pltpu.roll(x, (-step) % devices, 0)

    for a in range(3):
        total = piece(0, a) + moved(piece(1, a), sub_count) + moved(piece(2, a), -sub_count)
        x = piece(3, a)
        total = total + jnp.where(sub == sub_count - 1, moved(x, 1 - sub_count), moved(x, 1))
        x = piece(4, a)
        whole[a] = total + jnp.where(sub == 0, moved(x, sub_count - 1), moved(x, -1))
    squares = {}
    for a in range(3):
        for b in range(a, 3):
            squares[a, b] = jnp.sum(whole[a] * whole[b], axis=0, keepdims=True)
    order = list(squares)
    squares = jnp.concatenate([squares[k] for k in order] + [jnp.zeros((2, atoms), f32)], axis=0)
    squares = jnp.sum(squares, axis=1, keepdims=True)
    rest = jnp.sum(row_of_all(15), axis=0, keepdims=True)
    stress = [[None] * 3 for _ in range(3)]
    for i in range(3):
        for j in range(3):
            at = order.index((min(i, j), max(i, j)))
            stress[i][j] = rest[:, 3 * i + j : 3 * i + j + 1] + (time_step * time_step) * squares[at : at + 1]
    slab_at, sub_at = lax.axis_index("slab"), lax.axis_index("sub")
    mine = slab_at * sub_count + sub_at
    root, mass = own_facts[7:8], own_facts[8:9]
    for a in range(3):
        force = whole[a, pl.ds(mine, 1), :] * (mass * root)
        forces_out[a : a + 1, :] = force
        velocities_out[a : a + 1, :] = velocities[a : a + 1, :] + time_step * force / mass
    lane, row = iota((8, atoms), 1), iota((8, atoms), 0)
    facts = came[...]
    index = jnp.broadcast_to(facts[0:1].astype(jnp.int32), (8, atoms))
    count = arrivals.shape[1] // 4
    picked = jnp.zeros((8, atoms), f32)
    for i, (slab_step, sub_step) in enumerate(((-1, 0), (1, 0), (0, -1), (0, 1))):
        slab = lax.rem(slab_at + (slab_step + slab_count), slab_count)
        source = slab * sub_count + lax.rem(sub_at + (sub_step + sub_count), sub_count)
        force = [whole[a, pl.ds(source, 1), :] for a in range(3)]
        force = jnp.where(row == 0, force[0], jnp.where(row == 1, force[1], force[2]))
        found = jnp.take_along_axis(force, index, axis=1)
        picked = jnp.where((lane >= i * count) & (lane < (i + 1) * count), found, picked)
    speeds = [facts[1 + a : 2 + a] + time_step * picked[a : a + 1] * facts[7:8] for a in range(3)]

    def spread(value):
        return jnp.full((1, atoms), value, f32)

    old = [[spread(box[i, j]) for j in range(3)] for i in range(3)]
    volume = determinant(old)
    old_inverse = inverse(old)
    for i in range(3):
        stress[i][i] = stress[i][i] - outside_pressure * volume
    fresh = [[None] * 3 for _ in range(3)]
    for i in range(3):
        for j in range(3):
            push = stress[i][0] * old_inverse[j][0] + stress[i][1] * old_inverse[j][1] + stress[i][2] * old_inverse[j][2]
            speed = spread(box_speed[i, j]) + time_step * push / (box_mass * atoms_all)
            fresh[i][j] = old[i][j] + time_step * speed
            new_box_speed[i : i + 1, j : j + 1] = speed[:, :1]
            new_box[i : i + 1, j : j + 1] = fresh[i][j][:, :1]
    new_inverse = inverse(fresh)
    for i in range(3):
        move = sum(new_inverse[i][j] * velocities_out[j : j + 1, :] for j in range(3))
        positions_out[i : i + 1, :] = positions[i : i + 1, :] + time_step * move
    for i in range(3):
        move = sum(new_inverse[i][j] * speeds[j] for j in range(3))
        arrivals[i : i + 1, :] = (facts[4 + i : 5 + i] + time_step * move)[:, : 4 * count]
        arrivals[3 + i : 4 + i, :] = speeds[i][:, : 4 * count]


VM = pl.BlockSpec(memory_space=pltpu.VMEM)
HB = pl.BlockSpec(memory_space=pltpu.HBM)
SM = pl.BlockSpec(memory_space=pltpu.SMEM)


def shape(*dims, dtype=f32):
    return jax.ShapeDtypeStruct(dims, dtype)


def call(kernel, outs, scalar_inputs=(), far_inputs=False, far_outputs=(), scratch=(), flops=0, vmem=16, name=None):
    def run(*args):
        moved = sum(math.prod(x.shape) * x.dtype.itemsize for x in list(args) + list(outs))
        return pl.pallas_call(
            kernel,
            out_shape=tuple(outs),
            in_specs=[HB if far_inputs else SM if i in scalar_inputs else VM for i in range(len(args))],
            out_specs=tuple(HB if i in far_outputs else VM for i in range(len(outs))),
            scratch_shapes=list(scratch),
            compiler_params=pltpu.CompilerParams(vmem_limit_bytes=vmem * 1024 * 1024),
            cost_estimate=pl.CostEstimate(flops=flops, bytes_accessed=moved, transcendentals=0),
            name=name,
        )(*args)

    return run


def body(
    positions, velocities, species, ghost_species, neighbours, slot_mask, edge_vectors, send_slab, send_sub, migrants,
    embedding, energy_shift, masses, radial_one_in, radial_one_mid, radial_one_out, node_one,
    radial_two_in, radial_two_mid, radial_two_out, node_two, readout_linear, readout_hidden, readout_out,
    box_matrix, box_velocity,
):
    slots, atoms = neighbours.shape
    width = node_one.shape[1]
    hidden = radial_one_mid.shape[1]
    depth = 4 * width
    ghost_slab, ghost_sub = send_slab.shape[1], send_sub.shape[1]
    extended = atoms + 2 * ghost_slab + 2 * ghost_sub
    edges = slots * atoms
    devices = lax.axis_size("slab") * lax.axis_size("sub")
    species_row = species.reshape(1, atoms)
    ghost_row = ghost_species.reshape(1, -1)
    linear_row = readout_linear.reshape(1, -1)
    out_row = readout_out.reshape(1, -1)
    radial_one_in, radial_one_out = jnp.transpose(radial_one_in), jnp.transpose(radial_one_out)
    radial_two_in, radial_two_out = jnp.transpose(radial_two_in), jnp.transpose(radial_two_out)

    first_inputs = (
        edge_vectors, slot_mask, neighbours, species_row, ghost_row, embedding,
        radial_one_in, radial_one_mid, radial_one_out, node_one, send_slab, send_sub,
        velocities, positions, migrants, masses.reshape(1, -1), energy_shift.reshape(1, -1),
        readout_hidden, linear_row, out_row, radial_two_in, radial_two_mid, radial_two_out, node_two,
    )
    packed_rows = (
        8 * width + 6 * packed_step(slots) + FACTS + 6 * hidden + radial_two_in.shape[0] + packed_step(slots)
        + readout_hidden.shape[0] + 8 + 2 * radial_one_in.shape[0] * packed_step(slots)
    )
    kinds, sums, packed, to_minus, to_plus, to_sub = call(
        first_kernel,
        (
            shape(slots, atoms, dtype=jnp.int32),
            shape(5, width, atoms),
            shape(packed_rows, atoms),
            shape(ghost_slab, depth),
            shape(ghost_slab, depth),
            shape(2 * ghost_sub, depth),
        ),
        far_inputs=True,
        far_outputs=(1, 2),
        scratch=(
            pltpu.VMEM((6, slots, atoms), f32),
            pltpu.VMEM((2 * radial_one_in.shape[0], slots, atoms), f32),
            pltpu.VMEM((packed_rows, atoms), f32),
            pltpu.VMEM((5, width, atoms), f32),
        )
        + tuple(pltpu.VMEM(x.shape, x.dtype) for x in first_inputs)
        + (pltpu.SemaphoreType.DMA((FIRST_INPUTS,)), pltpu.SemaphoreType.DMA((4,))),
        flops=6 * edges * 26000,
        vmem=56,
        name="layer_one",
    )(
        *first_inputs
    )
    from_minus, from_plus, from_sub = trade(to_minus, to_plus, to_sub, 1)

    def radial(*refs):
        radial_kernel(
            *refs,
            slab_rows=ghost_slab,
            sub_rows=ghost_sub,
            moves=migrants.shape[1],
            basis_count=radial_two_in.shape[0],
        )

    (
        weights_all, slopes, onehot, outer, fold_high, fold_low, back_high, back_low,
        geo, picked_own, scalars, extras, facts, heads, waves,
    ) = call(
        radial,
        (
            shape(depth, edges),
            shape(3 * hidden, edges, dtype=bf16),
            shape(2 * extended, edges, dtype=bf16),
            shape(depth, 3 * hidden, dtype=bf16),
            shape(readout_hidden.shape[0], 3 * width, dtype=bf16),
            shape(readout_hidden.shape[0], 3 * width, dtype=bf16),
            shape(3 * width, readout_hidden.shape[0], dtype=bf16),
            shape(3 * width, readout_hidden.shape[0], dtype=bf16),
            shape(6, slots, atoms),
            shape(depth, edges),
            shape(width, atoms),
            shape(4, 8, 2 * atoms),
            shape(FACTS, atoms),
            shape(readout_hidden.shape[0] + 8, atoms),
            shape(2 * radial_two_in.shape[0], slots, atoms),
        ),
        flops=12 * edges * 10000,
        vmem=16,
        name="radial_two",
    )(
        packed,
    )

    energy, scalar_pull, picked_all, pulls, own_pull, back_minus, back_plus, back_sub = call(
        second_kernel,
        (
            shape(1, atoms),
            shape(width, atoms),
            shape(depth, edges),
            shape(4, width, atoms),
            shape(atoms, depth),
            shape(ghost_slab + 8, depth),
            shape(ghost_slab + 8, depth),
            shape(2 * (ghost_sub + 8), depth),
        ),
        scratch=(
            pltpu.VMEM((depth, 2 * (extended - atoms)), bf16),
            pltpu.VMEM((extended, depth), f32),
        ),
        flops=4 * edges * depth * extended * 2,
        vmem=20,
        name="layer_two",
    )(
        geo, picked_own, from_minus, from_plus, from_sub, scalars, extras,
        weights_all, onehot, fold_high, fold_low, back_high, back_low, heads,
    )
    ret_minus, ret_plus, ret_sub = trade(back_minus, back_plus, back_sub, -1)
    geo_pull, scalar_slope, vector_slope, vector_value, turned_high, turned_low, base = call(
        window_kernel,
        (
            shape(4, slots, atoms),
            shape(width, edges),
            shape(width, edges),
            shape(width, edges),
            shape(7 * width, width, dtype=bf16),
            shape(7 * width, width, dtype=bf16),
            shape(width, atoms),
        ),
        flops=12 * edges * 12000,
        vmem=20,
        name="radial_one",
    )(
        slopes, outer, picked_all, weights_all, pulls,
        geo, waves, kinds, scalar_pull, embedding,
        radial_one_in, radial_one_mid, radial_one_out, node_one, node_two, linear_row,
    )

    def back(*refs):
        third_kernel(*refs, moves=migrants.shape[1], slab_rows=ghost_slab, sub_rows=ghost_sub)

    everyone, came = call(
        back,
        (shape(devices, 16, atoms), shape(8, atoms)),
        scratch=(
            pltpu.VMEM((16, atoms), f32),
            pltpu.VMEM((4, width, atoms), f32),
            pltpu.VMEM((4, slots, atoms), f32),
        ),
        flops=6 * edges * 1000,
        vmem=12,
        name="layer_one_back",
    )(
        facts, geo, sums, geo_pull, own_pull, ret_minus, ret_plus, ret_sub,
        onehot, scalar_slope, vector_slope, vector_value, turned_high, turned_low, base,
    )
    everyone = lax.all_to_all(everyone, ("slab", "sub"), 0, 0, tiled=True)

    def last(*refs):
        fifth_kernel(
            *refs, atoms_all=atoms * devices, slab_count=lax.axis_size("slab"), sub_count=lax.axis_size("sub")
        )

    forces, new_velocities, new_positions, arrivals, new_box, new_box_velocity = call(
        last,
        (
            shape(3, atoms), shape(3, atoms), shape(3, atoms), shape(6, 4 * migrants.shape[1]),
            shape(3, 3), shape(3, 3),
        ),
        scalar_inputs=(3, 4),
        scratch=(pltpu.VMEM((3, devices, atoms), f32),),
        flops=1000000,
        vmem=8,
        name="box",
    )(everyone, facts, came, box_matrix, box_velocity)
    return energy.reshape(atoms), forces, new_velocities, new_positions, arrivals, new_box, new_box_velocity


def solution(mesh):
    split = ("slab", "sub")
    one, two, three, copied = P(split), P(None, split), P(None, None, split), P()
    placed = (two, two, one, one, two, two, three, two, two, two) + (copied,) * 16
    return jax.shard_map(
        body,
        mesh=mesh,
        in_specs=placed,
        out_specs=(one, two, two, two, two, copied, copied),
        check_vma=False,
    )
```

```python
import math

import jax
import jax.numpy as jnp
from jax import lax
from jax.experimental import pallas as pl
from jax.experimental.pallas import tpu as pltpu
from jax.sharding import PartitionSpec as P

cutoff = 5.0
neighbor_norm = 0.125
time_step = 0.5
outside_pressure = 0.5
box_mass = 0.125
highest = lax.Precision.HIGHEST
f32 = jnp.float32
bf16 = jnp.bfloat16
GROUP = 4


def shifted(block, axis, distance):
    count = lax.axis_size(axis)
    return lax.ppermute(block, axis, [((i - distance) % count, i) for i in range(count)])


def trade(to_minus, to_plus, to_sub, first):
    from_minus, from_plus = shifted(to_plus, "slab", 1), shifted(to_minus, "slab", -1)
    if lax.axis_size("sub") == 2:
        return from_minus, from_plus, shifted(to_sub, "sub", 1)
    one, two = jnp.split(to_sub, 2, axis=0)
    from_sub = jnp.concatenate([shifted(one, "sub", first), shifted(two, "sub", -first)], axis=0)
    return from_minus, from_plus, from_sub


def parts(x):
    high = x.astype(bf16)
    return high, (x - high.astype(f32)).astype(bf16)


def dot(a, b):
    return jnp.dot(a, b, preferred_element_type=f32)


def dot_nt(a, b):
    return lax.dot_general(a, b, (((1,), (1,)), ((), ())), preferred_element_type=f32)


def exact(a, b, dims=((1,), (0,))):
    return lax.dot_general(a, b, (dims, ((), ())), precision=highest, preferred_element_type=f32)


def product(weight, x):
    high, low = parts(x)
    return dot(weight[0], high) + dot(weight[0], low) + dot(weight[1], high)


def weight_stack(w):
    high = w.astype(bf16).astype(f32)
    return jnp.concatenate([high, high, w - high], axis=1).astype(bf16)


def weight_stack_t(w):
    high = w.astype(bf16).astype(f32)
    return jnp.transpose(jnp.concatenate([high, high, w - high], axis=0)).astype(bf16)


def value_stack(x):
    high, low = parts(x)
    return jnp.concatenate([high, low, high], axis=0)


def value_stack_small(x):
    high = x.astype(bf16).astype(f32)
    return jnp.concatenate([high, x - high, high], axis=0).astype(bf16)


def over_groups(count, step, carry):
    for i in range(count):
        carry = step(i, carry)
    return carry


def span_of(first, count):
    if isinstance(first, int):
        return pl.ds(first, count)
    return pl.ds(pl.multiple_of(first, count), count)


def iota(shape, axis):
    return lax.broadcasted_iota(jnp.int32, shape, axis)


def column(row):
    n = row.shape[1]
    return jnp.sum(jnp.where(iota((n, n), 0) == iota((n, n), 1), row, 0.0), axis=1, keepdims=True)


def sigmoid(x):
    return 0.5 + 0.5 * jnp.tanh(0.5 * x)


def basis(distance, inverse_distance, count):
    scaled = distance * (1.0 / cutoff)
    second = scaled * scaled
    fourth = second * second
    fifth = fourth * scaled
    sixth = fourth * second
    scale = math.sqrt(2.0 / cutoff)
    envelope = 1.0 + sixth * (-28.0 + scaled * (48.0 - 21.0 * scaled))
    front = scale * envelope * inverse_distance
    slope_envelope = fifth * (-168.0 + scaled * (336.0 - 168.0 * scaled)) * (1.0 / cutoff)
    slope_front = scale * inverse_distance * (slope_envelope - envelope * inverse_distance)
    angle = math.pi * scaled
    first_sine, first_cosine = jnp.sin(angle), jnp.cos(angle)
    sine, cosine = first_sine, first_cosine
    values, slopes = [], []
    for order in range(1, count + 1):
        if order > 1:
            sine, cosine = (
                sine * first_cosine + cosine * first_sine,
                cosine * first_cosine - sine * first_sine,
            )
        values.append(sine * front)
        slopes.append(sine * slope_front + cosine * (front * (order * math.pi / cutoff)))
    return values, slopes


def basis_group(waves, first, start, count):
    return jnp.concatenate([waves[start : start + count, first + j, :] for j in range(GROUP)], axis=1)


def hidden_values(values, inner, mid_a, mid_b):
    xs = [dot(inner, value_stack_small(value)) for value in values]
    for mid in (mid_a, mid_b):
        xs = [dot(mid, value_stack(x * sigmoid(x))) for x in xs]
    return [x * sigmoid(x) for x in xs]


def hidden_pairs(values, slopes, inner, mid_a, mid_b, between=()):
    between = list(between)

    def activated(x, dx):
        gate = sigmoid(x)
        h = x * gate
        return h, (gate + h * (1.0 - gate)) * dx

    pairs = [
        (dot(inner, value_stack_small(value)), dot(inner, value_stack_small(slope)))
        for value, slope in zip(values, slopes)
    ]
    for mid in (mid_a, mid_b):
        after = []
        for i, (x, dx) in enumerate(pairs):
            h, dh = activated(x, dx)
            after.append((dot(mid, value_stack(h)), dot(mid, value_stack(dh))))
            if between and i % 2:
                between.pop(0)()
        pairs = after
    pairs = [activated(x, dx) for x, dx in pairs]
    for work in between:
        work()
    return pairs


def species_matrix(first_mixing, embedding):
    lifted = exact(first_mixing, embedding, ((1,), (1,)))
    high = lifted.astype(bf16).astype(f32)
    rest = lifted - high
    mid = rest.astype(bf16).astype(f32)
    return jnp.concatenate([high, mid, rest - mid], axis=1).astype(bf16)


def picked_group(lifted, geo, kinds, first, species_count):
    blocks = []
    for j in range(GROUP):
        kind = kinds[pl.ds(first + j, 1), :]
        weight = geo[3, pl.ds(first + j, 1), :]
        blocks.append(jnp.where(iota((species_count, kind.shape[1]), 0) == kind, weight, 0.0))
    block = jnp.concatenate(blocks, axis=1)
    return dot(lifted, jnp.concatenate([block, block, block], axis=0).astype(bf16))


def send_onehot(facts, first, slab_rows, sub_rows):
    atoms = facts.shape[1]
    lengths = (slab_rows, slab_rows, sub_rows, sub_rows)
    rows = [facts[first + 9 + i : first + 10 + i, :n] for i, n in enumerate(lengths)]
    rows = jnp.concatenate(rows, axis=1)
    return (iota((atoms, rows.shape[1]), 0).astype(f32) == rows).astype(f32)


FIRST_INPUTS = 24
FACTS = 16


def packed_step(slots):
    return -(-slots // 8) * 8


def first_kernel(
    *refs,
):
    count = FIRST_INPUTS
    buffers, ready, gone = refs[-count - 2 : -2], refs[-2], refs[-1]
    copies = [pltpu.make_async_copy(refs[i], buffers[i], ready.at[i]) for i in range(count)]
    for copy in copies:
        copy.start()
    (
        edges, mask, neighbours, species, ghosts, embedding, radial_in, radial_mid, radial_out, node_one,
        send_slab, send_sub, velocities, positions, migrants, masses, shifts,
        hidden_head, linear_head, out_head, next_in, next_mid, next_out, node_two,
    ) = buffers
    (
        kinds, far_sums, far_packed, to_minus, to_plus, to_sub,
        geo, waves, packed, sums,
    ) = refs[count : -count - 2]
    for copy in copies[:2]:
        copy.wait()
    slots, atoms = mask.shape
    width = node_one.shape[1]
    species_count, basis_count = embedding.shape[0], radial_in.shape[0]
    ex, ey, ez = edges[0], edges[1], edges[2]
    square = ex * ex + ey * ey + ez * ez
    distance = jnp.sqrt(square)
    inverse_distance = 1.0 / distance
    for a, e in enumerate((ex, ey, ez)):
        geo[a] = e * inverse_distance
    geo[3] = mask[...].astype(f32) * neighbor_norm
    geo[4] = distance
    geo[5] = inverse_distance
    base = 5 * width
    step = packed_step(slots)
    values, slopes = basis(distance, inverse_distance, radial_in.shape[0])
    for i, wave in enumerate(values + slopes):
        waves[i] = wave
    for a in range(6):
        packed[base + a * step : base + a * step + slots] = geo[a]
    for copy in copies[2:5]:
        copy.wait()
    ghost_row = ghosts[...]
    extra = -ghost_row.shape[1] % atoms
    if extra:
        ghost_row = jnp.concatenate([ghost_row, jnp.zeros((1, extra), jnp.int32)], axis=1)
    tables = [species[...]] + [ghost_row[:, i : i + atoms] for i in range(0, ghost_row.shape[1], atoms)]
    pad = -slots % 8
    rows = neighbours[...]
    if pad:
        rows = jnp.concatenate([rows, jnp.zeros((pad, atoms), jnp.int32)], axis=0)
    inner_index = lax.rem(rows, atoms)
    block_index = lax.div(rows, atoms)
    found = jnp.zeros_like(rows)
    for i, table in enumerate(tables):
        spread = jnp.broadcast_to(table, rows.shape)
        got = jnp.take_along_axis(spread, inner_index, axis=1)
        found = jnp.where(block_index == i, got, found)
    kinds[...] = found[:slots]

    for copy in copies[5:10]:
        copy.wait()
    inner = weight_stack_t(radial_in[...])
    mid_a, mid_b = weight_stack(radial_mid[0]), weight_stack(radial_mid[1])
    outer = weight_stack_t(radial_out[...])
    lifted = species_matrix(node_one[0], embedding[...])
    sums[...] = jnp.zeros_like(sums)

    values = [basis_group(waves, i * GROUP, 0, basis_count) for i in range(slots // GROUP)]
    hidden = hidden_values(values, inner, mid_a, mid_b)

    def multiplied(step):
        if step == slots // GROUP:
            return None
        weights = dot(outer, value_stack(hidden[step]))
        return weights, picked_group(lifted, geo, kinds, step * GROUP, species_count)

    def group(step, carry):
        first = step * GROUP
        weights, picked = carry
        carry = multiplied(step + 1)
        totals = [0.0] * 4
        for j in range(GROUP):
            at = slice(j * atoms, (j + 1) * atoms)
            p = picked[:, at]
            totals[0] = totals[0] + weights[:width, at] * p
            q = weights[width:, at] * p
            for a in range(3):
                totals[a + 1] = totals[a + 1] + q * geo[a, pl.ds(first + j, 1), :]
        for a in range(4):
            sums[a] += totals[a]
        return carry

    over_groups(slots // GROUP, group, multiplied(0))

    early_sums = pltpu.make_async_copy(sums.at[:4], far_sums.at[:4], gone.at[2])
    early_sums.start()
    for copy in copies[10:]:
        copy.wait()
    mass = shift = jnp.zeros((1, atoms), f32)
    for i in range(masses.shape[1]):
        mass = jnp.where(species[...] == i, masses[:, i : i + 1], mass)
        shift = jnp.where(species[...] == i, shifts[:, i : i + 1], shift)
    facts = base + 6 * step
    packed[facts : facts + 1] = iota((1, atoms), 1).astype(f32)
    packed[facts + 1 : facts + 4] = velocities[...]
    packed[facts + 4 : facts + 7] = positions[...]
    packed[facts + 7 : facts + 8] = 1.0 / jnp.sqrt(mass)
    packed[facts + 8 : facts + 9] = mass
    packed[facts + 9 : facts + FACTS] = jnp.zeros((FACTS - 9, atoms), f32)
    for i, (lists, at) in enumerate(((send_slab, 1), (send_slab, 0), (send_sub, 1), (send_sub, 0))):
        packed[facts + 9 + i : facts + 10 + i, : lists.shape[1]] = lists[at : at + 1, :].astype(f32)
    count = migrants.shape[1]
    for i, at in enumerate((1, 0, 3, 2)):
        packed[facts + 13 : facts + 14, i * count : (i + 1) * count] = migrants[at : at + 1, :].astype(f32)
    inner_rows = next_mid.shape[1]
    start = facts + FACTS
    for i in range(3):
        packed[start : start + width] = node_two[i + 2]
        start += width
    for i in range(next_out.shape[1] // atoms):
        packed[start : start + inner_rows] = next_out[:, i * atoms : (i + 1) * atoms]
        start += inner_rows
    for i in range(2):
        packed[start : start + inner_rows, :inner_rows] = next_mid[i]
        start += inner_rows
    packed[start : start + next_in.shape[0], :inner_rows] = next_in[...]
    start += next_in.shape[0]
    packed[start : start + slots] = neighbours[...].astype(f32)
    start += step
    count = hidden_head.shape[0]
    packed[start : start + count] = hidden_head[...]
    packed[start + count : start + count + 1] = linear_head[...]
    packed[start + count + 1 : start + count + 2, : out_head.shape[1]] = out_head[...]
    packed[start + count + 2 : start + count + 3] = shift
    start += count + 8
    for i in range(waves.shape[0]):
        packed[start + i * step : start + i * step + slots] = waves[i]
    early = pltpu.make_async_copy(packed.at[base:], far_packed.at[base:], gone.at[0])
    early.start()
    own_onehot = (iota((species_count, atoms), 0) == species[...]).astype(f32)
    own = exact(embedding[...], own_onehot, ((0,), (0,)))
    scalar_sum = sums[0]
    vectors = [sums[1], sums[2], sums[3]]
    squares = vectors[0] * vectors[0] + vectors[1] * vectors[1] + vectors[2] * vectors[2]
    scalars = (
        own
        + product(parts(node_one[1]), scalar_sum)
        + product(parts(node_one[2]), scalar_sum * scalar_sum)
        + product(parts(node_one[3]), squares)
    )
    gate = product(parts(node_one[5]), scalar_sum)
    sums[4] = gate
    late_sums = pltpu.make_async_copy(sums.at[4:], far_sums.at[4:], gone.at[3])
    late_sums.start()
    turned = product(parts(node_one[4]), jnp.concatenate(vectors, axis=1))
    moved = turned + jnp.concatenate([gate * v for v in vectors], axis=1)
    packed[:width] = scalars
    x = product(parts(node_two[0]), scalars)
    y = product(parts(node_two[1]), moved)
    table = jnp.concatenate([x] + [y[:, a * atoms : (a + 1) * atoms] for a in range(3)], axis=0)
    packed[width : 5 * width] = table
    late = pltpu.make_async_copy(packed.at[:base], far_packed.at[:base], gone.at[1])
    late.start()
    pick = send_onehot(packed, facts, send_slab.shape[1], send_sub.shape[1]).astype(bf16)
    high, low = parts(table)
    sent = jnp.transpose(dot(high, pick) + dot(low, pick))
    slab_rows = send_slab.shape[1]
    to_plus[...] = sent[:slab_rows]
    to_minus[...] = sent[slab_rows : 2 * slab_rows]
    to_sub[...] = sent[2 * slab_rows :]
    for copy in (early, late, early_sums, late_sums):
        copy.wait()


def radial_kernel(
    packed,
    weights_all, slopes, onehot, outer, fold_high, fold_low, back_high, back_low,
    geo, picked_own, scalars, extras, facts, heads, waves, *, slab_rows, sub_rows, moves, basis_count,
):
    slots, atoms = geo.shape[1:]
    width = scalars.shape[0]
    depth = 4 * width
    inner_rows = slopes.shape[0] // 3
    scalars[...] = packed[:width]
    first_fact = 5 * width + 6 * packed_step(slots)
    start = first_fact + FACTS
    mixings = [packed[start + i * width : start + (i + 1) * width] for i in range(3)]
    start += 3 * width
    pieces = depth // atoms
    radial_out = [packed[start + i * inner_rows : start + (i + 1) * inner_rows] for i in range(pieces)]
    radial_out = jnp.concatenate(radial_out, axis=1)
    start += pieces * inner_rows
    radial_mid = [packed[start + i * inner_rows : start + (i + 1) * inner_rows, :inner_rows] for i in range(2)]
    start += 2 * inner_rows
    radial_in = packed[start : start + basis_count, :inner_rows]
    first_row = start + basis_count
    start = first_row + packed_step(slots)
    heads[...] = packed[start : start + heads.shape[0]]
    start += heads.shape[0]
    for i in range(2 * basis_count):
        waves[i] = packed[start + i * packed_step(slots) : start + i * packed_step(slots) + slots]
    table = jnp.concatenate(parts(packed[width : 5 * width]), axis=1)
    for a in range(6):
        start = 5 * width + a * packed_step(slots)
        geo[a] = packed[start : start + slots]
    facts[...] = packed[first_fact : first_fact + FACTS]
    listed = exact(facts[:8], send_onehot(facts, 0, slab_rows, sub_rows))
    moving = exact(facts[:8], (iota((atoms, 4 * moves), 0).astype(f32) == facts[13:14, : 4 * moves]).astype(f32))
    start = 0
    extras[...] = jnp.zeros_like(extras)
    for i, length in enumerate((slab_rows, slab_rows, sub_rows, sub_rows)):
        extras[i, :, :length] = listed[:, start : start + length]
        extras[i, :, atoms : atoms + moves] = moving[:, i * moves : (i + 1) * moves]
        start += length
    rows = onehot.shape[0] // 2
    outer[...] = weight_stack_t(radial_out)
    folded = product(parts(heads[: heads.shape[0] - 8]), jnp.concatenate(mixings, axis=1))
    fold_high[...], fold_low[...] = parts(folded)
    back_high[...], back_low[...] = parts(jnp.transpose(folded))
    inner = weight_stack_t(radial_in)
    mid_a, mid_b = weight_stack(radial_mid[0]), weight_stack(radial_mid[1])

    values, slopes_in = (
        [basis_group(waves, i * GROUP, start, basis_count) for i in range(slots // GROUP)] for start in (0, basis_count)
    )
    hidden = hidden_pairs(values, slopes_in, inner, mid_a, mid_b)

    def group(step, carry):
        first = step * GROUP
        at = span_of(step * GROUP * atoms, GROUP * atoms)
        h, dh = hidden[step]
        slopes[:, at] = value_stack(dh)
        blocks = []
        for j in range(GROUP):
            row = packed[first_row + first + j : first_row + first + j + 1]
            weight = geo[3, pl.ds(first + j, 1), :]
            row = row.astype(jnp.int32)
            blocks.append(jnp.where(iota((rows, atoms), 0) == row, weight, 0.0).astype(bf16))
        block = jnp.concatenate(blocks, axis=1)
        own, ghosts = block[:atoms], block[atoms:]
        both = jnp.concatenate([own, own], axis=0)
        onehot[:, at] = jnp.concatenate([both, ghosts, ghosts], axis=0)
        picked_own[:, at] = dot(table, both)
        weights_all[:, at] = dot(outer[...], value_stack(h))
        return carry

    over_groups(slots // GROUP, group, 0)


def second_kernel(
    geo, picked_own, from_minus, from_plus, from_sub, scalars, extras,
    weights_all, onehot, fold_high, fold_low, back_high, back_low, heads,
    energy, scalar_pull, picked_all, sums, own_pull, back_minus, back_plus, back_sub,
    table, pulled,
):
    slots, atoms = geo.shape[1], geo.shape[2]
    width = scalars.shape[0]
    depth = 4 * width
    ghosts = jnp.concatenate([from_minus[...], from_plus[...], from_sub[...]], axis=0)
    high = ghosts.astype(bf16).astype(f32)
    table[...] = jnp.transpose(jnp.concatenate([high, ghosts - high], axis=0)).astype(bf16)
    ghost_rows = ghosts.shape[0]
    sums[...] = jnp.zeros_like(sums)

    def units(first, j):
        return [geo[a, pl.ds(first + j, 1), :] for a in range(3)]

    def gathered(step):
        if step == slots // GROUP:
            return None
        return dot(table[...], onehot[2 * atoms :, span_of(step * GROUP * atoms, GROUP * atoms)])

    def forward(step, carry):
        first = step * GROUP
        at = span_of(step * GROUP * atoms, GROUP * atoms)
        picked = picked_own[:, at] + carry
        picked_all[:, at] = picked
        carry = gathered(step + 1)
        totals = [0.0] * 4
        for j in range(GROUP):
            span = slice(j * atoms, (j + 1) * atoms)
            here = span_of((step * GROUP + j) * atoms, atoms)
            p = [picked[a * width : (a + 1) * width, span] for a in range(4)]
            r = [weights_all[a * width : (a + 1) * width, here] for a in range(4)]
            u = units(first, j)
            along = p[1] * u[0] + p[2] * u[1] + p[3] * u[2]
            totals[0] = totals[0] + (r[0] * p[0] + r[3] * along)
            q = r[1] * p[0]
            for a in range(3):
                totals[a + 1] = totals[a + 1] + (q * u[a] + r[2] * p[a + 1])
        for a in range(4):
            sums[a] += totals[a]
        return carry

    over_groups(slots // GROUP, forward, gathered(0))

    scalar_sum = sums[0]
    vectors = [sums[1], sums[2], sums[3]]
    squares = vectors[0] * vectors[0] + vectors[1] * vectors[1] + vectors[2] * vectors[2]
    mixed = jnp.concatenate([scalar_sum, scalar_sum * scalar_sum, squares], axis=0)
    units_out = heads.shape[0] - 8
    readout_hidden = heads[:units_out]
    readout_linear, readout_out = heads[units_out : units_out + 1], heads[units_out + 1 : units_out + 2, :units_out]
    hidden_in = product(parts(readout_hidden), scalars[...]) + product((fold_high[...], fold_low[...]), mixed)
    hidden_gate = sigmoid(hidden_in)
    hidden = hidden_in * hidden_gate
    shift = heads[units_out + 2 : units_out + 3]
    energy[...] = shift + exact(readout_linear, scalars[...]) + exact(readout_out, hidden)
    hidden_pull = column(readout_out) * (hidden_gate + hidden * (1.0 - hidden_gate))
    scalar_pull[...] = exact(readout_hidden, hidden_pull, ((0,), (0,)))
    spread = product((back_high[...], back_low[...]), hidden_pull)
    double = 2.0 * spread[2 * width :]
    sums[0] = spread[:width] + 2.0 * scalar_sum * spread[width : 2 * width]
    for a in range(3):
        sums[a + 1] = vectors[a] * double
    pulled[...] = jnp.zeros_like(pulled)

    def scatter(at, split):
        chosen = jnp.concatenate([onehot[:atoms, at], onehot[2 * atoms : 2 * atoms + ghost_rows, at]], axis=0)
        pulled[...] += dot_nt(jnp.concatenate([chosen, chosen], axis=1), split)

    def backward(step, carry):
        first = step * GROUP
        at = span_of(step * GROUP * atoms, GROUP * atoms)
        highs, lows = [], []
        for j in range(GROUP):
            here = span_of((step * GROUP + j) * atoms, atoms)
            r = [weights_all[a * width : (a + 1) * width, here] for a in range(4)]
            u = units(first, j)
            ga = [sums[a] for a in range(4)]
            flow = ga[1] * u[0] + ga[2] * u[1] + ga[3] * u[2]
            pull = r[3] * ga[0]
            given = [r[0] * ga[0] + r[1] * flow] + [pull * u[a] + r[2] * ga[a + 1] for a in range(3)]
            high, low = parts(jnp.concatenate(given, axis=0))
            highs.append(high)
            lows.append(low)
        if carry is not None:
            scatter(*carry)
        return at, jnp.concatenate(highs + lows, axis=1)

    scatter(*over_groups(slots // GROUP, backward, None))
    own_pull[...] = pulled[:atoms]
    start = atoms
    fill = jnp.zeros((8, depth - extras.shape[2]), f32)
    half = back_sub.shape[0] // 2
    for out, offset, size, which in (
        (back_minus, 0, back_minus.shape[0], 1),
        (back_plus, 0, back_plus.shape[0], 0),
        (back_sub, 0, half, 3),
        (back_sub, half, half, 2),
    ):
        count = size - 8
        out[offset : offset + count] = pulled[start : start + count]
        out[offset + count : offset + size] = jnp.concatenate([extras[which], fill], axis=1)
        start += count


def window_kernel(
    slopes, outer_two, picked_all, weights_all, sums,
    geo, waves, kinds, scalar_pull, embedding, radial_in, radial_mid, radial_out, node_one, node_two, readout_linear,
    geo_pull, scalar_slope, vector_slope, vector_value, turned_high, turned_low, base,
):
    slots, atoms = kinds.shape
    width = node_one.shape[1]
    species_count, basis_count = embedding.shape[0], radial_in.shape[0]
    inner = weight_stack_t(radial_in[...])
    mid_a, mid_b = weight_stack(radial_mid[0]), weight_stack(radial_mid[1])
    outer = weight_stack_t(radial_out[...])
    lifted = species_matrix(node_one[0], embedding[...])
    scalar_mixing = jnp.concatenate([jnp.transpose(node_one[i]) for i in (1, 2, 3)], axis=0)
    base[...] = column(readout_linear[...]) + scalar_pull[...]
    turned = [scalar_mixing] + [jnp.transpose(m) for m in (node_two[1], node_one[4], node_one[5], node_two[0])]
    turned_high[...], turned_low[...] = parts(jnp.concatenate(turned, axis=0))

    def group(step, carry):
        first = step * GROUP
        at = span_of(step * GROUP * atoms, GROUP * atoms)
        h, dh = hidden[step]
        picked = picked_group(lifted, geo, kinds, first, species_count)
        weights_slope = dot(outer, value_stack(dh))
        scalar_slope[:, at] = weights_slope[:width] * picked
        vector_slope[:, at] = weights_slope[width:] * picked
        vector_value[:, at] = dot(outer[width:], value_stack(h)) * picked
        return carry

    def edge_group(step, carry):
        first = step * GROUP
        slope = dot(outer_two[...], slopes[:, span_of(step * GROUP * atoms, GROUP * atoms)])
        for j in range(GROUP):
            span = slice(j * atoms, (j + 1) * atoms)
            here = span_of((step * GROUP + j) * atoms, atoms)
            p = [picked_all[a * width : (a + 1) * width, here] for a in range(4)]
            r = [weights_all[a * width : (a + 1) * width, here] for a in (1, 3)]
            s = [slope[a * width : (a + 1) * width, span] for a in range(4)]
            u = [geo[a, pl.ds(first + j, 1), :] for a in range(3)]
            ga = [sums[a] for a in range(4)]
            along = p[1] * u[0] + p[2] * u[1] + p[3] * u[2]
            flow = ga[1] * u[0] + ga[2] * u[1] + ga[3] * u[2]
            cross = p[1] * ga[1] + p[2] * ga[2] + p[3] * ga[3]
            stretch = p[0] * (s[0] * ga[0] + s[1] * flow) + s[2] * cross + s[3] * (along * ga[0])
            geo_pull[0, pl.ds(first + j, 1), :] = jnp.sum(stretch, axis=0, keepdims=True)
            lean = r[0] * p[0]
            pull = r[1] * ga[0]
            for a in range(3):
                turn = lean * ga[a + 1] + pull * p[a + 1]
                geo_pull[a + 1, pl.ds(first + j, 1), :] = jnp.sum(turn, axis=0, keepdims=True)
        return carry

    values, slopes_in = (
        [basis_group(waves, i * GROUP, start, basis_count) for i in range(slots // GROUP)] for start in (0, basis_count)
    )
    works = [lambda i=i: edge_group(i, 0) for i in range(slots // GROUP)]
    hidden = hidden_pairs(values, slopes_in, inner, mid_a, mid_b, works)
    over_groups(slots // GROUP, group, 0)


def third_kernel(
    facts, geo, sums, geo_pull, own_pull, ret_minus, ret_plus, ret_sub,
    onehot, scalar_slope, vector_slope, vector_value, turned_high, turned_low, base,
    everyone, came,
    pieces, pulls, flat, *, moves, slab_rows, sub_rows,
):
    slots, atoms = geo.shape[1], geo.shape[2]
    width = sums.shape[1]
    half = sub_rows + 8
    ret_next, ret_prev = ret_sub.at[:half], ret_sub.at[half:]
    pick = send_onehot(facts, 0, slab_rows, sub_rows).astype(bf16)
    returned = jnp.concatenate(
        [ret_plus[:slab_rows], ret_minus[:slab_rows], ret_next[:sub_rows], ret_prev[:sub_rows]], axis=0
    )
    high, low = parts(returned)
    total = jnp.transpose(own_pull[...] + dot(pick, high) + dot(pick, low))
    x_pull = total[:width]
    y_pull = jnp.concatenate([total[a * width : (a + 1) * width] for a in (1, 2, 3)], axis=1)

    def turned(i, count=1):
        at = slice(i * width, (i + count) * width)
        return turned_high[at, :], turned_low[at, :]

    moved = product(turned(3), y_pull)
    gv = [moved[:, a * atoms : (a + 1) * atoms] for a in range(3)]
    scalar_sum, gate = sums[0], sums[4]
    vectors = [sums[1], sums[2], sums[3]]
    scalars = product(turned(6), x_pull) + base[...]
    spread = product(turned(0, 3), scalars)
    mixed = product(turned(4), moved)
    gated = product(turned(5), gv[0] * vectors[0] + gv[1] * vectors[1] + gv[2] * vectors[2])
    pulls[0] = spread[:width] + 2.0 * scalar_sum * spread[width : 2 * width] + gated
    double = 2.0 * spread[2 * width :]
    for a in range(3):
        pulls[a + 1] = vectors[a] * double + mixed[:, a * atoms : (a + 1) * atoms] + gate * gv[a]

    def contract(step, carry):
        first = step * GROUP
        for j in range(GROUP):
            here = span_of((step * GROUP + j) * atoms, atoms)
            row = pl.ds(first + j, 1)
            ga = [pulls[a] for a in range(4)]
            u = [geo[a, row, :] for a in range(3)]
            flow = ga[1] * u[0] + ga[2] * u[1] + ga[3] * u[2]
            stretch = scalar_slope[:, here] * ga[0] + vector_slope[:, here] * flow
            value = vector_value[:, here]
            flat[0, row, :] = jnp.sum(stretch, axis=0, keepdims=True)
            for a in range(3):
                flat[a + 1, row, :] = jnp.sum(value * ga[a + 1], axis=0, keepdims=True)
        return carry

    over_groups(slots // GROUP, contract, 0)
    stretch = flat[0] + geo_pull[0]
    turn = [flat[a + 1] + geo_pull[a + 1] for a in range(3)]
    u = [geo[a] for a in range(3)]
    inner = turn[0] * u[0] + turn[1] * u[1] + turn[2] * u[2]
    gradient = [stretch * u[a] + (turn[a] - inner * u[a]) * geo[5] for a in range(3)]
    at_row = iota((8, atoms), 0)
    own = jnp.zeros((8, atoms), f32)
    for a in range(3):
        flat[a] = gradient[a]
        own = jnp.where(at_row == a, jnp.sum(gradient[a], axis=0, keepdims=True), own)

    def push(step, carry):
        blocks = []
        for j in range(GROUP):
            row = pl.ds(step * GROUP + j, 1)
            block = jnp.where(at_row == 0, flat[0, row, :], jnp.where(at_row == 1, flat[1, row, :], flat[2, row, :]))
            blocks.append(block)
        block = jnp.concatenate(blocks, axis=1)
        top = block.astype(bf16).astype(f32)
        rest = block - top
        mid = rest.astype(bf16).astype(f32)
        split = jnp.concatenate([top, mid, rest - mid], axis=0).astype(bf16)
        at = span_of(step * GROUP * atoms, GROUP * atoms)
        chosen = jnp.concatenate([onehot[:atoms, at], onehot[2 * atoms : 2 * atoms + ghost_rows, at]], axis=0)
        return carry + dot_nt(chosen, split)

    ghost_rows = onehot.shape[0] // 2 - atoms
    zero = jnp.zeros((onehot.shape[0] // 2, 24), f32)
    pushed = over_groups(slots // GROUP, push, zero)
    pushed = jnp.transpose(pushed)
    pushed = (pushed[:8] + pushed[8:16] + pushed[16:]) * (1.0 / neighbor_norm)
    own = own - pushed[:, :atoms]
    velocities, mass = facts[1:4], facts[8:9]
    pieces[0:3] = (own * facts[7:8])[:3]
    blocks = ((ret_minus, slab_rows), (ret_plus, slab_rows), (ret_prev, sub_rows), (ret_next, sub_rows))
    start = atoms
    ghost_lines = [[0.0] * 3 for _ in range(3)]
    for i, (ref, count) in enumerate(blocks):
        told = ref[count : count + 8, :count]
        force = -pushed[:, start : start + count]
        start += count
        for a in range(3):
            for b in range(3):
                ghost_lines[a][b] = ghost_lines[a][b] + told[a + 1 : a + 2] * force[b : b + 1]
        scaled = force * told[7:8]
        top = scaled.astype(bf16).astype(f32)
        rest = scaled - top
        mid = rest.astype(bf16).astype(f32)
        split = jnp.concatenate([top, mid, rest - mid], axis=0).astype(bf16)
        place = (iota((atoms, count), 0) == told[0:1].astype(jnp.int32)).astype(bf16)
        spread = dot_nt(split, place)
        pieces[3 * i + 3 : 3 * i + 6] = (spread[:8] + spread[8:16] + spread[16:])[:3]
    came[...] = jnp.zeros_like(came)
    for i, (ref, count) in enumerate(blocks):
        came[:, i * moves : (i + 1) * moves] = ref[count : count + 8, atoms : atoms + moves]

    def line(a, b):
        start = velocities[a : a + 1] * velocities[b : b + 1] * mass
        mixed = velocities[a : a + 1] * own[b : b + 1] + velocities[b : b + 1] * own[a : a + 1]
        return start + time_step * mixed - jnp.sum(u[a] * geo[4] * gradient[b], axis=0, keepdims=True)

    lines = jnp.concatenate([line(a, b) for a in range(3) for b in range(3)] + [jnp.zeros((7, atoms), f32)], axis=0)
    ghosts = [time_step * (ghost_lines[a][b] + ghost_lines[b][a]) for a in range(3) for b in range(3)]
    ghosts = jnp.concatenate(ghosts + [jnp.zeros((7, slab_rows), f32)], axis=0)
    summed = jnp.sum(lines, axis=1, keepdims=True) + jnp.sum(ghosts, axis=1, keepdims=True)
    row = jnp.zeros((1, atoms), f32)
    for i in range(9):
        row = jnp.where(iota((1, atoms), 1) == i, summed[i : i + 1], row)
    pieces[15:16] = row
    for i in range(everyone.shape[0]):
        everyone[i] = pieces[...]


def determinant(m):
    return (
        m[0][0] * (m[1][1] * m[2][2] - m[1][2] * m[2][1])
        - m[0][1] * (m[1][0] * m[2][2] - m[1][2] * m[2][0])
        + m[0][2] * (m[1][0] * m[2][1] - m[1][1] * m[2][0])
    )


def inverse(m):
    whole = determinant(m)
    return [
        [
            (
                m[(j + 1) % 3][(i + 1) % 3] * m[(j + 2) % 3][(i + 2) % 3]
                - m[(j + 1) % 3][(i + 2) % 3] * m[(j + 2) % 3][(i + 1) % 3]
            )
            / whole
            for j in range(3)
        ]
        for i in range(3)
    ]


def fifth_kernel(
    pieces, own_facts, came, box, box_speed,
    forces_out, velocities_out, positions_out, arrivals, new_box, new_box_speed,
    whole, *, atoms_all, slab_count, sub_count,
):
    atoms = own_facts.shape[1]
    velocities, positions = own_facts[1:4], own_facts[4:7]
    devices = slab_count * sub_count
    sub = lax.rem(iota((devices, atoms), 0), sub_count)

    def row_of_all(r):
        return pieces[:, r, :]

    def piece(i, a):
        return row_of_all(3 * i + a)

    def moved(x, step):
        return pltpu.roll(x, (-step) % devices, 0)

    for a in range(3):
        total = piece(0, a) + moved(piece(1, a), sub_count) + moved(piece(2, a), -sub_count)
        x = piece(3, a)
        total = total + jnp.where(sub == sub_count - 1, moved(x, 1 - sub_count), moved(x, 1))
        x = piece(4, a)
        whole[a] = total + jnp.where(sub == 0, moved(x, sub_count - 1), moved(x, -1))
    squares = {}
    for a in range(3):
        for b in range(a, 3):
            squares[a, b] = jnp.sum(whole[a] * whole[b], axis=0, keepdims=True)
    order = list(squares)
    squares = jnp.concatenate([squares[k] for k in order] + [jnp.zeros((2, atoms), f32)], axis=0)
    squares = jnp.sum(squares, axis=1, keepdims=True)
    rest = jnp.sum(row_of_all(15), axis=0, keepdims=True)
    stress = [[None] * 3 for _ in range(3)]
    for i in range(3):
        for j in range(3):
            at = order.index((min(i, j), max(i, j)))
            stress[i][j] = rest[:, 3 * i + j : 3 * i + j + 1] + (time_step * time_step) * squares[at : at + 1]
    slab_at, sub_at = lax.axis_index("slab"), lax.axis_index("sub")
    mine = slab_at * sub_count + sub_at
    root, mass = own_facts[7:8], own_facts[8:9]
    for a in range(3):
        force = whole[a, pl.ds(mine, 1), :] * (mass * root)
        forces_out[a : a + 1, :] = force
        velocities_out[a : a + 1, :] = velocities[a : a + 1, :] + time_step * force / mass
    lane, row = iota((8, atoms), 1), iota((8, atoms), 0)
    facts = came[...]
    index = jnp.broadcast_to(facts[0:1].astype(jnp.int32), (8, atoms))
    count = arrivals.shape[1] // 4
    picked = jnp.zeros((8, atoms), f32)
    for i, (slab_step, sub_step) in enumerate(((-1, 0), (1, 0), (0, -1), (0, 1))):
        slab = lax.rem(slab_at + (slab_step + slab_count), slab_count)
        source = slab * sub_count + lax.rem(sub_at + (sub_step + sub_count), sub_count)
        force = [whole[a, pl.ds(source, 1), :] for a in range(3)]
        force = jnp.where(row == 0, force[0], jnp.where(row == 1, force[1], force[2]))
        found = jnp.take_along_axis(force, index, axis=1)
        picked = jnp.where((lane >= i * count) & (lane < (i + 1) * count), found, picked)
    speeds = [facts[1 + a : 2 + a] + time_step * picked[a : a + 1] * facts[7:8] for a in range(3)]

    def spread(value):
        return jnp.full((1, atoms), value, f32)

    old = [[spread(box[i, j]) for j in range(3)] for i in range(3)]
    volume = determinant(old)
    old_inverse = inverse(old)
    for i in range(3):
        stress[i][i] = stress[i][i] - outside_pressure * volume
    fresh = [[None] * 3 for _ in range(3)]
    for i in range(3):
        for j in range(3):
            push = stress[i][0] * old_inverse[j][0] + stress[i][1] * old_inverse[j][1] + stress[i][2] * old_inverse[j][2]
            speed = spread(box_speed[i, j]) + time_step * push / (box_mass * atoms_all)
            fresh[i][j] = old[i][j] + time_step * speed
            new_box_speed[i : i + 1, j : j + 1] = speed[:, :1]
            new_box[i : i + 1, j : j + 1] = fresh[i][j][:, :1]
    new_inverse = inverse(fresh)
    for i in range(3):
        move = sum(new_inverse[i][j] * velocities_out[j : j + 1, :] for j in range(3))
        positions_out[i : i + 1, :] = positions[i : i + 1, :] + time_step * move
    for i in range(3):
        move = sum(new_inverse[i][j] * speeds[j] for j in range(3))
        arrivals[i : i + 1, :] = (facts[4 + i : 5 + i] + time_step * move)[:, : 4 * count]
        arrivals[3 + i : 4 + i, :] = speeds[i][:, : 4 * count]


VM = pl.BlockSpec(memory_space=pltpu.VMEM)
HB = pl.BlockSpec(memory_space=pltpu.HBM)
SM = pl.BlockSpec(memory_space=pltpu.SMEM)


def shape(*dims, dtype=f32):
    return jax.ShapeDtypeStruct(dims, dtype)


def call(kernel, outs, scalar_inputs=(), far_inputs=False, far_outputs=(), scratch=(), flops=0, vmem=16, name=None):
    def run(*args):
        moved = sum(math.prod(x.shape) * x.dtype.itemsize for x in list(args) + list(outs))
        return pl.pallas_call(
            kernel,
            out_shape=tuple(outs),
            in_specs=[HB if far_inputs else SM if i in scalar_inputs else VM for i in range(len(args))],
            out_specs=tuple(HB if i in far_outputs else VM for i in range(len(outs))),
            scratch_shapes=list(scratch),
            compiler_params=pltpu.CompilerParams(vmem_limit_bytes=vmem * 1024 * 1024),
            cost_estimate=pl.CostEstimate(flops=flops, bytes_accessed=moved, transcendentals=0),
            name=name,
        )(*args)

    return run


def body(
    positions, velocities, species, ghost_species, neighbours, slot_mask, edge_vectors, send_slab, send_sub, migrants,
    embedding, energy_shift, masses, radial_one_in, radial_one_mid, radial_one_out, node_one,
    radial_two_in, radial_two_mid, radial_two_out, node_two, readout_linear, readout_hidden, readout_out,
    box_matrix, box_velocity,
):
    slots, atoms = neighbours.shape
    width = node_one.shape[1]
    hidden = radial_one_mid.shape[1]
    depth = 4 * width
    ghost_slab, ghost_sub = send_slab.shape[1], send_sub.shape[1]
    extended = atoms + 2 * ghost_slab + 2 * ghost_sub
    edges = slots * atoms
    devices = lax.axis_size("slab") * lax.axis_size("sub")
    species_row = species.reshape(1, atoms)
    ghost_row = ghost_species.reshape(1, -1)
    linear_row = readout_linear.reshape(1, -1)
    out_row = readout_out.reshape(1, -1)
    radial_one_in, radial_one_out = jnp.transpose(radial_one_in), jnp.transpose(radial_one_out)
    radial_two_in, radial_two_out = jnp.transpose(radial_two_in), jnp.transpose(radial_two_out)

    first_inputs = (
        edge_vectors, slot_mask, neighbours, species_row, ghost_row, embedding,
        radial_one_in, radial_one_mid, radial_one_out, node_one, send_slab, send_sub,
        velocities, positions, migrants, masses.reshape(1, -1), energy_shift.reshape(1, -1),
        readout_hidden, linear_row, out_row, radial_two_in, radial_two_mid, radial_two_out, node_two,
    )
    packed_rows = (
        8 * width + 6 * packed_step(slots) + FACTS + 6 * hidden + radial_two_in.shape[0] + packed_step(slots)
        + readout_hidden.shape[0] + 8 + 2 * radial_one_in.shape[0] * packed_step(slots)
    )
    kinds, sums, packed, to_minus, to_plus, to_sub = call(
        first_kernel,
        (
            shape(slots, atoms, dtype=jnp.int32),
            shape(5, width, atoms),
            shape(packed_rows, atoms),
            shape(ghost_slab, depth),
            shape(ghost_slab, depth),
            shape(2 * ghost_sub, depth),
        ),
        far_inputs=True,
        far_outputs=(1, 2),
        scratch=(
            pltpu.VMEM((6, slots, atoms), f32),
            pltpu.VMEM((2 * radial_one_in.shape[0], slots, atoms), f32),
            pltpu.VMEM((packed_rows, atoms), f32),
            pltpu.VMEM((5, width, atoms), f32),
        )
        + tuple(pltpu.VMEM(x.shape, x.dtype) for x in first_inputs)
        + (pltpu.SemaphoreType.DMA((FIRST_INPUTS,)), pltpu.SemaphoreType.DMA((4,))),
        flops=6 * edges * 26000,
        vmem=56,
        name="layer_one",
    )(
        *first_inputs
    )
    from_minus, from_plus, from_sub = trade(to_minus, to_plus, to_sub, 1)

    def radial(*refs):
        radial_kernel(
            *refs,
            slab_rows=ghost_slab,
            sub_rows=ghost_sub,
            moves=migrants.shape[1],
            basis_count=radial_two_in.shape[0],
        )

    (
        weights_all, slopes, onehot, outer, fold_high, fold_low, back_high, back_low,
        geo, picked_own, scalars, extras, facts, heads, waves,
    ) = call(
        radial,
        (
            shape(depth, edges),
            shape(3 * hidden, edges, dtype=bf16),
            shape(2 * extended, edges, dtype=bf16),
            shape(depth, 3 * hidden, dtype=bf16),
            shape(readout_hidden.shape[0], 3 * width, dtype=bf16),
            shape(readout_hidden.shape[0], 3 * width, dtype=bf16),
            shape(3 * width, readout_hidden.shape[0], dtype=bf16),
            shape(3 * width, readout_hidden.shape[0], dtype=bf16),
            shape(6, slots, atoms),
            shape(depth, edges),
            shape(width, atoms),
            shape(4, 8, 2 * atoms),
            shape(FACTS, atoms),
            shape(readout_hidden.shape[0] + 8, atoms),
            shape(2 * radial_two_in.shape[0], slots, atoms),
        ),
        flops=12 * edges * 10000,
        vmem=16,
        name="radial_two",
    )(
        packed,
    )

    energy, scalar_pull, picked_all, pulls, own_pull, back_minus, back_plus, back_sub = call(
        second_kernel,
        (
            shape(1, atoms),
            shape(width, atoms),
            shape(depth, edges),
            shape(4, width, atoms),
            shape(atoms, depth),
            shape(ghost_slab + 8, depth),
            shape(ghost_slab + 8, depth),
            shape(2 * (ghost_sub + 8), depth),
        ),
        scratch=(
            pltpu.VMEM((depth, 2 * (extended - atoms)), bf16),
            pltpu.VMEM((extended, depth), f32),
        ),
        flops=4 * edges * depth * extended * 2,
        vmem=20,
        name="layer_two",
    )(
        geo, picked_own, from_minus, from_plus, from_sub, scalars, extras,
        weights_all, onehot, fold_high, fold_low, back_high, back_low, heads,
    )
    ret_minus, ret_plus, ret_sub = trade(back_minus, back_plus, back_sub, -1)
    geo_pull, scalar_slope, vector_slope, vector_value, turned_high, turned_low, base = call(
        window_kernel,
        (
            shape(4, slots, atoms),
            shape(width, edges),
            shape(width, edges),
            shape(width, edges),
            shape(7 * width, width, dtype=bf16),
            shape(7 * width, width, dtype=bf16),
            shape(width, atoms),
        ),
        flops=12 * edges * 12000,
        vmem=20,
        name="radial_one",
    )(
        slopes, outer, picked_all, weights_all, pulls,
        geo, waves, kinds, scalar_pull, embedding,
        radial_one_in, radial_one_mid, radial_one_out, node_one, node_two, linear_row,
    )

    def back(*refs):
        third_kernel(*refs, moves=migrants.shape[1], slab_rows=ghost_slab, sub_rows=ghost_sub)

    everyone, came = call(
        back,
        (shape(devices, 16, atoms), shape(8, atoms)),
        scratch=(
            pltpu.VMEM((16, atoms), f32),
            pltpu.VMEM((4, width, atoms), f32),
            pltpu.VMEM((4, slots, atoms), f32),
        ),
        flops=6 * edges * 1000,
        vmem=12,
        name="layer_one_back",
    )(
        facts, geo, sums, geo_pull, own_pull, ret_minus, ret_plus, ret_sub,
        onehot, scalar_slope, vector_slope, vector_value, turned_high, turned_low, base,
    )
    everyone = lax.all_to_all(everyone, ("slab", "sub"), 0, 0, tiled=True)

    def last(*refs):
        fifth_kernel(
            *refs, atoms_all=atoms * devices, slab_count=lax.axis_size("slab"), sub_count=lax.axis_size("sub")
        )

    forces, new_velocities, new_positions, arrivals, new_box, new_box_velocity = call(
        last,
        (
            shape(3, atoms), shape(3, atoms), shape(3, atoms), shape(6, 4 * migrants.shape[1]),
            shape(3, 3), shape(3, 3),
        ),
        scalar_inputs=(3, 4),
        scratch=(pltpu.VMEM((3, devices, atoms), f32),),
        flops=1000000,
        vmem=8,
        name="box",
    )(everyone, facts, came, box_matrix, box_velocity)
    return energy.reshape(atoms), forces, new_velocities, new_positions, arrivals, new_box, new_box_velocity


def solution(mesh):
    split = ("slab", "sub")
    one, two, three, copied = P(split), P(None, split), P(None, None, split), P()
    placed = (two, two, one, one, two, two, three, two, two, two) + (copied,) * 16
    return jax.shard_map(
        body,
        mesh=mesh,
        in_specs=placed,
        out_specs=(one, two, two, two, two, copied, copied),
        check_vma=False,
    )
```
